32 devices in a mesh: dp: 8 (over y, x, core), tensor: 4 (over z).
Axes of the slice: x: 2, y: 2, z: 4, core: 2. Of those that a mesh axis runs over, the one named last changes fastest.
Arguments:
- sequence: bfloat16 [32, 532, 768], P('dp', 'tensor'), may hold values from -6 to 6
- query_key_value_weight: bfloat16 [768, 3, 768], P(None, None, 'tensor'), may hold values from -0.21875 to 0.21875
- qv_bias: bfloat16 [2, 768], P(None, 'tensor'), may hold values from -3 to 3
- output_weight: bfloat16 [768, 768], P('tensor'), may hold values from -0.875 to 0.875
- out_bias: bfloat16 [768], replicated, may hold values from -2 to 2
- up_weight: bfloat16 [768, 3072], P(None, 'tensor'), may hold values from -0.21875 to 0.21875
- up_bias: bfloat16 [3072], P('tensor'), may hold values from -3 to 3
- down_weight: bfloat16 [3072, 768], P('tensor'), may hold values from -0.21875 to 0.21875
- back_bias: bfloat16 [768], replicated, may hold values from -2 to 2
- gain_one: bfloat16 [768], replicated, may hold values from 0.099609375 to 1.8984375
- shift_one: bfloat16 [768], replicated, may hold values from -2 to 2
- gain_two: bfloat16 [768], replicated, may hold values from 0.099609375 to 1.8984375
- shift_two: bfloat16 [768], replicated, may hold values from -2 to 2
- init_memory: bfloat16 [10, 768], replicated, may hold values from -6 to 6
- reset: int32 [32], P('dp'), may hold values from 0 to 1
- starts: int32 [32, 512], P('dp'), may hold values from 0 to 1, as said below
- cotangent: bfloat16 [32, 532, 768], P('dp', 'tensor'), may hold values from -6 to 6
Outputs:
- output: bfloat16 [32, 532, 768], P('dp', 'tensor')
- input_grad: float32 [32, 532, 768], P('dp', 'tensor')
- query_key_value_gradient: float32 [768, 3, 768], P(None, None, 'tensor')
- grad_qv_bias: float32 [2, 768], P(None, 'tensor')
- output_weight_gradient: float32 [768, 768], P('tensor')
- grad_out_bias: float32 [768], replicated
- up_weight_gradient: float32 [768, 3072], P(None, 'tensor')
- grad_in_bias: float32 [3072], P('tensor')
- down_weight_gradient: float32 [3072, 768], P('tensor')
- grad_back_bias: float32 [768], replicated
- grad_gain_one: float32 [768], replicated
- grad_shift_one: float32 [768], replicated
- grad_gain_two: float32 [768], replicated
- grad_shift_two: float32 [768], replicated
- grad_memory: float32 [10, 768], replicated
The draws below stay inside these ranges and needn't reach their ends.
Inputs may be any that keep to these rules, and one draw needn't show every extreme that they name: `starts`: the first entry of every segment is 1; in some segment it is the only 1.
All inputs are finite; a program needn't handle non-finite values.
Results may differ from the reference program's by a relative error of at most 0.017.
Values may be sent and summed in bfloat16 or wider, within the bound.
A program may use at most 192 MiB of HBM per device.

```python
import jax
import jax.numpy as jnp
from jax import lax

D = 768
H = 12
FF = 3072
MEM = 10
SEG = 512
SEGS_DEV = 4
DH = 64
ROWS = 532
SEGS = 32


def draw_starts(key, part):
    key = jax.random.fold_in(key, 7)
    key_bits, key_whole = jax.random.split(key)
    drawn = jax.random.randint(key_bits, (SEGS, SEG), 0, SEG // 8 + 2)
    whole = jax.random.randint(key_whole, (), 0, SEGS)
    seg_index = jnp.arange(SEGS)[:, None]
    token_index = jnp.arange(SEG)[None, :]
    flags = (drawn == 0) & (seg_index != whole)
    flags = flags | (token_index == 0)
    return flags.astype(jnp.int32)


def with_ends(values, key, low, largest):
    dims = values.shape
    spot = [jax.random.randint(jax.random.fold_in(key, axis), (), 0, dims[axis]) for axis in range(len(dims))]
    values = values.at[tuple(spot)].set(low)
    longest = dims.index(max(dims))
    spot[longest] = (spot[longest] + 1) % dims[longest]
    return values.at[tuple(spot)].set(largest)


def shard_levels(own_key, extent, shards, least, high):
    def one(dim, blocks):
        heights = jax.random.uniform(jax.random.fold_in(jax.random.fold_in(own_key, 6), dim), (blocks,), jnp.float32, least / len(shards), high / len(shards))
        return jnp.repeat(jnp.exp(heights), extent[dim] // blocks).reshape((-1,) + (1,) * (len(extent) - dim - 1))

    loudness = one(*shards[0])
    for cut in shards[1:]:
        loudness = loudness * one(*cut)
    return loudness


def normal_values(own_key, dims, scale, bound, pieces=(), kind=jnp.bfloat16):
    values = scale * jax.random.normal(own_key, dims, jnp.float32)
    if pieces:
        values = values * shard_levels(own_key, dims, pieces, -0.22, 0.18)
    return jnp.clip(values, -bound, bound).astype(kind)


def setup_inputs(seed: int = 0) -> dict:
    splits = jax.random.split(jax.random.key(seed), 18)
    return {
        "sequence": normal_values(splits[0], (SEGS, ROWS, D), 1.0, 6.0, ((0, 8), (1, 4))),
        "query_key_value_weight": normal_values(splits[1], (D, 3, D), D ** -0.5, 0.21875, ((2, 4),)),
        "qv_bias": normal_values(splits[2], (2, D), 0.5, 3.0, ((1, 4),)),
        "output_weight": normal_values(splits[3], (D, D), (D // 16) ** -0.5, 0.875, ((0, 4),)),
        "out_bias": normal_values(splits[4], (D,), 0.3, 2.0),
        "up_weight": normal_values(splits[5], (D, FF), D ** -0.5, 0.21875, ((1, 4),)),
        "up_bias": normal_values(splits[6], (FF,), 0.5, 3.0, ((0, 4),)),
        "down_weight": normal_values(splits[7], (FF, D), (FF // 4) ** -0.5, 0.21875, ((0, 4),)),
        "back_bias": normal_values(splits[8], (D,), 0.3, 2.0),
        "gain_one": jnp.clip(1.0 + 0.18 * jax.random.normal(splits[9], (D,), jnp.float32), 0.099609375, 1.8984375).astype(jnp.bfloat16),
        "shift_one": normal_values(splits[10], (D,), 0.3, 2.0),
        "gain_two": jnp.clip(1.0 + 0.18 * jax.random.normal(splits[11], (D,), jnp.float32), 0.099609375, 1.8984375).astype(jnp.bfloat16),
        "shift_two": normal_values(splits[12], (D,), 0.3, 2.0),
        "init_memory": normal_values(splits[13], (MEM, D), 1.0, 6.0),
        "reset": with_ends(jax.random.randint(splits[14], (SEGS,), 0, 2), jax.random.fold_in(splits[14], 1), 0, 1).astype(jnp.int32),
        "starts": draw_starts(jax.random.fold_in(splits[17], 71), 0),
        "cotangent": normal_values(splits[16], (SEGS, ROWS, D), 1.0, 6.0, ((0, 8), (1, 4))),
    }


PRECISE_MODE = lax.Precision.HIGHEST
NEGATIVE = -1e+30
EPSILON = 1e-05

@jax.custom_vjp
def reduced_precision(v):
    return lax.optimization_barrier(v.astype(jnp.bfloat16)).astype(jnp.float32)

@jax.custom_vjp
def reduced_backward(v):
    return v

def low_keep(v):
    return (reduced_precision(v), None)

def low_pass(kept, grad):
    return (grad,)

def back_keep(v):
    return (v, None)

def back_low(kept, grad):
    return (reduced_precision(grad),)
reduced_precision.defvjp(low_keep, low_pass)
reduced_backward.defvjp(back_keep, back_low)

def both_round(value):
    return reduced_backward(reduced_precision(value))

def layer_norm(values_in, norm_gain, norm_shift):
    row_mean = lax.optimization_barrier(jnp.mean(values_in, axis=-1, keepdims=True))
    centred = values_in - row_mean
    row_var = lax.optimization_barrier(jnp.mean(centred * centred, axis=-1, keepdims=True))
    return centred * lax.rsqrt(row_var + EPSILON) * norm_gain + norm_shift

def group_layer(inputs, doc_rows, use_init, params):
    query_key_value_weight, qv_bias, output_weight, out_bias, up_weight, up_bias, down_weight, back_bias, gain_one, shift_one, gain_two, shift_two, init_memory = params
    group = inputs.shape[0]
    length = inputs.shape[1]
    memory_table = jnp.concatenate([init_memory, jnp.zeros((SEG, D), jnp.float32), init_memory], 0)
    layer_input = jnp.where(use_init[:, :, None], memory_table[None], inputs)
    projected_rows = jnp.einsum('eon,nxa->eoxa', reduced_precision(layer_input), query_key_value_weight, precision=PRECISE_MODE)
    head_shape = (group, length, H, DH)
    queries = both_round(projected_rows[:, :, 0] + qv_bias[0]).reshape(head_shape)
    keys_all = both_round(projected_rows[:, :, 1]).reshape(head_shape)
    values_all = both_round(projected_rows[:, :, 2] + qv_bias[1]).reshape(head_shape)
    allowed = (doc_rows[:, :, None] == doc_rows[:, None, :]) | (doc_rows[:, :, None] < 0) | (doc_rows[:, None, :] < 0)
    scores = reduced_backward(jnp.einsum('sqhe,skhe->shqk', queries, keys_all, precision=PRECISE_MODE) * DH ** (-0.5))
    scores = jnp.where(allowed[:, None], scores, NEGATIVE)
    top = lax.optimization_barrier(jnp.max(scores, axis=-1, keepdims=True))
    weights = jnp.exp(scores - top)
    probs = weights / lax.optimization_barrier(jnp.sum(weights, axis=-1, keepdims=True))
    mixed_rows_value = both_round(jnp.einsum('shqk,skhe->sqhe', reduced_precision(probs), values_all, precision=PRECISE_MODE)).reshape(group, length, D)
    attended_rows = reduced_backward(jnp.einsum('cui,ir->cur', mixed_rows_value, output_weight, precision=PRECISE_MODE))
    normalized = layer_norm(layer_input + attended_rows + out_bias, gain_one, shift_one)
    pre_activation = reduced_backward(jnp.einsum('bre,ek->brk', reduced_precision(normalized), up_weight, precision=PRECISE_MODE) + up_bias)
    hidden_rows = reduced_precision(jax.nn.gelu(pre_activation, approximate=False))
    feed_rows = reduced_backward(jnp.einsum('cui,ir->cur', hidden_rows, down_weight, precision=PRECISE_MODE))
    return layer_norm(normalized + feed_rows + back_bias, gain_two, shift_two)

def reference(sequence, query_key_value_weight, qv_bias, output_weight, out_bias, up_weight, up_bias, down_weight, back_bias, gain_one, shift_one, gain_two, shift_two, init_memory, reset, starts, cotangent):
    doc_ids = jnp.cumsum(starts, axis=1).astype(jnp.int32)
    marker = jnp.full((SEGS, MEM), -1, jnp.int32)
    doc_rows = jnp.concatenate([marker, doc_ids, marker], 1)
    position = jnp.arange(ROWS, dtype=jnp.int32)
    is_memory = (position < MEM) | (position >= MEM + SEG)
    use_init = (reset[:, None] > 0) & is_memory[None, :]
    weights_list = [query_key_value_weight, qv_bias, output_weight, out_bias, up_weight, up_bias, down_weight, back_bias, gain_one, shift_one, gain_two, shift_two, init_memory]
    weights_list = [item.astype(jnp.float32) for item in weights_list]
    groups = SEGS // SEGS_DEV
    doc_groups = doc_rows.reshape(groups, SEGS_DEV, ROWS)
    use_groups = use_init.reshape(groups, SEGS_DEV, ROWS)

    def forward(inputs, *params):

        def one_group(block):
            return group_layer(block[0], block[1], block[2], params)
        result = lax.map(jax.checkpoint(one_group), (inputs.reshape(groups, SEGS_DEV, ROWS, D), doc_groups, use_groups))
        return result.reshape(SEGS, ROWS, D)
    result, pullback = jax.vjp(forward, sequence.astype(jnp.float32), *weights_list)
    grads = pullback(cotangent.astype(jnp.float32))
    return (result.astype(jnp.bfloat16), grads[0], grads[1], grads[2], grads[3], grads[4], grads[5], grads[6], grads[7], grads[8], grads[9], grads[10], grads[11], grads[12], grads[13])
```

```python
import functools

import jax
import jax.numpy as jnp
from jax import lax
from jax.experimental import pallas as pl
from jax.experimental.pallas import tpu as pltpu
from jax.sharding import PartitionSpec as P

DH = 64
NEGATIVE = -1e30
EPSILON = 1e-05
INNER = 8
MIB = 1 << 20

f32 = jnp.float32
bf16 = jnp.bfloat16
NN = (((1,), (0,)), ((), ()))
NT = (((1,), (1,)), ((), ()))
TN = (((0,), (0,)), ((), ()))
MESH = pl.DeviceIdType.MESH


def dot(a, b, dims=NN):
    return lax.dot_general(a, b, dims, preferred_element_type=f32)


def each(count, body):
    def step(i, carry):
        body(i)
        return carry

    lax.fori_loop(0, count, step, 0)


class Place:
    def __init__(self, planes):
        self.planes = planes
        self.dp = lax.axis_index("dp")
        self.t = lax.axis_index("tensor")
        self.core = self.dp % 2
        self.x = (self.dp // 2) % 2
        self.y = (self.dp // 4) % 2
        self.to_core = (self.dp + 1 - 2 * self.core, self.t)
        self.to_x = (self.dp + 2 - 4 * self.x, self.t)
        self.to_y = (self.dp + 4 - 8 * self.y, self.t)

    def plane(self, j):
        return lax.rem(self.t + j, self.planes)

    def to_plane(self, j):
        return (self.dp, self.plane(j))

    def partners(self):
        return [self.to_core, self.to_x, self.to_y] + [
            self.to_plane(j) for j in range(1, self.planes)
        ]

    def greet(self):
        barrier = pltpu.get_barrier_semaphore()
        partners = self.partners()
        for device in partners:
            pl.semaphore_signal(barrier, inc=1, device_id=device, device_id_type=MESH)
        pl.semaphore_wait(barrier, len(partners))


class Rows:
    def __init__(self, place, rows):
        self.piece = rows // (2 * INNER)
        self.half = rows // 2
        quarter = rows // 4
        core, x, y = place.core, place.x, place.y
        at = lambda n: pl.multiple_of(n, 16)
        base = core * self.half
        self.mine = at(base)
        self.others = at((1 - core) * self.half)
        self.a = at(base + (2 * y + x) * self.piece)
        self.b = at(base + quarter + (2 * x + y) * self.piece)
        self.a_pair = at(base + 2 * y * self.piece)
        self.b_pair = at(base + quarter + 2 * x * self.piece)
        self.a_far_pair = at(base + 2 * (1 - y) * self.piece)
        self.b_far_pair = at(base + quarter + 2 * (1 - x) * self.piece)
        self.a_far = at(base + (2 * y + 1 - x) * self.piece)
        self.b_far = at(base + quarter + (2 * x + 1 - y) * self.piece)


class Links:
    def __init__(self, send, recv):
        self.send, self.recv, self.count, self.all = send, recv, 0, []

    def copy(self, src, dst, device):
        k = self.count
        self.count += 1
        made = pltpu.make_async_remote_copy(
            src_ref=src,
            dst_ref=dst,
            send_sem=self.send.at[k],
            recv_sem=self.recv.at[k],
            device_id=device,
            device_id_type=MESH,
        )
        self.all.append(made)
        return made

    def finish(self):
        for made in self.all:
            made.wait_send()


def start(copies):
    for c in copies:
        c.start()


def arrive(copies):
    for c in copies:
        c.wait_recv()


FORWARD_LINKS = 96
FORWARD_LOCALS = 24


def forward_kernel(
    planes,
    heads,
    x_in,
    c_in,
    a_in,
    u_in,
    d_in,
    bias_in,
    vec_ref,
    qcode_ref,
    kcode_ref,
    a_out,
    u_out,
    d_out,
    x_out,
    q_out,
    k_out,
    v_out,
    p_out,
    o_out,
    xhat_out,
    hb_out,
    act_out,
    slope_out,
    g2_out,
    y_out,
    rstd_ref,
    small_ref,
    a_w,
    u_w,
    d_w,
    xs,
    cs,
    bias,
    q_s,
    k_s,
    v_s,
    p_s,
    o_s,
    o3,
    mask,
    acc,
    xhat_s,
    hb_s,
    act_s,
    slope_s,
    y_s,
    send,
    recv,
    local,
):
    place = Place(planes)
    t = place.t
    others = range(1, planes)
    block, width = xs.shape[1], xs.shape[2]
    rows = planes * block
    hp = heads // planes
    hw = hp * DH
    links = Links(send, recv)
    r = Rows(place, a_in.shape[0])
    piece = r.piece

    def keep(k, src, dst):
        return pltpu.make_async_copy(src, dst, local.at[k])

    ins, weights, outs = (a_in, u_in, d_in), (a_w, u_w, d_w), (a_out, u_out, d_out)
    own = [keep(w, ins[w], weights[w].at[t]) for w in range(3)]
    own_x = keep(3, x_in.at[t], xs.at[t])
    own_c = keep(4, c_in.at[t], cs.at[t])
    own_bias = keep(5, bias_in, bias.at[t])

    z_send, s1, s2, cc = [], [], [], []
    for w in range(3):
        z, one, two, three = [], [], [], []
        for j in others:
            s = place.plane(planes - j)
            to = place.to_plane(j)
            for at in (r.a, r.b):
                z.append(
                    links.copy(
                        ins[w].at[pl.ds(at, piece)], weights[w].at[t, pl.ds(at, piece)], to
                    )
                )
            for at, size, to, into in (
                (r.a, piece, place.to_x, one),
                (r.b, piece, place.to_y, one),
                (r.a_pair, 2 * piece, place.to_y, two),
                (r.b_pair, 2 * piece, place.to_x, two),
                (r.mine, r.half, place.to_core, three),
            ):
                ref = weights[w].at[s, pl.ds(at, size)]
                into.append(links.copy(ref, ref, to))
        z_send.append(z)
        s1.append(one)
        s2.append(two)
        cc.append(three)
    x_send = [links.copy(x_in.at[place.plane(j)], xs.at[t], place.to_plane(j)) for j in others]
    c_send = [links.copy(c_in.at[place.plane(j)], cs.at[t], place.to_plane(j)) for j in others]
    b_send = [links.copy(bias_in, bias.at[t], place.to_plane(j)) for j in others]

    start([own_x, *own, own_bias, own_c])
    place.greet()
    start(z_send[0])
    start(b_send)
    start(x_send)

    for c in range(planes):
        span = pl.ds(c * block, block)
        qc = qcode_ref[span, :]
        kc = kcode_ref[...]
        allowed = ((qc == kc) | (qc < 0) | (kc < 0)) & (kc != -2)
        mask[span, :] = jnp.where(allowed, 0.0, NEGATIVE)

    arrive(z_send[0])
    start(s1[0])
    start(z_send[1])
    arrive(s1[0])
    start(s2[0])
    for c in (own_x, *own, own_bias, own_c):
        c.wait()
    arrive(x_send)
    arrive(b_send)
    arrive(s2[0])
    start(cc[0])
    start(z_send[2])

    out_copies = []

    def leave(k, src, dst):
        c = keep(k, src, dst)
        out_copies.append(c)
        return c

    leave_x = [leave(6 + j, xs.at[j], x_out.at[j]) for j in range(planes)]
    start(leave_x)
    acc[...] = xs[...].reshape(rows, width).astype(f32) + vec_ref[0:1, :]

    def attention(j):
        s = place.plane(j)

        @pl.when(j == 1)
        def _():
            arrive(cc[0])
            arrive(z_send[1])
            start(s1[1])

        @pl.when(j == 2)
        def _():
            arrive(s1[1])
            start(s2[1])
            arrive(z_send[2])
            start(s1[2])
            start(c_send)

        @pl.when(j == 3)
        def _():
            arrive(s2[1])
            start(cc[1])
            arrive(s1[2])
            start(s2[2])

        x = xs[...].reshape(rows, width)
        qkv = dot(x, a_w[s, 0 : 3 * hw, :], NT)
        b = bias[s, 1:2, :].astype(f32)
        for i in range(hp):
            cols = slice(i * DH, (i + 1) * DH)
            bq, bv = b[:, cols], b[:, hw + i * DH : hw + (i + 1) * DH]
            q = (qkv[:, cols] + bq).astype(bf16)
            q_s[s * hp + i] = (q.astype(f32) * (DH**-0.5)).astype(bf16)
            k_s[s * hp + i] = qkv[:, hw + i * DH : hw + (i + 1) * DH].astype(bf16)
            v_s[s * hp + i] = (qkv[:, 2 * hw + i * DH : 2 * hw + (i + 1) * DH] + bv).astype(bf16)

        def head(i):
            h = s * hp + i
            k, v = k_s[h], v_s[h]
            for c in range(planes):
                span = pl.ds(c * block, block)
                scores = dot(q_s[h, span, :], k, NT) + mask[span, :]
                e = jnp.exp(scores - jnp.max(scores, axis=1, keepdims=True))
                p = (e / jnp.sum(e, axis=1, keepdims=True)).astype(bf16)
                p_s[h, span, :] = p
                o3[i, span, :] = dot(p, v).astype(bf16)

        each(hp, head)
        o = jnp.concatenate([o3[i] for i in range(hp)], axis=1)
        o_s[s] = o
        acc[...] += dot(o, a_w[s, 3 * hw :, :])

    each(planes, attention)
    start(
        [
            leave(10, q_s, q_out),
            leave(11, k_s, k_out),
            leave(12, v_s, v_out),
            leave(13, p_s, p_out),
            leave(14, o_s, o_out),
            leave(15, a_w, a_out),
        ]
    )

    vec = lambda i: vec_ref[i : i + 1, :]

    def first_norm(c):
        span = pl.ds(pl.multiple_of(c * block, block), block)
        v = acc[span, :]
        v = v - jnp.mean(v, axis=1, keepdims=True)
        rstd = lax.rsqrt(jnp.mean(v * v, axis=1, keepdims=True) + EPSILON)
        xhat = v * rstd
        rstd_ref[span, :] = rstd
        xhat_s[span, :] = xhat
        h = xhat * vec(2) + vec(3)
        hb_s[span, :] = h.astype(bf16)
        acc[span, :] = h + vec(1)

    each(planes, first_norm)
    start([leave(16, xhat_s, xhat_out), leave(17, hb_s, hb_out)])
    arrive(s2[2])
    start(cc[2])
    arrive(cc[1])
    start([leave(18, u_w, u_out)])

    def up(j):
        s = place.plane(j)
        for c in range(planes):
            span = pl.ds(c * block, block)
            z = dot(hb_s[span, :], u_w[s]) + bias[s, 0:1, :].astype(f32)
            phi = 0.5 + 0.5 * lax.erf(z * (0.5**0.5))
            act_s[s, span, :] = (z * phi).astype(bf16)
            slope_s[s, span, :] = (phi + z * jnp.exp(-0.5 * z * z) * 0.3989422804014327).astype(
                bf16
            )

    each(planes, up)
    start([leave(19, act_s, act_out), leave(20, slope_s, slope_out)])
    arrive(cc[2])
    start([leave(21, d_w, d_out)])

    def down(s):
        acc[...] += dot(act_s[s], d_w[s])

    each(planes, down)
    arrive(c_send)

    zero = jnp.zeros((1, width), f32)

    def second_norm(c, sums):
        span = pl.ds(pl.multiple_of(c * block, block), block)
        v = acc[span, :]
        v = v - jnp.mean(v, axis=1, keepdims=True)
        rstd = lax.rsqrt(jnp.mean(v * v, axis=1, keepdims=True) + EPSILON)
        xhat = v * rstd
        y_s[c] = (xhat * vec(4) + vec(5)).astype(bf16)
        g = cs[c].astype(f32)
        d = g * vec(4)
        g2 = rstd * (
            d
            - jnp.mean(d, axis=1, keepdims=True)
            - xhat * jnp.mean(d * xhat, axis=1, keepdims=True)
        )
        acc[span, :] = g2
        add = lambda v: jnp.sum(v, axis=0, keepdims=True)
        return sums[0] + add(g * xhat), sums[1] + add(g), sums[2] + add(g2)

    sums = lax.fori_loop(0, planes, second_norm, (zero, zero, zero))
    small_ref[...] = jnp.concatenate(list(sums) + [jnp.zeros((5, width), f32)], axis=0)
    start([leave(22, acc, g2_out), leave(23, y_s, y_out)])
    for c in out_copies:
        c.wait()
    links.finish()


def forward_call(planes, heads, x_in, c_in, a_in, u_in, d_in, bias_in, vecs, qcode, kcode):
    block, width = x_in.shape[1:]
    rows = planes * block
    hw = heads // planes * DH
    shard = a_in.shape
    S = jax.ShapeDtypeStruct
    V = pltpu.VMEM
    outs = (
        S((planes, *shard), bf16),
        S((planes, *shard), bf16),
        S((planes, *shard), bf16),
        S((planes, block, width), bf16),
        S((heads, rows, DH), bf16),
        S((heads, rows, DH), bf16),
        S((heads, rows, DH), bf16),
        S((heads, rows, rows), bf16),
        S((planes, rows, hw), bf16),
        S((rows, width), f32),
        S((rows, width), bf16),
        S((planes, rows, shard[1]), bf16),
        S((planes, rows, shard[1]), bf16),
        S((rows, width), f32),
        S((planes, block, width), bf16),
        S((rows, 1), f32),
        S((8, width), f32),
    )
    any_spec = pl.BlockSpec(memory_space=pl.ANY)
    vmem_spec = pl.BlockSpec(memory_space=pltpu.VMEM)
    return pl.pallas_call(
        functools.partial(forward_kernel, planes, heads),
        out_shape=outs,
        in_specs=[any_spec] * 6 + [vmem_spec] * 3,
        out_specs=[any_spec] * 15 + [vmem_spec] * 2,
        scratch_shapes=[
            V((planes, *shard), bf16),
            V((planes, *shard), bf16),
            V((planes, *shard), bf16),
            V((planes, block, width), bf16),
            V((planes, block, width), bf16),
            V((planes, *bias_in.shape), bf16),
            V((heads, rows, DH), bf16),
            V((heads, rows, DH), bf16),
            V((heads, rows, DH), bf16),
            V((heads, rows, rows), bf16),
            V((planes, rows, hw), bf16),
            V((heads // planes, rows, DH), bf16),
            V((rows, rows), f32),
            V((rows, width), f32),
            V((rows, width), f32),
            V((rows, width), bf16),
            V((planes, rows, shard[1]), bf16),
            V((planes, rows, shard[1]), bf16),
            V((planes, block, width), bf16),
            pltpu.SemaphoreType.DMA((FORWARD_LINKS,)),
            pltpu.SemaphoreType.DMA((FORWARD_LINKS,)),
            pltpu.SemaphoreType.DMA((FORWARD_LOCALS,)),
        ],
        compiler_params=pltpu.CompilerParams(
            collective_id=0, has_side_effects=True, vmem_limit_bytes=62 * MIB
        ),
    )(x_in, c_in, a_in, u_in, d_in, bias_in, vecs, qcode, kcode)


BACKWARD_LINKS = 80
BACKWARD_LOCALS = 24
SMALL = 32


def backward_kernel(
    planes,
    heads,
    edges,
    a_in,
    u_in,
    d_in,
    x_in,
    q_in,
    k_in,
    v_in,
    p_in,
    o_in,
    xhat_in,
    hb_in,
    act_in,
    slope_in,
    g2_in,
    y_in,
    rstd_ref,
    small_in,
    vec_ref,
    flag_ref,
    ga_out,
    gu_out,
    gd_out,
    dx_out,
    y_out,
    small_ref,
    a_w,
    u_w,
    d_w,
    xs,
    q_s,
    k_s,
    v_s,
    p2,
    o_s,
    xhat_s,
    hb_s,
    act2,
    dz_s,
    acc,
    gb_s,
    dxs,
    do3,
    delta3,
    d9,
    ds_s,
    full,
    half_in,
    pair_in,
    one_in,
    z_in,
    sm,
    sm_in,
    send,
    recv,
    local,
):
    place = Place(planes)
    t = place.t
    others = range(1, planes)
    block, width = xs.shape[1], xs.shape[2]
    rows = planes * block
    hp = heads // planes
    hw = hp * DH
    links = Links(send, recv)
    r = Rows(place, a_w.shape[1])
    piece, half = r.piece, r.half
    weights = (a_w, u_w, d_w)
    g_outs = (ga_out, gu_out, gd_out)

    def keep(k, src, dst):
        return pltpu.make_async_copy(src, dst, local.at[k])

    get = lambda k, src, dst: keep(k, src, dst)
    load_g2 = get(0, g2_in, acc)
    load_d = get(1, d_in, d_w)
    load_u = get(2, u_in, u_w)
    load_a = get(3, a_in, a_w)
    load_hb = get(4, hb_in, hb_s)
    load_xhat = get(5, xhat_in, xhat_s)
    load_o = get(6, o_in, o_s)
    load_qkv = [get(7, q_in, q_s), get(8, k_in, k_s), get(9, v_in, v_s)]
    load_x = get(10, x_in, xs)
    load_slope = get(11, slope_in, dz_s)
    act_load = lambda s: keep(12 + s % 2, act_in.at[s], act2.at[s % 2])
    p_load = lambda h: keep(14 + h % 2, p_in.at[h], p2.at[h % 2])

    start([load_g2, load_d, load_slope])
    act_load(0).start()
    start([load_hb, load_u, load_xhat, load_a, load_o, *load_qkv, load_x])

    class Way:
        pass

    ways = []
    for w in range(3):
        g = weights[w]
        way = Way()
        way.core = [
            links.copy(g.at[s, pl.ds(r.others, half)], half_in.at[w, s], place.to_core)
            for s in range(planes)
        ]
        way.pair = [
            links.copy(g.at[:, pl.ds(r.a_far_pair, 2 * piece)], pair_in.at[w, 0], place.to_y),
            links.copy(g.at[:, pl.ds(r.b_far_pair, 2 * piece)], pair_in.at[w, 1], place.to_x),
        ]
        way.one = [
            links.copy(g.at[:, pl.ds(r.a_far, piece)], one_in.at[w, 0], place.to_x),
            links.copy(g.at[:, pl.ds(r.b_far, piece)], one_in.at[w, 1], place.to_y),
        ]
        way.z = []
        for j in others:
            for i, at in enumerate((r.a, r.b)):
                way.z.append(
                    links.copy(
                        g.at[place.plane(j), pl.ds(at, piece)],
                        z_in.at[w, j - 1, i],
                        place.to_plane(j),
                    )
                )
        f = full.at[w]
        way.back1 = [
            links.copy(f.at[pl.ds(r.a, piece)], f.at[pl.ds(r.a, piece)], place.to_x),
            links.copy(f.at[pl.ds(r.b, piece)], f.at[pl.ds(r.b, piece)], place.to_y),
        ]
        way.back2 = [
            links.copy(
                f.at[pl.ds(r.a_pair, 2 * piece)], f.at[pl.ds(r.a_pair, 2 * piece)], place.to_y
            ),
            links.copy(
                f.at[pl.ds(r.b_pair, 2 * piece)], f.at[pl.ds(r.b_pair, 2 * piece)], place.to_x
            ),
        ]
        way.back3 = [
            links.copy(f.at[pl.ds(r.mine, half)], f.at[pl.ds(r.mine, half)], place.to_core)
        ]
        way.out = keep(16 + w, f, g_outs[w])
        ways.append(way)

    def add_rows(g, s, at, size, got):
        span = pl.ds(at, size)
        g[s, span, :] = (g[s, span, :].astype(f32) + got.astype(f32)).astype(bf16)

    def after_core(w):
        way, g = ways[w], weights[w]
        arrive(way.core)
        for c in way.core:
            c.wait_send()
        each(planes, lambda s: add_rows(g, s, r.mine, half, half_in[w, s]))
        start(way.pair)

    def after_pair(w):
        way, g = ways[w], weights[w]
        arrive(way.pair)

        def add(s):
            add_rows(g, s, r.a_pair, 2 * piece, pair_in[w, 0, s])
            add_rows(g, s, r.b_pair, 2 * piece, pair_in[w, 1, s])

        each(planes, add)
        start(way.one)

    def after_one(w):
        way, g = ways[w], weights[w]
        arrive(way.one)

        def add(s):
            add_rows(g, s, r.a, piece, one_in[w, 0, s])
            add_rows(g, s, r.b, piece, one_in[w, 1, s])

        each(planes, add)
        start(way.z)

    def after_z(w):
        way, g = ways[w], weights[w]
        arrive(way.z)
        for i, at in enumerate((r.a, r.b)):
            v = g[t, pl.ds(at, piece), :].astype(f32)
            for j in others:
                v = v + z_in[w, j - 1, i].astype(f32)
            full[w, pl.ds(at, piece), :] = v.astype(bf16)
        start(way.back1)

    def after_back1(w):
        arrive(ways[w].back1)
        start(ways[w].back2)

    def after_back2(w):
        arrive(ways[w].back2)
        start(ways[w].back3)

    def after_back3(w):
        arrive(ways[w].back3)
        ways[w].out.start()

    y_send = [links.copy(y_in.at[place.plane(j)], y_out.at[t], place.to_plane(j)) for j in others]
    dx_send = [links.copy(dxs.at[place.plane(j)], dx_out.at[t], place.to_plane(j)) for j in others]
    own_y = keep(19, y_in.at[t], y_out.at[t])
    own_dx = keep(20, dxs.at[t], dx_out.at[t])
    small_hop = [
        [links.copy(sm.at[0], sm_in.at[0], place.to_core)],
        [links.copy(sm.at[1], sm_in.at[1], place.to_x)],
        [links.copy(sm.at[2], sm_in.at[2], place.to_y)],
        [links.copy(sm.at[3], sm_in.at[2 + j], place.to_plane(j)) for j in others],
    ]

    place.greet()

    load_g2.wait()
    for c in range(planes):
        span = pl.ds(c * block, block)
        gb_s[span, :] = acc[span, :].astype(bf16)
    load_d.wait()
    load_slope.wait()
    sm[0] = jnp.zeros((SMALL, width), f32)
    sm[0, 0:3, :] = small_in[0:3, :]

    def down(s):
        act_load(s).wait()

        @pl.when(s + 1 < planes)
        def _():
            act_load(s + 1).start()

        for c in range(planes):
            span = pl.ds(c * block, block)
            du = dot(gb_s[span, :], d_w[s], NT)
            dz_s[s, span, :] = (du * dz_s[s, span, :].astype(f32)).astype(bf16)
        d_w[s] = dot(act2[s % 2], gb_s[...], TN).astype(bf16)
        for k in range(planes):
            pl.when(s == k)(ways[2].core[k].start)

    each(planes, down)
    load_hb.wait()
    load_u.wait()

    def up(s):
        dz = dz_s[s]
        sm[0, pl.ds(6 + s, 1), :] = jnp.sum(dz.astype(f32), axis=0, keepdims=True)
        acc[...] += dot(dz, u_w[s], NT)
        u_w[s] = dot(hb_s[...], dz, TN).astype(bf16)
        for k in range(planes):
            pl.when(s == k)(ways[1].core[k].start)

        @pl.when(s == 1)
        def _():
            after_core(2)

    each(planes, up)
    load_xhat.wait()
    p_load(0).start()

    zero = jnp.zeros((1, width), f32)
    vec = lambda i: vec_ref[i : i + 1, :]

    def first_norm(c, sums):
        span = pl.ds(pl.multiple_of(c * block, block), block)
        xhat = xhat_s[span, :]
        g = acc[span, :]
        d = g * vec(2)
        g1 = rstd_ref[span, :] * (
            d
            - jnp.mean(d, axis=1, keepdims=True)
            - xhat * jnp.mean(d * xhat, axis=1, keepdims=True)
        )
        acc[span, :] = g1
        gb_s[span, :] = g1.astype(bf16)
        add = lambda v: jnp.sum(v, axis=0, keepdims=True)
        return sums[0] + add(g * xhat), sums[1] + add(g), sums[2] + add(g1)

    sums = lax.fori_loop(0, planes, first_norm, (zero, zero, zero))
    sm[0, 3:6, :] = jnp.concatenate(list(sums), axis=0)
    after_core(1)
    start(y_send)
    own_y.start()
    for c in (load_a, load_o, *load_qkv, load_x):
        c.wait()

    def attention(s):
        wo = a_w[s, 3 * hw :, :]
        do = dot(gb_s[...], wo, NT).astype(bf16)
        o = o_s[s]
        prod = do.astype(f32) * o.astype(f32)
        for i in range(hp):
            cols = slice(i * DH, (i + 1) * DH)
            do3[i] = do[:, cols]
            delta3[i] = jnp.sum(prod[:, cols], axis=1, keepdims=True)

        def head(i):
            h = s * hp + i
            p_load(h).wait()

            @pl.when(h + 1 < heads)
            def _():
                p_load(h + 1).start()

            pl.when(h == 1)(lambda: after_pair(2))
            pl.when(h == 3)(lambda: after_one(2))
            pl.when(h == 5)(lambda: after_pair(1))
            pl.when(h == 7)(lambda: (after_one(1), after_z(2)) and None)
            pl.when(h == 8)(lambda: after_back1(2))
            pl.when(h == 9)(lambda: after_back2(2))
            pl.when(h == 10)(lambda: after_back3(2))
            pl.when(h == 11)(lambda: after_z(1))

            slot = h % 2
            k, v = k_s[h], v_s[h]
            for c in range(planes):
                span = pl.ds(c * block, block)
                dp = dot(do3[i, span, :], v, NT)
                ds = (p2[slot, span, :].astype(f32) * (dp - delta3[i, span, :])).astype(bf16)
                ds_s[span, :] = ds
                d9[i, span, :] = (dot(ds, k) * (DH**-0.5)).astype(bf16)
            d9[hp + i] = dot(ds_s[...], q_s[h], TN).astype(bf16)
            d9[2 * hp + i] = dot(p2[slot], do3[i], TN).astype(bf16)

        each(hp, head)
        dqkv = jnp.concatenate([d9[i] for i in range(3 * hp)], axis=1)
        sums = jnp.sum(dqkv.astype(f32), axis=0, keepdims=True)
        sm[0, pl.ds(10 + s, 1), 0:hw] = sums[:, 0:hw]
        sm[0, pl.ds(10 + s, 1), hw : 2 * hw] = sums[:, 2 * hw :]
        acc[...] += dot(dqkv, a_w[s, 0 : 3 * hw, :])
        a_w[s, 0 : 3 * hw, :] = dot(dqkv, xs[...].reshape(rows, width), TN).astype(bf16)
        a_w[s, 3 * hw :, :] = dot(o, gb_s[...], TN).astype(bf16)
        for k in range(planes):
            pl.when(s == k)(ways[0].core[k].start)

    each(planes, attention)

    mem, first, last = edges
    flag = flag_ref[0:1, 0:1]
    sm[0, 14 : 14 + mem, :] = (acc[first : first + mem, :] + acc[last : last + mem, :]) * flag
    start(small_hop[0])
    for c in range(planes):
        dxs[c] = acc[pl.ds(c * block, block), :].astype(bf16)
    start(dx_send)
    own_dx.start()
    after_core(0)

    arrive(small_hop[0])
    sm[1] = sm[0] + sm_in[0]
    start(small_hop[1])
    after_back1(1)
    arrive(small_hop[1])
    sm[2] = sm[1] + sm_in[1]
    start(small_hop[2])
    after_back2(1)
    after_pair(0)
    arrive(small_hop[2])
    sm[3] = sm[2] + sm_in[2]
    start(small_hop[3])
    after_back3(1)
    after_one(0)
    arrive(small_hop[3])
    total = sm[3]
    parts = [sm[3]] + [sm_in[2 + j] for j in others]
    total = jnp.zeros((SMALL, width), f32)
    for s in range(planes):
        for j in range(planes):
            hit = lax.rem(t + planes - j, planes) == s
            total = total + jnp.where(hit, parts[j], 0.0)
    small_ref[...] = total
    after_z(0)
    after_back1(0)
    after_back2(0)
    after_back3(0)

    arrive(y_send)
    arrive(dx_send)
    own_y.wait()
    own_dx.wait()
    for way in ways:
        way.out.wait()
    core_waited = {id(c) for way in ways for c in way.core}
    for made in links.all:
        if id(made) not in core_waited:
            made.wait_send()


def backward_call(planes, heads, edges, saved, vecs, flag):
    a_w, x_s, q_s = saved[0], saved[3], saved[4]
    shard = a_w.shape[1:]
    block, width = x_s.shape[1:]
    rows = planes * block
    hp = heads // planes
    hw = hp * DH
    piece, half = shard[0] // (2 * INNER), shard[0] // 2
    S = jax.ShapeDtypeStruct
    V = pltpu.VMEM
    outs = (
        S(shard, bf16),
        S(shard, bf16),
        S(shard, bf16),
        S((planes, block, width), bf16),
        S((planes, block, width), bf16),
        S((SMALL, width), f32),
    )
    any_spec = pl.BlockSpec(memory_space=pl.ANY)
    vmem_spec = pl.BlockSpec(memory_space=pltpu.VMEM)
    return pl.pallas_call(
        functools.partial(backward_kernel, planes, heads, edges),
        out_shape=outs,
        in_specs=[any_spec] * 15 + [vmem_spec] * 4,
        out_specs=[any_spec] * 5 + [vmem_spec],
        scratch_shapes=[
            V((planes, *shard), bf16),
            V((planes, *shard), bf16),
            V((planes, *shard), bf16),
            V((planes, block, width), bf16),
            V((heads, rows, DH), bf16),
            V((heads, rows, DH), bf16),
            V((heads, rows, DH), bf16),
            V((2, rows, rows), bf16),
            V((planes, rows, hw), bf16),
            V((rows, width), f32),
            V((rows, width), bf16),
            V((2, rows, shard[1]), bf16),
            V((planes, rows, shard[1]), bf16),
            V((rows, width), f32),
            V((rows, width), bf16),
            V((planes, block, width), bf16),
            V((hp, rows, DH), bf16),
            V((hp, rows, 1), f32),
            V((3 * hp, rows, DH), bf16),
            V((rows, rows), bf16),
            V((3, *shard), bf16),
            V((3, planes, half, shard[1]), bf16),
            V((3, 2, planes, 2 * piece, shard[1]), bf16),
            V((3, 2, planes, piece, shard[1]), bf16),
            V((3, planes - 1, 2, piece, shard[1]), bf16),
            V((4, SMALL, width), f32),
            V((2 + planes, SMALL, width), f32),
            pltpu.SemaphoreType.DMA((BACKWARD_LINKS,)),
            pltpu.SemaphoreType.DMA((BACKWARD_LINKS,)),
            pltpu.SemaphoreType.DMA((BACKWARD_LOCALS,)),
        ],
        compiler_params=pltpu.CompilerParams(
            collective_id=1, has_side_effects=True, vmem_limit_bytes=63 * MIB
        ),
    )(*saved, vecs, flag)


def shards(
    dp_size,
    planes,
    sequence,
    query_key_value_weight,
    qv_bias,
    output_weight,
    out_bias,
    up_weight,
    up_bias,
    down_weight,
    back_bias,
    gain_one,
    shift_one,
    gain_two,
    shift_two,
    init_memory,
    reset,
    starts,
    cotangent,
):
    segs, local_rows, width = sequence.shape
    mem = init_memory.shape[0]
    tokens = starts.shape[1]
    hw = query_key_value_weight.shape[2]
    heads = hw * planes // DH
    assert segs == planes and hw * 4 == width and dp_size % INNER == 0
    block = -(-local_rows // 16) * 16
    pad = ((0, 0), (0, block - local_rows), (0, 0))
    t = lax.axis_index("tensor")

    first_row = t * local_rows
    position = first_row + jnp.arange(local_rows, dtype=jnp.int32)
    is_memory = (position < mem) | (position >= mem + tokens)
    use_init = ((reset[:, None] > 0) & is_memory[None, :])[:, :, None]
    table = jnp.concatenate([init_memory, jnp.zeros((tokens, width), bf16), init_memory], 0)
    local_table = lax.dynamic_slice_in_dim(table, first_row, local_rows, 0)
    x_in = jnp.pad(jnp.where(use_init, local_table[None], sequence), pad)
    c_in = jnp.pad(cotangent, pad)

    a_in = jnp.concatenate(
        [query_key_value_weight.transpose(1, 2, 0).reshape(3 * hw, width), output_weight], 0
    )
    qv_row = jnp.concatenate([qv_bias.reshape(2 * hw), jnp.zeros((width - 2 * hw,), bf16)])
    bias_in = jnp.concatenate([up_bias[None], qv_row[None], jnp.zeros((14, width), bf16)], 0)
    zero = jnp.zeros((width,), bf16)
    vecs = jnp.stack(
        [out_bias, back_bias, gain_one, shift_one, gain_two, shift_two, zero, zero]
    ).astype(f32)

    own_starts = lax.dynamic_slice_in_dim(starts, t, 1, 0)[0]
    docs = jnp.cumsum(own_starts)
    marker = jnp.full((mem,), -1, jnp.int32)
    codes = jnp.concatenate([marker, docs, marker]).reshape(planes, local_rows)
    codes = jnp.pad(codes, ((0, 0), (0, block - local_rows)), constant_values=-2)
    codes = codes.reshape(planes * block)
    flag = jnp.broadcast_to(
        lax.dynamic_slice_in_dim((reset > 0).astype(f32), t, 1, 0)[:, None], (8, 128)
    )

    saved = forward_call(
        planes,
        heads,
        x_in,
        c_in,
        a_in,
        up_weight,
        down_weight,
        bias_in,
        vecs,
        codes[:, None],
        codes[None, :],
    )
    last = planes * local_rows - mem
    edges = (mem, 0, last // local_rows * block + last % local_rows)
    ga, gu, gd, dx, y, small = backward_call(planes, heads, edges, saved, vecs, flag)

    output = y[:, :local_rows]
    input_grad = jnp.where(use_init, 0.0, dx[:, :local_rows].astype(f32))
    ga, gu, gd = ga.astype(f32), gu.astype(f32), gd.astype(f32)
    if dp_size > INNER:
        groups = [[o * INNER + i for o in range(dp_size // INNER)] for i in range(INNER)]
        ga, gu, gd, small = lax.psum((ga, gu, gd, small), "dp", axis_index_groups=groups)
    own = lambda first: lax.dynamic_slice_in_dim(small, first + t, 1, 0)[0]
    return (
        output,
        input_grad,
        ga[: 3 * hw].reshape(3, hw, width).transpose(2, 0, 1),
        own(10)[: 2 * hw].reshape(2, hw),
        ga[3 * hw :],
        small[5],
        gu,
        own(6),
        gd,
        small[2],
        small[3],
        small[4],
        small[0],
        small[1],
        small[14 : 14 + mem],
    )


def solution(mesh):
    in_specs = (
        P("dp", "tensor", None),
        P(None, None, "tensor"),
        P(None, "tensor"),
        P("tensor", None),
        P(),
        P(None, "tensor"),
        P("tensor"),
        P("tensor", None),
        P(),
        P(),
        P(),
        P(),
        P(),
        P(),
        P("dp"),
        P("dp", None),
        P("dp", "tensor", None),
    )
    out_specs = (
        P("dp", "tensor", None),
        P("dp", "tensor", None),
        P(None, None, "tensor"),
        P(None, "tensor"),
        P("tensor", None),
        P(),
        P(None, "tensor"),
        P("tensor"),
        P("tensor", None),
        P(),
        P(),
        P(),
        P(),
        P(),
        P(),
    )
    return jax.shard_map(
        functools.partial(shards, mesh.shape["dp"], mesh.shape["tensor"]),
        mesh=mesh,
        in_specs=in_specs,
        out_specs=out_specs,
        check_vma=False,
    )
```

```python
import functools

import jax
import jax.numpy as jnp
from jax import lax
from jax.experimental import pallas as pl
from jax.experimental.pallas import tpu as pltpu
from jax.sharding import PartitionSpec as P

DH = 64
NEGATIVE = -1e30
EPSILON = 1e-05
INNER = 8
MIB = 1 << 20

f32 = jnp.float32
bf16 = jnp.bfloat16
NN = (((1,), (0,)), ((), ()))
NT = (((1,), (1,)), ((), ()))
TN = (((0,), (0,)), ((), ()))
MESH = pl.DeviceIdType.MESH


def dot(a, b, dims=NN):
    return lax.dot_general(a, b, dims, preferred_element_type=f32)


def each(count, body):
    def step(i, carry):
        body(i)
        return carry

    lax.fori_loop(0, count, step, 0)


class Place:
    def __init__(self, planes):
        self.planes = planes
        self.dp = lax.axis_index("dp")
        self.t = lax.axis_index("tensor")
        self.core = self.dp % 2
        self.x = (self.dp // 2) % 2
        self.y = (self.dp // 4) % 2
        self.to_core = (self.dp + 1 - 2 * self.core, self.t)
        self.to_x = (self.dp + 2 - 4 * self.x, self.t)
        self.to_y = (self.dp + 4 - 8 * self.y, self.t)

    def plane(self, j):
        return lax.rem(self.t + j, self.planes)

    def to_plane(self, j):
        return (self.dp, self.plane(j))

    def partners(self):
        return [self.to_core, self.to_x, self.to_y] + [
            self.to_plane(j) for j in range(1, self.planes)
        ]

    def greet(self):
        barrier = pltpu.get_barrier_semaphore()
        partners = self.partners()
        for device in partners:
            pl.semaphore_signal(barrier, inc=1, device_id=device, device_id_type=MESH)
        pl.semaphore_wait(barrier, len(partners))


class Rows:
    def __init__(self, place, rows):
        self.piece = rows // (2 * INNER)
        self.half = rows // 2
        quarter = rows // 4
        core, x, y = place.core, place.x, place.y
        at = lambda n: pl.multiple_of(n, 16)
        base = core * self.half
        self.mine = at(base)
        self.others = at((1 - core) * self.half)
        self.a = at(base + (2 * y + x) * self.piece)
        self.b = at(base + quarter + (2 * x + y) * self.piece)
        self.a_pair = at(base + 2 * y * self.piece)
        self.b_pair = at(base + quarter + 2 * x * self.piece)
        self.a_far_pair = at(base + 2 * (1 - y) * self.piece)
        self.b_far_pair = at(base + quarter + 2 * (1 - x) * self.piece)
        self.a_far = at(base + (2 * y + 1 - x) * self.piece)
        self.b_far = at(base + quarter + (2 * x + 1 - y) * self.piece)


class Links:
    def __init__(self, send, recv):
        self.send, self.recv, self.count, self.all = send, recv, 0, []

    def copy(self, src, dst, device, recv=None, only=None):
        k = self.count
        self.count += 1
        made = pltpu.make_async_remote_copy(
            src_ref=src,
            dst_ref=dst,
            send_sem=self.send.at[k],
            recv_sem=self.recv.at[k] if recv is None else recv,
            device_id=device,
            device_id_type=MESH,
        )
        self.all.append((made, only))
        return made

    def finish(self, copies=None):
        for made, only in list(self.all):
            if copies is None or any(made is c for c in copies):
                self.all = [entry for entry in self.all if entry[0] is not made]
                if only is None:
                    made.wait_send()
                else:
                    pl.when(only)(made.wait_send)


def start(copies):
    for c in copies:
        c.start()


def arrive(copies):
    for c in copies:
        c.wait_recv()


class Way:
    pass


LINKS = 200
LOCALS = 24
SMALL = 32


def layer_kernel(
    planes,
    heads,
    edges,
    x_in,
    c_in,
    a_in,
    u_in,
    d_in,
    bias_in,
    vec_ref,
    qcode_ref,
    kcode_ref,
    flag_ref,
    ga_out,
    gu_out,
    gd_out,
    dx_out,
    y_out,
    p_hbm,
    small_ref,
    a_w,
    u_w,
    d_w,
    xs,
    cs,
    bias,
    q_s,
    k_s,
    v_s,
    p2,
    o_s,
    o3,
    delta3,
    d9,
    ds_s,
    mask,
    acc,
    xhat_s,
    rstd_s,
    hb_s,
    act_s,
    dz_s,
    gb_s,
    half_in,
    pair_in,
    one_in,
    z_in,
    sm,
    sm_in,
    send,
    recv,
    recv_z,
    local,
):
    place = Place(planes)
    t = place.t
    others = range(1, planes)
    block, width = xs.shape[1], xs.shape[2]
    rows = planes * block
    hp = heads // planes
    hw = hp * DH
    links = Links(send, recv)
    r = Rows(place, a_in.shape[0])
    piece, half = r.piece, r.half
    vec = lambda i: vec_ref[i : i + 1, :]
    add_up = lambda v: jnp.sum(v, axis=0, keepdims=True)

    def keep(k, src, dst):
        return pltpu.make_async_copy(src, dst, local.at[k])

    ins, weights, g_outs = (a_in, u_in, d_in), (a_w, u_w, d_w), (ga_out, gu_out, gd_out)

    low = t // 2
    mirror = lambda n: n + low * (planes - 1 - 2 * n)

    def slot_shard(i):
        return mirror(i - mirror(t) if i == 1 else i)

    def neighbour(to):
        inside = (to >= 0) & (to < planes)
        return (place.dp, lax.rem(to + planes, planes)), inside

    gather = []
    for w in range(3):
        way = Way()
        way.own, way.z, way.one, way.two, way.core = [], [], [], [], []
        for step in (1, -1):
            device, inside = neighbour(t + step)
            way.own.append(
                (
                    inside,
                    [
                        links.copy(
                            ins[w].at[pl.ds(at, piece)],
                            weights[w].at[t, pl.ds(at, piece)],
                            device,
                            recv_z.at[w, t, n],
                            inside,
                        )
                        for n, at in enumerate((r.a, r.b))
                    ],
                )
            )
        for i in others:
            s = slot_shard(i)
            below = (t - s + planes - 1) // planes
            device, inside = neighbour(t + 2 * below - 1)
            here = lambda at, size: weights[w].at[s, pl.ds(at, size)]
            same = lambda at, size, to: links.copy(here(at, size), here(at, size), to)
            way.z.append(
                (
                    inside,
                    [
                        links.copy(
                            here(at, piece), here(at, piece), device, recv_z.at[w, s, n], inside
                        )
                        for n, at in enumerate((r.a, r.b))
                    ],
                )
            )
            way.one.append([same(r.a, piece, place.to_x), same(r.b, piece, place.to_y)])
            way.two.append(
                [same(r.a_pair, 2 * piece, place.to_y), same(r.b_pair, 2 * piece, place.to_x)]
            )
            way.core.append([same(r.mine, half, place.to_core)])
        gather.append(way)

    def when_start(inside, copies):
        pl.when(inside)(lambda: start(copies))

    def get_own(w):
        for inside, copies in gather[w].own:
            when_start(inside, copies)

    def get_z(w, i):
        inside, copies = gather[w].z[i - 1]
        arrive(copies)
        when_start(inside, copies)
        start(gather[w].one[i - 1])

    def get_one(w, i):
        arrive(gather[w].one[i - 1])
        start(gather[w].two[i - 1])

    def get_two(w, i):
        arrive(gather[w].two[i - 1])
        start(gather[w].core[i - 1])

    def get_core(w, i):
        arrive(gather[w].core[i - 1])

    def release(w):
        way = gather[w]
        links.finish([c for _, z in way.z for c in z])
        links.finish([c for part in way.one + way.two + way.core for c in part])

    ways = []
    for w in range(3):
        g = weights[w]
        way = Way()
        if w == 0:
            way.core, way.pair, way.one, way.z = [], [], [], []
            for i in range(planes):
                s = place.plane(i + 1)
                cut = lambda at, size: g.at[s, pl.ds(at, size)]
                way.core.append(
                    [links.copy(cut(r.others, half), half_in.at[0, i], place.to_core)]
                )
                way.pair.append(
                    [
                        links.copy(cut(r.a_far_pair, 2 * piece), pair_in.at[0, 0, i], place.to_y),
                        links.copy(cut(r.b_far_pair, 2 * piece), pair_in.at[0, 1, i], place.to_x),
                    ]
                )
                way.one.append(
                    [
                        links.copy(cut(r.a_far, piece), one_in.at[0, 0, i], place.to_x),
                        links.copy(cut(r.b_far, piece), one_in.at[0, 1, i], place.to_y),
                    ]
                )
                if i + 1 < planes:
                    to = place.to_plane(i + 1)
                    way.z.append(
                        [
                            links.copy(cut(r.a, piece), z_in.at[0, i, 0], to),
                            links.copy(cut(r.b, piece), z_in.at[0, i, 1], to),
                        ]
                    )
        else:
            way.core = [
                links.copy(g.at[s, pl.ds(r.others, half)], half_in.at[w, s], place.to_core)
                for s in range(planes)
            ]
            way.pair = [
                links.copy(g.at[:, pl.ds(r.a_far_pair, 2 * piece)], pair_in.at[w, 0], place.to_y),
                links.copy(g.at[:, pl.ds(r.b_far_pair, 2 * piece)], pair_in.at[w, 1], place.to_x),
            ]
            way.one = [
                links.copy(g.at[:, pl.ds(r.a_far, piece)], one_in.at[w, 0], place.to_x),
                links.copy(g.at[:, pl.ds(r.b_far, piece)], one_in.at[w, 1], place.to_y),
            ]
            way.z = []
            for j in others:
                for i, at in enumerate((r.a, r.b)):
                    way.z.append(
                        links.copy(
                            g.at[place.plane(j), pl.ds(at, piece)],
                            z_in.at[w, j - 1, i],
                            place.to_plane(j),
                        )
                    )
        at_home = lambda at: pl.multiple_of(at - r.mine, 16)
        f = half_in.at[w, 0]
        same = lambda at, size, to: links.copy(
            f.at[pl.ds(at_home(at), size)], f.at[pl.ds(at_home(at), size)], to
        )
        way.back1 = [same(r.a, piece, place.to_x), same(r.b, piece, place.to_y)]
        way.back2 = [
            same(r.a_pair, 2 * piece, place.to_y),
            same(r.b_pair, 2 * piece, place.to_x),
        ]
        mine = g_outs[w].at[pl.ds(r.mine, half)]
        way.back3 = [links.copy(f, mine, place.to_core)]
        way.out = keep(8 + w, f, mine)
        ways.append(way)

    def add_rows(g, s, at, size, got):
        span = pl.ds(at, size)
        g[s, span, :] = (g[s, span, :].astype(f32) + got.astype(f32)).astype(bf16)

    def after_core(w):
        way, g = ways[w], weights[w]
        arrive(way.core)
        each(planes, lambda s: add_rows(g, s, r.mine, half, half_in[w, s]))
        start(way.pair)

    def after_pair(w):
        way, g = ways[w], weights[w]
        arrive(way.pair)

        def add(s):
            add_rows(g, s, r.a_pair, 2 * piece, pair_in[w, 0, s])
            add_rows(g, s, r.b_pair, 2 * piece, pair_in[w, 1, s])

        each(planes, add)
        start(way.one)

    def after_one(w):
        way, g = ways[w], weights[w]
        arrive(way.one)

        def add(s):
            add_rows(g, s, r.a, piece, one_in[w, 0, s])
            add_rows(g, s, r.b, piece, one_in[w, 1, s])

        each(planes, add)
        start(way.z)

    def part_core(i):
        arrive(ways[0].core[i])
        add_rows(a_w, place.plane(i + 1), r.mine, half, half_in[0, i])
        start(ways[0].pair[i])

    def part_pair(i):
        arrive(ways[0].pair[i])
        s = place.plane(i + 1)
        add_rows(a_w, s, r.a_pair, 2 * piece, pair_in[0, 0, i])
        add_rows(a_w, s, r.b_pair, 2 * piece, pair_in[0, 1, i])
        start(ways[0].one[i])

    def part_one(i):
        arrive(ways[0].one[i])
        s = place.plane(i + 1)
        add_rows(a_w, s, r.a, piece, one_in[0, 0, i])
        add_rows(a_w, s, r.b, piece, one_in[0, 1, i])
        if i + 1 < planes:
            start(ways[0].z[i])

    def after_z(w):
        way, g = ways[w], weights[w]
        if w == 0:
            for z in way.z:
                arrive(z)
        else:
            arrive(way.z)
        for i, at in enumerate((r.a, r.b)):
            v = g[t, pl.ds(at, piece), :].astype(f32)
            for j in others:
                v = v + z_in[w, j - 1, i].astype(f32)
            half_in[w, 0, pl.ds(pl.multiple_of(at - r.mine, 16), piece), :] = v.astype(bf16)
        start(way.back1)

    def after_back1(w):
        arrive(ways[w].back1)
        start(ways[w].back2)

    def after_back2(w):
        arrive(ways[w].back2)
        start(ways[w].back3)
        ways[w].out.start()

    def after_back3(w):
        arrive(ways[w].back3)

    x_send = [links.copy(x_in.at[place.plane(j)], xs.at[t], place.to_plane(j)) for j in others]
    c_send = [links.copy(c_in.at[place.plane(j)], cs.at[t], place.to_plane(j)) for j in others]
    b_send = [links.copy(bias_in, bias.at[t], place.to_plane(j)) for j in others]
    y_send = [links.copy(cs.at[place.plane(j)], y_out.at[t], place.to_plane(j)) for j in others]
    dx_rows = lambda j: act_s.at[0, pl.ds(pl.multiple_of(place.plane(j) * block, 16), block)]
    dx_send = [links.copy(dx_rows(j), dx_out.at[t], place.to_plane(j)) for j in others]
    small_hop = [
        [links.copy(sm.at[0], sm_in.at[0], place.to_core)],
        [links.copy(sm.at[1], sm_in.at[1], place.to_x)],
        [links.copy(sm.at[2], sm_in.at[2], place.to_y)],
        [links.copy(sm.at[3], sm_in.at[2 + j], place.to_plane(j)) for j in others],
    ]
    own = [keep(w, ins[w], weights[w].at[t]) for w in range(3)]
    own_x = keep(3, x_in.at[t], xs.at[t])
    own_c = keep(4, c_in.at[t], cs.at[t])
    own_bias = keep(5, bias_in, bias.at[t])
    own_y = keep(6, cs.at[t], y_out.at[t])
    own_dx = keep(7, dx_rows(0), dx_out.at[t])

    def p_at(m):
        return p_hbm.at[m]

    p_save = lambda m: keep(12 + m % 2, p2.at[m % 2], p_at(m))

    start([own_x, *own, own_bias, own_c])
    place.greet()
    get_own(0)
    start(b_send)
    start(x_send)

    for c in range(planes):
        span = pl.ds(c * block, block)
        qc = qcode_ref[span, :]
        kc = kcode_ref[...]
        allowed = ((qc == kc) | (qc < 0) | (kc < 0)) & (kc != -2)
        mask[span, :] = jnp.where(allowed, 0.0, NEGATIVE)
    sm[0] = jnp.zeros((SMALL, width), f32)

    get_z(0, 1)
    get_z(0, 2)
    get_one(0, 1)
    get_z(0, 3)
    get_own(1)
    get_one(0, 2)
    get_two(0, 1)
    get_one(0, 3)
    get_two(0, 2)
    for c in (own_x, *own, own_bias, own_c):
        c.wait()
    arrive(x_send)
    arrive(b_send)
    acc[...] = xs[...].reshape(rows, width).astype(f32) + vec(0)

    forward_pokes = [
        (1, lambda: get_two(0, 3)),
        (1, lambda: get_z(1, 1)),
        (2, lambda: get_z(1, 2)),
        (3, lambda: get_one(1, 1)),
        (4, lambda: get_z(1, 3)),
        (4, lambda: get_own(2)),
        (5, lambda: get_one(1, 2)),
        (6, lambda: get_two(1, 1)),
        (6, lambda: get_z(2, 1)),
        (7, lambda: get_one(1, 3)),
        (8, lambda: get_two(1, 2)),
        (8, lambda: get_z(2, 2)),
        (9, lambda: get_one(2, 1)),
        (10, lambda: get_z(2, 3)),
        (10, lambda: start(c_send)),
        (10, lambda: get_two(1, 3)),
        (11, lambda: get_one(2, 2)),
    ]

    def forward_order(j):
        picked = t
        for i in others:
            picked = jnp.where(j == i, slot_shard(i), picked)
        return picked

    def attention(j):
        s = forward_order(j)
        for i in others:
            pl.when(j == i)(lambda: get_core(0, i))

        x = xs[...].reshape(rows, width)
        qkv = dot(x, a_w[s, 0 : 3 * hw, :], NT)
        b = bias[s, 1:2, :].astype(f32)
        for i in range(hp):
            cols = slice(i * DH, (i + 1) * DH)
            bq, bv = b[:, cols], b[:, hw + i * DH : hw + (i + 1) * DH]
            q = (qkv[:, cols] + bq).astype(bf16)
            q_s[s * hp + i] = (q.astype(f32) * (DH**-0.5)).astype(bf16)
            k_s[s * hp + i] = qkv[:, hw + i * DH : hw + (i + 1) * DH].astype(bf16)
            v_s[s * hp + i] = (qkv[:, 2 * hw + i * DH : 2 * hw + (i + 1) * DH] + bv).astype(bf16)

        def head(i):
            h = s * hp + i
            m = j * hp + i
            for n, poke in forward_pokes:
                pl.when(m == n)(poke)
            pl.when(m >= 2)(lambda: p_save(m).wait())
            k, v = k_s[h], v_s[h]
            for c in range(planes):
                span = pl.ds(c * block, block)
                scores = dot(q_s[h, span, :], k, NT) + mask[span, :]
                e = jnp.exp(scores - jnp.max(scores, axis=1, keepdims=True))
                p = (e / jnp.sum(e, axis=1, keepdims=True)).astype(bf16)
                p2[m % 2, span, :] = p
                o3[i, span, :] = dot(p, v).astype(bf16)
            keep(12 + m % 2, p2.at[m % 2], p_at(h)).start()

        each(hp, head)
        o = jnp.concatenate([o3[i] for i in range(hp)], axis=1)
        o_s[s] = o
        acc[...] += dot(o, a_w[s, 3 * hw :, :])

    each(planes, attention)

    def first_norm(c):
        span = pl.ds(pl.multiple_of(c * block, block), block)
        v = acc[span, :]
        v = v - jnp.mean(v, axis=1, keepdims=True)
        rstd = lax.rsqrt(jnp.mean(v * v, axis=1, keepdims=True) + EPSILON)
        xhat = v * rstd
        rstd_s[span, :] = rstd
        xhat_s[span, :] = xhat
        h = xhat * vec(2) + vec(3)
        hb_s[span, :] = h.astype(bf16)
        acc[span, :] = h + vec(1)

    each(planes, first_norm)
    get_one(2, 3)
    get_two(2, 1)

    def up(j):
        s = forward_order(j)
        for i in others:
            pl.when(j == i)(lambda: get_core(1, i))
        pl.when(j == 1)(lambda: get_two(2, 2))
        pl.when(j == 2)(lambda: get_two(2, 3))
        for c in range(planes):
            span = pl.ds(c * block, block)
            z = dot(hb_s[span, :], u_w[s]) + bias[s, 0:1, :].astype(f32)
            phi = 0.5 + 0.5 * lax.erf(z * (0.5**0.5))
            act_s[s, span, :] = (z * phi).astype(bf16)
            dz_s[s, span, :] = (phi + z * jnp.exp(-0.5 * z * z) * 0.3989422804014327).astype(bf16)

    each(planes, up)

    def down(j):
        s = forward_order(j)
        for i in others:
            pl.when(j == i)(lambda: get_core(2, i))
        acc[...] += dot(act_s[s], d_w[s])

    each(planes, down)
    arrive(c_send)

    zero = jnp.zeros((1, width), f32)

    def second_norm(c, sums):
        span = pl.ds(pl.multiple_of(c * block, block), block)
        v = acc[span, :]
        v = v - jnp.mean(v, axis=1, keepdims=True)
        rstd = lax.rsqrt(jnp.mean(v * v, axis=1, keepdims=True) + EPSILON)
        xhat = v * rstd
        g = cs[c].astype(f32)
        cs[c] = (xhat * vec(4) + vec(5)).astype(bf16)
        d = g * vec(4)
        g2 = rstd * (
            d
            - jnp.mean(d, axis=1, keepdims=True)
            - xhat * jnp.mean(d * xhat, axis=1, keepdims=True)
        )
        acc[span, :] = g2
        gb_s[span, :] = g2.astype(bf16)
        return sums[0] + add_up(g * xhat), sums[1] + add_up(g), sums[2] + add_up(g2)

    sums = lax.fori_loop(0, planes, second_norm, (zero, zero, zero))
    sm[0, 0:3, :] = jnp.concatenate(list(sums), axis=0)
    start(y_send)
    own_y.start()

    def back_down(s):
        for c in range(planes):
            span = pl.ds(c * block, block)
            du = dot(gb_s[span, :], d_w[s], NT)
            dz_s[s, span, :] = (du * dz_s[s, span, :].astype(f32)).astype(bf16)
        d_w[s] = dot(act_s[s], gb_s[...], TN).astype(bf16)
        for k in range(planes):
            pl.when(s == k)(ways[2].core[k].start)

    release(2)
    each(planes, back_down)

    def back_up(s):
        dz = dz_s[s]
        sm[0, pl.ds(6 + s, 1), :] = add_up(dz.astype(f32))
        acc[...] += dot(dz, u_w[s], NT)
        u_w[s] = dot(hb_s[...], dz, TN).astype(bf16)
        for k in range(planes):
            pl.when(s == k)(ways[1].core[k].start)
        pl.when(s == 1)(lambda: after_core(2))

    release(1)
    each(planes, back_up)
    for m in (heads - 2, heads - 1):
        p_save(m).wait()

    p_load = lambda m: keep(
        12 + m % 2, p_at(place.plane(m // hp + 1) * hp + m % hp), p2.at[m % 2]
    )
    p_load(0).start()

    def back_first_norm(c, sums):
        span = pl.ds(pl.multiple_of(c * block, block), block)
        xhat = xhat_s[span, :]
        g = acc[span, :]
        d = g * vec(2)
        g1 = rstd_s[span, :] * (
            d
            - jnp.mean(d, axis=1, keepdims=True)
            - xhat * jnp.mean(d * xhat, axis=1, keepdims=True)
        )
        acc[span, :] = g1
        gb_s[span, :] = g1.astype(bf16)
        return sums[0] + add_up(g * xhat), sums[1] + add_up(g), sums[2] + add_up(g1)

    sums = lax.fori_loop(0, planes, back_first_norm, (zero, zero, zero))
    sm[0, 3:6, :] = jnp.concatenate(list(sums), axis=0)
    after_core(1)

    back_pokes = [
        (1, lambda: after_pair(2)),
        (3, lambda: after_one(2)),
        (3, lambda: part_core(0)),
        (4, lambda: after_pair(1)),
        (5, lambda: part_pair(0)),
        (6, lambda: after_one(1)),
        (6, lambda: part_core(1)),
        (7, lambda: part_one(0)),
        (8, lambda: part_pair(1)),
        (8, lambda: after_z(2)),
        (9, lambda: after_back1(2)),
        (9, lambda: part_core(2)),
        (10, lambda: part_one(1)),
        (10, lambda: after_back2(2)),
        (11, lambda: part_pair(2)),
        (11, lambda: after_z(1)),
        (11, lambda: after_back3(2)),
    ]

    def back_attention(n):
        s = place.plane(n + 1)
        do = dot(gb_s[...], a_w[s, 3 * hw :, :], NT).astype(bf16)
        o = o_s[s]
        prod = do.astype(f32) * o.astype(f32)
        for i in range(hp):
            cols = slice(i * DH, (i + 1) * DH)
            o3[i] = do[:, cols]
            delta3[i] = jnp.sum(prod[:, cols], axis=1, keepdims=True)

        def head(i):
            h = s * hp + i
            m = n * hp + i
            p_load(m).wait()
            pl.when(m + 1 < heads)(lambda: p_load(m + 1).start())
            for k, poke in back_pokes:
                pl.when(m == k)(poke)
            slot = m % 2
            k, v = k_s[h], v_s[h]
            for c in range(planes):
                span = pl.ds(c * block, block)
                dp = dot(o3[i, span, :], v, NT)
                ds = (p2[slot, span, :].astype(f32) * (dp - delta3[i, span, :])).astype(bf16)
                ds_s[span, :] = ds
                d9[i, span, :] = (dot(ds, k) * (DH**-0.5)).astype(bf16)
            d9[hp + i] = dot(ds_s[...], q_s[h], TN).astype(bf16)
            d9[2 * hp + i] = dot(p2[slot], o3[i], TN).astype(bf16)

        each(hp, head)
        dqkv = jnp.concatenate([d9[i] for i in range(3 * hp)], axis=1)
        sums = add_up(dqkv.astype(f32))
        sm[0, pl.ds(10 + s, 1), 0:hw] = sums[:, 0:hw]
        sm[0, pl.ds(10 + s, 1), hw : 2 * hw] = sums[:, 2 * hw :]
        acc[...] += dot(dqkv, a_w[s, 0 : 3 * hw, :])
        a_w[s, 0 : 3 * hw, :] = dot(dqkv, xs[...].reshape(rows, width), TN).astype(bf16)
        a_w[s, 3 * hw :, :] = dot(o, gb_s[...], TN).astype(bf16)
        for k in range(planes):
            pl.when(n == k)(ways[0].core[k][0].start)

    release(0)
    each(planes, back_attention)

    for c in range(planes):
        span = pl.ds(c * block, block)
        act_s[0, span, :] = acc[span, :].astype(bf16)
    start(dx_send)
    own_dx.start()
    mem, first, last = edges
    flag = flag_ref[0:1, 0:1]
    sm[0, 14 : 14 + mem, :] = (acc[first : first + mem, :] + acc[last : last + mem, :]) * flag
    start(small_hop[0])
    part_core(3)
    part_one(2)
    after_back1(1)
    arrive(small_hop[0])
    sm[1] = sm[0] + sm_in[0]
    start(small_hop[1])
    after_back2(1)
    part_pair(3)
    arrive(small_hop[1])
    sm[2] = sm[1] + sm_in[1]
    start(small_hop[2])
    after_back3(1)
    part_one(3)
    after_z(0)
    arrive(small_hop[2])
    sm[3] = sm[2] + sm_in[2]
    start(small_hop[3])
    after_back1(0)
    after_back2(0)
    arrive(small_hop[3])
    parts = [sm[3]] + [sm_in[2 + j] for j in others]
    total = jnp.zeros((SMALL, width), f32)
    for s in range(planes):
        for j in range(planes):
            hit = lax.rem(t + planes - j, planes) == s
            total = total + jnp.where(hit, parts[j], 0.0)
    small_ref[...] = total
    after_back3(0)

    arrive(y_send)
    arrive(dx_send)
    own_y.wait()
    own_dx.wait()
    for way in ways:
        way.out.wait()
    links.finish()


def layer_call(planes, heads, edges, x_in, c_in, a_in, u_in, d_in, bias_in, small_ins):
    block, width = x_in.shape[1:]
    rows = planes * block
    hp = heads // planes
    hw = hp * DH
    shard = a_in.shape
    hidden = shard[1]
    piece, half = shard[0] // (2 * INNER), shard[0] // 2
    S = jax.ShapeDtypeStruct
    V = pltpu.VMEM
    outs = (
        S(shard, bf16),
        S(shard, bf16),
        S(shard, bf16),
        S((planes, block, width), bf16),
        S((planes, block, width), bf16),
        S((heads, rows, rows), bf16),
        S((SMALL, width), f32),
    )
    any_spec = pl.BlockSpec(memory_space=pl.ANY)
    vmem_spec = pl.BlockSpec(memory_space=pltpu.VMEM)
    return pl.pallas_call(
        functools.partial(layer_kernel, planes, heads, edges),
        out_shape=outs,
        in_specs=[any_spec] * 6 + [vmem_spec] * 4,
        out_specs=[any_spec] * 6 + [vmem_spec],
        scratch_shapes=[
            V((planes, *shard), bf16),
            V((planes, *shard), bf16),
            V((planes, *shard), bf16),
            V((planes, block, width), bf16),
            V((planes, block, width), bf16),
            V((planes, *bias_in.shape), bf16),
            V((heads, rows, DH), bf16),
            V((heads, rows, DH), bf16),
            V((heads, rows, DH), bf16),
            V((2, rows, rows), bf16),
            V((planes, rows, hw), bf16),
            V((hp, rows, DH), bf16),
            V((hp, rows, 1), f32),
            V((3 * hp, rows, DH), bf16),
            V((rows, rows), bf16),
            V((rows, rows), f32),
            V((rows, width), f32),
            V((rows, width), f32),
            V((rows, 1), f32),
            V((rows, width), bf16),
            V((planes, rows, hidden), bf16),
            V((planes, rows, hidden), bf16),
            V((rows, width), bf16),
            V((3, planes, half, hidden), bf16),
            V((3, 2, planes, 2 * piece, hidden), bf16),
            V((3, 2, planes, piece, hidden), bf16),
            V((3, planes - 1, 2, piece, hidden), bf16),
            V((4, SMALL, width), f32),
            V((2 + planes, SMALL, width), f32),
            pltpu.SemaphoreType.DMA((LINKS,)),
            pltpu.SemaphoreType.DMA((LINKS,)),
            pltpu.SemaphoreType.DMA((3, planes, 2)),
            pltpu.SemaphoreType.DMA((LOCALS,)),
        ],
        compiler_params=pltpu.CompilerParams(
            collective_id=0, has_side_effects=True, vmem_limit_bytes=63 * MIB
        ),
    )(x_in, c_in, a_in, u_in, d_in, bias_in, *small_ins)


def shards(
    dp_size,
    planes,
    sequence,
    query_key_value_weight,
    qv_bias,
    output_weight,
    out_bias,
    up_weight,
    up_bias,
    down_weight,
    back_bias,
    gain_one,
    shift_one,
    gain_two,
    shift_two,
    init_memory,
    reset,
    starts,
    cotangent,
):
    segs, local_rows, width = sequence.shape
    mem = init_memory.shape[0]
    tokens = starts.shape[1]
    hw = query_key_value_weight.shape[2]
    heads = hw * planes // DH
    assert segs == planes == 4 and hw * 4 == width and dp_size % INNER == 0
    block = -(-local_rows // 16) * 16
    pad = ((0, 0), (0, block - local_rows), (0, 0))
    t = lax.axis_index("tensor")

    first_row = t * local_rows
    position = first_row + jnp.arange(local_rows, dtype=jnp.int32)
    is_memory = (position < mem) | (position >= mem + tokens)
    use_init = ((reset[:, None] > 0) & is_memory[None, :])[:, :, None]
    table = jnp.concatenate([init_memory, jnp.zeros((tokens, width), bf16), init_memory], 0)
    local_table = lax.dynamic_slice_in_dim(table, first_row, local_rows, 0)
    x_in = jnp.pad(jnp.where(use_init, local_table[None], sequence), pad)
    c_in = jnp.pad(cotangent, pad)

    a_in = jnp.concatenate(
        [query_key_value_weight.transpose(1, 2, 0).reshape(3 * hw, width), output_weight], 0
    )
    qv_row = jnp.concatenate([qv_bias.reshape(2 * hw), jnp.zeros((width - 2 * hw,), bf16)])
    bias_in = jnp.concatenate([up_bias[None], qv_row[None], jnp.zeros((14, width), bf16)], 0)
    zero = jnp.zeros((width,), bf16)
    vecs = jnp.stack(
        [out_bias, back_bias, gain_one, shift_one, gain_two, shift_two, zero, zero]
    ).astype(f32)

    own_starts = lax.dynamic_slice_in_dim(starts, t, 1, 0)[0]
    docs = jnp.cumsum(own_starts)
    marker = jnp.full((mem,), -1, jnp.int32)
    codes = jnp.concatenate([marker, docs, marker]).reshape(planes, local_rows)
    codes = jnp.pad(codes, ((0, 0), (0, block - local_rows)), constant_values=-2)
    codes = codes.reshape(planes * block)
    flag = jnp.broadcast_to(
        lax.dynamic_slice_in_dim((reset > 0).astype(f32), t, 1, 0)[:, None], (8, 128)
    )

    last = planes * local_rows - mem
    edges = (mem, 0, last // local_rows * block + last % local_rows)
    ga, gu, gd, dx, y, _, small = layer_call(
        planes,
        heads,
        edges,
        x_in,
        c_in,
        a_in,
        up_weight,
        down_weight,
        bias_in,
        (vecs, codes[:, None], codes[None, :], flag),
    )

    output = y[:, :local_rows]
    input_grad = jnp.where(use_init, 0.0, dx[:, :local_rows].astype(f32))
    ga, gu, gd = ga.astype(f32), gu.astype(f32), gd.astype(f32)
    if dp_size > INNER:
        groups = [[o * INNER + i for o in range(dp_size // INNER)] for i in range(INNER)]
        ga, gu, gd, small = lax.psum((ga, gu, gd, small), "dp", axis_index_groups=groups)
    own = lambda first: lax.dynamic_slice_in_dim(small, first + t, 1, 0)[0]
    return (
        output,
        input_grad,
        ga[: 3 * hw].reshape(3, hw, width).transpose(2, 0, 1),
        own(10)[: 2 * hw].reshape(2, hw),
        ga[3 * hw :],
        small[5],
        gu,
        own(6),
        gd,
        small[2],
        small[3],
        small[4],
        small[0],
        small[1],
        small[14 : 14 + mem],
    )


def solution(mesh):
    in_specs = (
        P("dp", "tensor", None),
        P(None, None, "tensor"),
        P(None, "tensor"),
        P("tensor", None),
        P(),
        P(None, "tensor"),
        P("tensor"),
        P("tensor", None),
        P(),
        P(),
        P(),
        P(),
        P(),
        P(),
        P("dp"),
        P("dp", None),
        P("dp", "tensor", None),
    )
    out_specs = (
        P("dp", "tensor", None),
        P("dp", "tensor", None),
        P(None, None, "tensor"),
        P(None, "tensor"),
        P("tensor", None),
        P(),
        P(None, "tensor"),
        P("tensor"),
        P("tensor", None),
        P(),
        P(),
        P(),
        P(),
        P(),
        P(),
    )
    return jax.shard_map(
        functools.partial(shards, mesh.shape["dp"], mesh.shape["tensor"]),
        mesh=mesh,
        in_specs=in_specs,
        out_specs=out_specs,
        check_vma=False,
    )
```

```python
import functools

import jax
import jax.numpy as jnp
from jax import lax
from jax.experimental import pallas as pl
from jax.experimental.pallas import tpu as pltpu
from jax.sharding import PartitionSpec as P

DH = 64
NEGATIVE = -1e30
EPSILON = 1e-05
INNER = 8
MIB = 1 << 20

f32 = jnp.float32
bf16 = jnp.bfloat16
NN = (((1,), (0,)), ((), ()))
NT = (((1,), (1,)), ((), ()))
TN = (((0,), (0,)), ((), ()))
MESH = pl.DeviceIdType.MESH


def dot(a, b, dims=NN):
    return lax.dot_general(a, b, dims, preferred_element_type=f32)


def each(count, body):
    def step(i, carry):
        body(i)
        return carry

    lax.fori_loop(0, count, step, 0)


class Place:
    def __init__(self, planes):
        self.planes = planes
        self.dp = lax.axis_index("dp")
        self.t = lax.axis_index("tensor")
        self.core = self.dp % 2
        self.x = (self.dp // 2) % 2
        self.y = (self.dp // 4) % 2
        self.to_core = (self.dp + 1 - 2 * self.core, self.t)
        self.to_x = (self.dp + 2 - 4 * self.x, self.t)
        self.to_y = (self.dp + 4 - 8 * self.y, self.t)

    def plane(self, j):
        return lax.rem(self.t + j, self.planes)

    def to_plane(self, j):
        return (self.dp, self.plane(j))

    def partners(self):
        return [self.to_core, self.to_x, self.to_y] + [
            self.to_plane(j) for j in range(1, self.planes)
        ]

    def greet(self):
        barrier = pltpu.get_barrier_semaphore()
        partners = self.partners()
        for device in partners:
            pl.semaphore_signal(barrier, inc=1, device_id=device, device_id_type=MESH)
        pl.semaphore_wait(barrier, len(partners))


class Rows:
    def __init__(self, place, rows):
        self.piece = rows // (2 * INNER)
        self.half = rows // 2
        quarter = rows // 4
        core, x, y = place.core, place.x, place.y
        at = lambda n: pl.multiple_of(n, 16)
        base = core * self.half
        self.mine = at(base)
        self.others = at((1 - core) * self.half)
        self.a = at(base + (2 * y + x) * self.piece)
        self.b = at(base + quarter + (2 * x + y) * self.piece)
        self.a_pair = at(base + 2 * y * self.piece)
        self.b_pair = at(base + quarter + 2 * x * self.piece)
        self.a_far_pair = at(base + 2 * (1 - y) * self.piece)
        self.b_far_pair = at(base + quarter + 2 * (1 - x) * self.piece)
        self.a_far = at(base + (2 * y + 1 - x) * self.piece)
        self.b_far = at(base + quarter + (2 * x + 1 - y) * self.piece)


class Links:
    def __init__(self, send, recv):
        self.send, self.recv, self.count, self.all = send, recv, 0, []

    def copy(self, src, dst, device, recv=None, only=None):
        k = self.count
        self.count += 1
        made = pltpu.make_async_remote_copy(
            src_ref=src,
            dst_ref=dst,
            send_sem=self.send.at[k],
            recv_sem=self.recv.at[k] if recv is None else recv,
            device_id=device,
            device_id_type=MESH,
        )
        self.all.append((made, only))
        return made

    def finish(self, copies=None):
        for made, only in list(self.all):
            if copies is None or any(made is c for c in copies):
                self.all = [entry for entry in self.all if entry[0] is not made]
                if only is None:
                    made.wait_send()
                else:
                    pl.when(only)(made.wait_send)


def start(copies):
    for c in copies:
        c.start()


def arrive(copies):
    for c in copies:
        c.wait_recv()


def mirror_end(t, low, planes):
    return t + low * (planes - 1 - 2 * t)


class Way:
    pass


LINKS = 200
LOCALS = 24
SMALL = 16


def layer_kernel(
    planes,
    heads,
    block,
    x_in,
    c_in,
    a_in,
    u_in,
    d_in,
    bias_in,
    init_ref,
    starts_ref,
    reset_ref,
    ga_out,
    gu_out,
    gd_out,
    dx_out,
    y_out,
    p_hbm,
    small_ref,
    a_w,
    u_w,
    d_w,
    xs,
    cs,
    x_s,
    bias,
    q_s,
    k_s,
    v_s,
    p2,
    o_s,
    o3,
    delta3,
    d9,
    ds_s,
    mask,
    acc,
    xhat_s,
    rstd_s,
    hb_s,
    act_s,
    dz_s,
    gb_s,
    half_in,
    pair_in,
    one_in,
    z_in,
    sm,
    sm_in,
    send,
    recv,
    recv_z,
    local,
):
    place = Place(planes)
    t = place.t
    others = range(1, planes)
    real, width = xs.shape[1:]
    rows = planes * block
    mem = init_ref.shape[0]
    hp = heads // planes
    hw = hp * DH
    links = Links(send, recv)
    r = Rows(place, a_in.shape[0])
    piece, half = r.piece, r.half
    vec = lambda i: bias_in[2 + i : 3 + i, :].astype(f32)
    add_up = lambda v: jnp.sum(v, axis=0, keepdims=True)

    def keep(k, src, dst):
        return pltpu.make_async_copy(src, dst, local.at[k])

    ins, weights, g_outs = (a_in, u_in, d_in), (a_w, u_w, d_w), (ga_out, gu_out, gd_out)

    low = t // 2
    middle = mirror_end(t, low, planes) == 1
    mirror = lambda n: n + low * (planes - 1 - 2 * n)

    def slot_shard(i):
        return mirror(i - mirror(t) if i == 1 else i)

    def neighbour(to):
        inside = (to >= 0) & (to < planes)
        return (place.dp, lax.rem(to + planes, planes)), inside

    gather = []
    for w in range(3):
        way = Way()
        way.own, way.z, way.one, way.two, way.core = [], [], [], [], []
        for step in (1, -1):
            device, inside = neighbour(t + step)
            way.own.append(
                (
                    inside,
                    [
                        links.copy(
                            ins[w].at[pl.ds(at, piece)],
                            weights[w].at[t, pl.ds(at, piece)],
                            device,
                            recv_z.at[w, t, n],
                            inside,
                        )
                        for n, at in enumerate((r.a, r.b))
                    ],
                )
            )
        for i in others:
            s = slot_shard(i)
            below = (t - s + planes - 1) // planes
            device, inside = neighbour(t + 2 * below - 1)
            here = lambda at, size: weights[w].at[s, pl.ds(at, size)]
            same = lambda at, size, to: links.copy(here(at, size), here(at, size), to)
            way.z.append(
                (
                    inside,
                    [
                        links.copy(
                            here(at, piece), here(at, piece), device, recv_z.at[w, s, n], inside
                        )
                        for n, at in enumerate((r.a, r.b))
                    ],
                )
            )
            way.one.append([same(r.a, piece, place.to_x), same(r.b, piece, place.to_y)])
            way.two.append(
                [same(r.a_pair, 2 * piece, place.to_y), same(r.b_pair, 2 * piece, place.to_x)]
            )
            way.core.append([same(r.mine, half, place.to_core)])
        gather.append(way)

    def when_start(inside, copies):
        pl.when(inside)(lambda: start(copies))

    def get_own(w):
        for inside, copies in gather[w].own:
            when_start(inside, copies)

    def get_z(w, i):
        inside, copies = gather[w].z[i - 1]
        arrive(copies)
        when_start(inside, copies)
        start(gather[w].one[i - 1])

    def get_stage(w, d):
        if d == 1:
            get_z(w, 1)
            pl.when(middle)(lambda: get_z(w, 2))
        elif d == 2:
            pl.when(middle)(lambda: get_z(w, 3))
            pl.when(~middle)(lambda: get_z(w, 2))
        else:
            pl.when(~middle)(lambda: get_z(w, 3))

    def get_one(w, i):
        arrive(gather[w].one[i - 1])
        start(gather[w].two[i - 1])

    def get_two(w, i):
        arrive(gather[w].two[i - 1])
        start(gather[w].core[i - 1])

    def get_core(w, i):
        arrive(gather[w].core[i - 1])

    def release(w):
        way = gather[w]
        links.finish([c for _, z in way.z for c in z])
        links.finish([c for part in way.one + way.two + way.core for c in part])

    def spread(sends, d):
        def go(plane, *picks):
            pl.when(t == plane)(lambda: start([sends[j - 1] for j in picks]))

        if d == 0:
            go(0, 1, 2, 3)
            go(3, 3, 2, 1)
        elif d == 1:
            go(1, 1, 2)
            go(2, 3, 2)
        else:
            go(1, 3)
            go(2, 1)

    back_order = (2, 1, 3, 0)
    ways = []
    for w in range(3):
        g = weights[w]
        way = Way()
        way.core, way.pair, way.one, way.z = [], [], [], []
        for i in range(planes):
            j = back_order[i]
            s = place.plane(j)
            cut = lambda at, size: g.at[s, pl.ds(at, size)]
            way.core.append([links.copy(cut(r.others, half), half_in.at[w, i], place.to_core)])
            way.pair.append(
                [
                    links.copy(cut(r.a_far_pair, 2 * piece), pair_in.at[w, 0, i], place.to_y),
                    links.copy(cut(r.b_far_pair, 2 * piece), pair_in.at[w, 1, i], place.to_x),
                ]
            )
            way.one.append(
                [
                    links.copy(cut(r.a_far, piece), one_in.at[w, 0, i], place.to_x),
                    links.copy(cut(r.b_far, piece), one_in.at[w, 1, i], place.to_y),
                ]
            )
            if i + 1 < planes:
                way.z.append(
                    [
                        links.copy(cut(r.a, piece), z_in.at[w, i, 0], place.to_plane(j)),
                        links.copy(cut(r.b, piece), z_in.at[w, i, 1], place.to_plane(j)),
                    ]
                )
        at_home = lambda at: pl.multiple_of(at - r.mine, 16)
        f = half_in.at[w, 0]
        same = lambda at, size, to: links.copy(
            f.at[pl.ds(at_home(at), size)], f.at[pl.ds(at_home(at), size)], to
        )
        way.back1 = [same(r.a, piece, place.to_x), same(r.b, piece, place.to_y)]
        way.back2 = [
            same(r.a_pair, 2 * piece, place.to_y),
            same(r.b_pair, 2 * piece, place.to_x),
        ]
        mine = g_outs[w].at[pl.ds(r.mine, half)]
        way.back3 = [links.copy(f, mine, place.to_core)]
        way.out = keep(8 + w, f, mine)
        ways.append(way)

    def add_rows(g, s, at, size, got):
        span = pl.ds(at, size)
        g[s, span, :] = (g[s, span, :].astype(f32) + got.astype(f32)).astype(bf16)

    def back_shard(n):
        j = 0
        for i in range(planes - 1):
            j = jnp.where(n == i, back_order[i], j)
        return place.plane(j)

    def part_core(w, i):
        arrive(ways[w].core[i])
        add_rows(weights[w], back_shard(i), r.mine, half, half_in[w, i])
        start(ways[w].pair[i])

    def part_pair(w, i):
        arrive(ways[w].pair[i])
        s = back_shard(i)
        add_rows(weights[w], s, r.a_pair, 2 * piece, pair_in[w, 0, i])
        add_rows(weights[w], s, r.b_pair, 2 * piece, pair_in[w, 1, i])
        start(ways[w].one[i])

    def part_one(w, i):
        arrive(ways[w].one[i])
        s = back_shard(i)
        add_rows(weights[w], s, r.a, piece, one_in[w, 0, i])
        add_rows(weights[w], s, r.b, piece, one_in[w, 1, i])
        if i + 1 < planes:
            start(ways[w].z[i])

    def after_z(w):
        for z in ways[w].z:
            arrive(z)
        for i, at in enumerate((r.a, r.b)):
            v = weights[w][t, pl.ds(at, piece), :].astype(f32)
            for j in others:
                v = v + z_in[w, j - 1, i].astype(f32)
            half_in[w, 0, pl.ds(pl.multiple_of(at - r.mine, 16), piece), :] = v.astype(bf16)
        start(ways[w].back1)

    def after_back1(w):
        arrive(ways[w].back1)
        start(ways[w].back2)

    def after_back2(w):
        arrive(ways[w].back2)
        start(ways[w].back3)
        ways[w].out.start()

    def after_back3(w):
        arrive(ways[w].back3)

    x_send = [links.copy(x_in.at[place.plane(j)], xs.at[t], place.to_plane(j)) for j in others]
    c_send = [links.copy(c_in.at[place.plane(j)], cs.at[t], place.to_plane(j)) for j in others]
    b_send = [links.copy(bias_in, bias.at[t], place.to_plane(j)) for j in others]
    y_send = [links.copy(cs.at[place.plane(j)], y_out.at[t], place.to_plane(j)) for j in others]
    dx_send = [links.copy(xs.at[place.plane(j)], dx_out.at[t], place.to_plane(j)) for j in others]
    hops = []
    for e in range(2):
        mine, got = sm.at[e], sm_in.at[e]
        hops.append(
            [
                [links.copy(mine.at[0], got.at[0], place.to_core)],
                [links.copy(mine.at[1], got.at[1], place.to_x)],
                [links.copy(mine.at[2], got.at[2], place.to_y)],
                [links.copy(mine.at[3], got.at[2 + j], place.to_plane(j)) for j in others],
            ]
        )

    def hop(e, n):
        arrive(hops[e][n])
        if n < 3:
            sm[e, n + 1] = sm[e, n] + sm_in[e, n]
            start(hops[e][n + 1])
            return
        parts = [sm[e, 3]] + [sm_in[e, 2 + j] for j in others]
        total = jnp.zeros_like(parts[0])
        for s in range(planes):
            for j in range(planes):
                hit = lax.rem(t + planes - j, planes) == s
                total = total + jnp.where(hit, parts[j], 0.0)
        small_ref[e * SMALL : (e + 1) * SMALL, :] = total

    own = [keep(w, ins[w], weights[w].at[t]) for w in range(3)]
    own_x = keep(3, x_in.at[t], xs.at[t])
    own_c = keep(4, c_in.at[t], cs.at[t])
    own_y = keep(6, cs.at[t], y_out.at[t])
    own_dx = keep(7, xs.at[t], dx_out.at[t])

    def p_at(m):
        return p_hbm.at[m]

    p_save = lambda m: keep(12 + m % 2, p2.at[m % 2], p_at(m))

    start([own_x, *own, own_c])
    place.greet()
    get_own(0)
    start(b_send)
    spread(x_send, 0)

    bias[t] = bias_in[...]
    tokens = starts_ref.shape[1]

    def token_of(shape, axis):
        n = lax.broadcasted_iota(jnp.int32, shape, axis)
        inside = n % block
        return (n // block) * real + inside - mem, inside

    upto, _ = token_of((tokens, rows), 1)
    begun = lax.broadcasted_iota(jnp.int32, (tokens, rows), 0) <= upto
    begun = jnp.where(begun, 1.0, 0.0).astype(bf16)
    own_starts = starts_ref[pl.ds(t, 1), :].astype(f32).astype(bf16)
    docs = dot(jnp.broadcast_to(own_starts, (8, tokens)), begun)

    def codes(docs, axis):
        token, inside = token_of(docs.shape, axis)
        docs = jnp.where((token < 0) | (token >= tokens), -1.0, docs)
        return jnp.where(inside >= real, -2.0, docs)

    kc = codes(docs, 1)[0:1, :]
    qcodes = codes(docs.T, 0)[:, 0:1]
    for c in range(planes):
        span = slice(c * block, (c + 1) * block)
        qc = qcodes[span, :]
        allowed = ((qc == kc) | (qc < 0) | (kc < 0)) & (kc != -2.0)
        mask[span, :] = jnp.where(allowed, 0.0, NEGATIVE)
    for e in range(2):
        sm[e, 0] = jnp.zeros((SMALL, width), f32)

    get_stage(0, 1)
    spread(x_send, 1)
    get_stage(0, 2)
    spread(x_send, 2)
    get_own(1)
    get_own(2)
    get_one(0, 1)
    get_one(0, 2)
    get_two(0, 1)
    get_stage(0, 3)
    get_two(0, 2)
    get_one(0, 3)
    for c in (own_x, *own, own_c):
        c.wait()
    arrive(x_send)
    arrive(b_send)
    afresh = reset_ref[t] > 0
    for c in range(planes):
        x_s[c, 0:real, :] = xs[c]
        x_s[c, real:block, :] = jnp.zeros((block - real, width), bf16)
    last = real - mem
    x_s[0, 0:mem, :] = jnp.where(afresh, init_ref[...], xs[0, 0:mem, :])
    x_s[planes - 1, last:real, :] = jnp.where(afresh, init_ref[...], xs[planes - 1, last:real, :])
    acc[...] = x_s[...].reshape(rows, width).astype(f32) + vec(0)

    forward_pokes = [
        (0, lambda: get_two(0, 3)),
        (1, lambda: get_stage(1, 1)),
        (2, lambda: get_stage(2, 1)),
        (2, lambda: spread(c_send, 0)),
        (2, lambda: spread(c_send, 1)),
        (3, lambda: get_one(1, 1)),
        (4, lambda: get_stage(1, 2)),
        (4, lambda: get_one(2, 1)),
        (5, lambda: get_two(1, 1)),
        (5, lambda: get_stage(2, 2)),
        (5, lambda: spread(c_send, 2)),
        (6, lambda: get_one(1, 2)),
        (7, lambda: get_two(2, 1)),
        (7, lambda: get_one(2, 2)),
        (8, lambda: get_two(1, 2)),
        (8, lambda: get_stage(1, 3)),
        (9, lambda: get_stage(2, 3)),
        (9, lambda: get_two(2, 2)),
        (10, lambda: get_one(1, 3)),
        (11, lambda: get_one(2, 3)),
    ]

    def forward_order(j):
        picked = t
        for i in others:
            picked = jnp.where(j == i, slot_shard(i), picked)
        return picked

    def attention(j):
        s = forward_order(j)
        for i in others:
            pl.when(j == i)(lambda: get_core(0, i))

        x = x_s[...].reshape(rows, width)
        qkv = dot(x, a_w[s, 0 : 3 * hw, :], NT)
        b = bias[s, 1:2, :].astype(f32)
        for i in range(hp):
            cols = slice(i * DH, (i + 1) * DH)
            bq, bv = b[:, cols], b[:, hw + i * DH : hw + (i + 1) * DH]
            q = (qkv[:, cols] + bq).astype(bf16)
            q_s[s * hp + i] = (q.astype(f32) * (DH**-0.5)).astype(bf16)
            k_s[s * hp + i] = qkv[:, hw + i * DH : hw + (i + 1) * DH].astype(bf16)
            v_s[s * hp + i] = (qkv[:, 2 * hw + i * DH : 2 * hw + (i + 1) * DH] + bv).astype(bf16)

        def head(i):
            h = s * hp + i
            m = j * hp + i
            for n, poke in forward_pokes:
                pl.when(m == n)(poke)
            pl.when(m >= 2)(lambda: p_save(m).wait())
            k, v = k_s[h], v_s[h]
            for c in range(planes):
                span = pl.ds(c * block, block)
                scores = dot(q_s[h, span, :], k, NT) + mask[span, :]
                e = jnp.exp(scores - jnp.max(scores, axis=1, keepdims=True))
                p = (e / jnp.sum(e, axis=1, keepdims=True)).astype(bf16)
                p2[m % 2, span, :] = p
                o3[i, span, :] = dot(p, v).astype(bf16)
            keep(12 + m % 2, p2.at[m % 2], p_at(h)).start()

        each(hp, head)
        o = jnp.concatenate([o3[i] for i in range(hp)], axis=1)
        o_s[s] = o
        acc[...] += dot(o, a_w[s, 3 * hw :, :])

    each(planes, attention)

    def first_norm(c):
        span = pl.ds(pl.multiple_of(c * block, block), block)
        v = acc[span, :]
        v = v - jnp.mean(v, axis=1, keepdims=True)
        rstd = lax.rsqrt(jnp.mean(v * v, axis=1, keepdims=True) + EPSILON)
        xhat = v * rstd
        rstd_s[span, :] = rstd
        xhat_s[span, :] = xhat
        h = xhat * vec(2) + vec(3)
        hb_s[span, :] = h.astype(bf16)
        acc[span, :] = h + vec(1)

    each(planes, first_norm)
    get_two(1, 3)

    def up(j):
        s = forward_order(j)
        for i in others:
            pl.when(j == i)(lambda: get_core(1, i))
        pl.when(j == 1)(lambda: get_two(2, 3))
        for c in range(planes):
            span = pl.ds(c * block, block)
            z = dot(hb_s[span, :], u_w[s]) + bias[s, 0:1, :].astype(f32)
            phi = 0.5 + 0.5 * lax.erf(z * (0.5**0.5))
            act_s[s, span, :] = (z * phi).astype(bf16)
            dz_s[s, span, :] = (phi + z * jnp.exp(-0.5 * z * z) * 0.3989422804014327).astype(bf16)

    each(planes, up)

    def down(j):
        s = forward_order(j)
        for i in others:
            pl.when(j == i)(lambda: get_core(2, i))
        acc[...] += dot(act_s[s], d_w[s])

    each(planes, down)
    arrive(c_send)

    zero = jnp.zeros((1, width), f32)

    def second_norm(c, sums):
        span = pl.ds(pl.multiple_of(c * block, block), block)
        v = acc[span, :]
        v = v - jnp.mean(v, axis=1, keepdims=True)
        rstd = lax.rsqrt(jnp.mean(v * v, axis=1, keepdims=True) + EPSILON)
        xhat = v * rstd
        gb_s[span, :] = jnp.zeros((block, width), bf16)
        gb_s[pl.ds(pl.multiple_of(c * block, block), real), :] = cs[c]
        g = gb_s[span, :].astype(f32)
        cs[c] = (xhat * vec(4) + vec(5)).astype(bf16)[0:real]
        d = g * vec(4)
        g2 = rstd * (
            d
            - jnp.mean(d, axis=1, keepdims=True)
            - xhat * jnp.mean(d * xhat, axis=1, keepdims=True)
        )
        acc[span, :] = g2
        gb_s[span, :] = g2.astype(bf16)
        return sums[0] + add_up(g * xhat), sums[1] + add_up(g), sums[2] + add_up(g2)

    sums = lax.fori_loop(0, planes, second_norm, (zero, zero, zero))
    sm[0, 0, 0:3, :] = jnp.concatenate(list(sums), axis=0)
    start(y_send)
    own_y.start()

    def poke_at(n, pokes):
        for k, poke in pokes:
            pl.when(n == k)(poke)

    down_pokes = [(2, lambda: part_core(2, 0)), (3, lambda: part_core(2, 1))]
    up_pokes = [
        (0, lambda: part_core(2, 2)),
        (0, lambda: part_pair(2, 0)),
        (1, lambda: part_core(2, 3)),
        (2, lambda: part_pair(2, 1)),
        (2, lambda: part_core(1, 0)),
        (3, lambda: part_core(1, 1)),
    ]

    def back_down(n):
        s = back_shard(n)
        poke_at(n, down_pokes)
        for c in range(planes):
            span = pl.ds(c * block, block)
            du = dot(gb_s[span, :], d_w[s], NT)
            dz_s[s, span, :] = (du * dz_s[s, span, :].astype(f32)).astype(bf16)
        d_w[s] = dot(act_s[s], gb_s[...], TN).astype(bf16)
        for k in range(planes):
            pl.when(n == k)(ways[2].core[k][0].start)

    release(2)
    each(planes, back_down)

    def back_up(n):
        s = back_shard(n)
        poke_at(n, up_pokes)
        dz = dz_s[s]
        sm[0, 0, pl.ds(6 + s, 1), :] = add_up(dz.astype(f32))
        acc[...] += dot(dz, u_w[s], NT)
        u_w[s] = dot(hb_s[...], dz, TN).astype(bf16)
        for k in range(planes):
            pl.when(n == k)(ways[1].core[k][0].start)

    release(1)
    each(planes, back_up)
    for m in (heads - 2, heads - 1):
        p_save(m).wait()

    p_load = lambda m: keep(
        12 + m % 2, p_at(back_shard(m // hp) * hp + m % hp), p2.at[m % 2]
    )
    p_load(0).start()

    def back_first_norm(c, sums):
        span = pl.ds(pl.multiple_of(c * block, block), block)
        xhat = xhat_s[span, :]
        g = acc[span, :]
        d = g * vec(2)
        g1 = rstd_s[span, :] * (
            d
            - jnp.mean(d, axis=1, keepdims=True)
            - xhat * jnp.mean(d * xhat, axis=1, keepdims=True)
        )
        acc[span, :] = g1
        gb_s[span, :] = g1.astype(bf16)
        return sums[0] + add_up(g * xhat), sums[1] + add_up(g), sums[2] + add_up(g1)

    sums = lax.fori_loop(0, planes, back_first_norm, (zero, zero, zero))
    sm[0, 0, 3:6, :] = jnp.concatenate(list(sums), axis=0)
    start(hops[0][0])
    part_pair(2, 2)
    part_one(2, 0)

    back_pokes = [
        (0, lambda: part_core(1, 2)),
        (0, lambda: part_pair(2, 3)),
        (1, lambda: part_core(1, 3)),
        (1, lambda: part_one(2, 1)),
        (1, lambda: hop(0, 0)),
        (2, lambda: part_pair(1, 0)),
        (3, lambda: part_pair(1, 1)),
        (3, lambda: part_one(2, 2)),
        (3, lambda: hop(0, 1)),
        (4, lambda: part_core(0, 0)),
        (5, lambda: part_pair(1, 2)),
        (5, lambda: part_one(2, 3)),
        (5, lambda: hop(0, 2)),
        (6, lambda: part_pair(1, 3)),
        (6, lambda: part_one(1, 0)),
        (7, lambda: part_core(0, 1)),
        (7, lambda: part_pair(0, 0)),
        (8, lambda: part_one(1, 1)),
        (9, lambda: part_one(1, 2)),
        (9, lambda: part_one(0, 0)),
        (9, lambda: part_pair(0, 1)),
        (10, lambda: part_core(0, 2)),
        (10, lambda: part_one(1, 3)),
        (10, lambda: after_z(2)),
        (11, lambda: part_one(0, 1)),
        (11, lambda: after_back1(2)),
    ]

    def back_attention(n):
        s = back_shard(n)
        do = dot(gb_s[...], a_w[s, 3 * hw :, :], NT).astype(bf16)
        o = o_s[s]
        prod = do.astype(f32) * o.astype(f32)
        for i in range(hp):
            cols = slice(i * DH, (i + 1) * DH)
            o3[i] = do[:, cols]
            delta3[i] = jnp.sum(prod[:, cols], axis=1, keepdims=True)

        def head(i):
            h = s * hp + i
            m = n * hp + i
            p_load(m).wait()
            pl.when(m + 1 < heads)(lambda: p_load(m + 1).start())
            poke_at(m, back_pokes)
            slot = m % 2
            k, v = k_s[h], v_s[h]
            for c in range(planes):
                span = pl.ds(c * block, block)
                dp = dot(o3[i, span, :], v, NT)
                ds = (p2[slot, span, :].astype(f32) * (dp - delta3[i, span, :])).astype(bf16)
                ds_s[span, :] = ds
                d9[i, span, :] = (dot(ds, k) * (DH**-0.5)).astype(bf16)
            d9[hp + i] = dot(ds_s[...], q_s[h], TN).astype(bf16)
            d9[2 * hp + i] = dot(p2[slot], o3[i], TN).astype(bf16)

        each(hp, head)
        dqkv = jnp.concatenate([d9[i] for i in range(3 * hp)], axis=1)
        sums = add_up(dqkv.astype(f32))
        sm[1, 0, pl.ds(10 + s, 1), 0:hw] = sums[:, 0:hw]
        sm[1, 0, pl.ds(10 + s, 1), hw : 2 * hw] = sums[:, 2 * hw :]
        acc[...] += dot(dqkv, a_w[s, 0 : 3 * hw, :])
        a_w[s, 0 : 3 * hw, :] = dot(dqkv, x_s[...].reshape(rows, width), TN).astype(bf16)
        a_w[s, 3 * hw :, :] = dot(o, gb_s[...], TN).astype(bf16)
        for k in range(planes):
            pl.when(n == k)(ways[0].core[k][0].start)

    release(0)
    each(planes, back_attention)

    for c in range(planes):
        xs[c] = acc[c * block : c * block + real, :].astype(bf16)
    start(dx_send[1:2])
    own_dx.start()
    dx_last = (planes - 1) * block + last
    both = acc[0:mem, :] + acc[dx_last : dx_last + mem, :]
    sm[1, 0, 0:mem, :] = jnp.where(afresh, both, 0.0)
    start(hops[1][0])
    part_core(0, 3)
    part_pair(0, 2)
    hop(1, 0)
    after_z(1)
    after_back2(2)
    part_one(0, 2)
    part_pair(0, 3)
    start(dx_send[0:1])
    hop(1, 1)
    after_back1(1)
    hop(1, 2)
    start(dx_send[2:3])
    part_one(0, 3)
    after_back2(1)
    after_z(0)
    after_back1(0)
    hop(0, 3)
    after_back3(2)
    after_back2(0)
    hop(1, 3)
    after_back3(1)
    after_back3(0)

    arrive(y_send)
    arrive(dx_send)
    own_y.wait()
    own_dx.wait()
    for way in ways:
        way.out.wait()
    links.finish()


def layer_call(planes, heads, x_in, c_in, a_in, u_in, d_in, bias_in, init, starts, reset):
    real, width = x_in.shape[1:]
    block = -(-real // 16) * 16
    rows = planes * block
    hp = heads // planes
    hw = hp * DH
    shard = a_in.shape
    hidden = shard[1]
    piece, half = shard[0] // (2 * INNER), shard[0] // 2
    S = jax.ShapeDtypeStruct
    V = pltpu.VMEM
    outs = (
        S(shard, bf16),
        S(shard, bf16),
        S(shard, bf16),
        S((planes, real, width), bf16),
        S((planes, real, width), bf16),
        S((heads, rows, rows), bf16),
        S((2 * SMALL, width), f32),
    )
    any_spec = pl.BlockSpec(memory_space=pl.ANY)
    vmem_spec = pl.BlockSpec(memory_space=pltpu.VMEM)
    return pl.pallas_call(
        functools.partial(layer_kernel, planes, heads, block),
        out_shape=outs,
        in_specs=[any_spec] * 5 + [vmem_spec] * 3 + [pl.BlockSpec(memory_space=pltpu.SMEM)],
        out_specs=[any_spec] * 6 + [vmem_spec],
        scratch_shapes=[
            V((planes, *shard), bf16),
            V((planes, *shard), bf16),
            V((planes, *shard), bf16),
            V((planes, real, width), bf16),
            V((planes, real, width), bf16),
            V((planes, block, width), bf16),
            V((planes, *bias_in.shape), bf16),
            V((heads, rows, DH), bf16),
            V((heads, rows, DH), bf16),
            V((heads, rows, DH), bf16),
            V((2, rows, rows), bf16),
            V((planes, rows, hw), bf16),
            V((hp, rows, DH), bf16),
            V((hp, rows, 1), f32),
            V((3 * hp, rows, DH), bf16),
            V((rows, rows), bf16),
            V((rows, rows), f32),
            V((rows, width), f32),
            V((rows, width), f32),
            V((rows, 1), f32),
            V((rows, width), bf16),
            V((planes, rows, hidden), bf16),
            V((planes, rows, hidden), bf16),
            V((rows, width), bf16),
            V((3, planes, half, hidden), bf16),
            V((3, 2, planes, 2 * piece, hidden), bf16),
            V((3, 2, planes, piece, hidden), bf16),
            V((3, planes - 1, 2, piece, hidden), bf16),
            V((2, 4, SMALL, width), f32),
            V((2, 2 + planes, SMALL, width), f32),
            pltpu.SemaphoreType.DMA((LINKS,)),
            pltpu.SemaphoreType.DMA((LINKS,)),
            pltpu.SemaphoreType.DMA((3, planes, 2)),
            pltpu.SemaphoreType.DMA((LOCALS,)),
        ],
        compiler_params=pltpu.CompilerParams(
            collective_id=0, has_side_effects=True, vmem_limit_bytes=63 * MIB
        ),
    )(x_in, c_in, a_in, u_in, d_in, bias_in, init, starts, reset)


def shards(
    dp_size,
    planes,
    sequence,
    query_key_value_weight,
    qv_bias,
    output_weight,
    out_bias,
    up_weight,
    up_bias,
    down_weight,
    back_bias,
    gain_one,
    shift_one,
    gain_two,
    shift_two,
    init_memory,
    reset,
    starts,
    cotangent,
):
    segs, local_rows, width = sequence.shape
    mem = init_memory.shape[0]
    tokens = starts.shape[1]
    hw = query_key_value_weight.shape[2]
    heads = hw * planes // DH
    assert segs == planes == 4 and mem <= local_rows and dp_size % INNER == 0
    t = lax.axis_index("tensor")
    position = t * local_rows + jnp.arange(local_rows, dtype=jnp.int32)
    is_memory = (position < mem) | (position >= mem + tokens)
    use_init = ((reset[:, None] > 0) & is_memory[None, :])[:, :, None]

    a_in = jnp.concatenate(
        [query_key_value_weight.transpose(1, 2, 0).reshape(3 * hw, width), output_weight], 0
    )
    qv_row = jnp.pad(qv_bias.reshape(2 * hw), (0, width - 2 * hw))
    bias_in = jnp.stack(
        [up_bias, qv_row, out_bias, back_bias, gain_one, shift_one, gain_two, shift_two]
        + [jnp.zeros((width,), bf16)] * 8
    )
    ga, gu, gd, dx, y, _, small = layer_call(
        planes,
        heads,
        sequence,
        cotangent,
        a_in,
        up_weight,
        down_weight,
        bias_in,
        init_memory,
        starts,
        reset,
    )

    input_grad = jnp.where(use_init, 0.0, dx.astype(f32))
    ga, gu, gd = ga.astype(f32), gu.astype(f32), gd.astype(f32)
    if dp_size > INNER:
        groups = [[o * INNER + i for o in range(dp_size // INNER)] for i in range(INNER)]
        ga, gu, gd, small = lax.psum((ga, gu, gd, small), "dp", axis_index_groups=groups)
    own = lambda first: lax.dynamic_slice_in_dim(small, first + t, 1, 0)[0]
    return (
        y,
        input_grad,
        ga[: 3 * hw].reshape(3, hw, width).transpose(2, 0, 1),
        own(SMALL + 10)[: 2 * hw].reshape(2, hw),
        ga[3 * hw :],
        small[5],
        gu,
        own(6),
        gd,
        small[2],
        small[3],
        small[4],
        small[0],
        small[1],
        small[SMALL : SMALL + mem],
    )


def solution(mesh):
    in_specs = (
        P("dp", "tensor", None),
        P(None, None, "tensor"),
        P(None, "tensor"),
        P("tensor", None),
        P(),
        P(None, "tensor"),
        P("tensor"),
        P("tensor", None),
        P(),
        P(),
        P(),
        P(),
        P(),
        P(),
        P("dp"),
        P("dp", None),
        P("dp", "tensor", None),
    )
    out_specs = (
        P("dp", "tensor", None),
        P("dp", "tensor", None),
        P(None, None, "tensor"),
        P(None, "tensor"),
        P("tensor", None),
        P(),
        P(None, "tensor"),
        P("tensor"),
        P("tensor", None),
        P(),
        P(),
        P(),
        P(),
        P(),
        P(),
    )
    return jax.shard_map(
        functools.partial(shards, mesh.shape["dp"], mesh.shape["tensor"]),
        mesh=mesh,
        in_specs=in_specs,
        out_specs=out_specs,
        check_vma=False,
    )
```

```python
import functools

import jax
import jax.numpy as jnp
from jax import lax
from jax.experimental import pallas as pl
from jax.experimental.pallas import tpu as pltpu
from jax.sharding import PartitionSpec as P

DH = 64
NEGATIVE = -1e30
EPSILON = 1e-05
INNER = 8
MIB = 1 << 20

f32 = jnp.float32
bf16 = jnp.bfloat16
NN = (((1,), (0,)), ((), ()))
NT = (((1,), (1,)), ((), ()))
TN = (((0,), (0,)), ((), ()))
MESH = pl.DeviceIdType.MESH


def dot(a, b, dims=NN):
    return lax.dot_general(a, b, dims, preferred_element_type=f32)


def each(count, body):
    def step(i, carry):
        body(i)
        return carry

    lax.fori_loop(0, count, step, 0)


class Place:
    def __init__(self, planes):
        self.planes = planes
        self.dp = lax.axis_index("dp")
        self.t = lax.axis_index("tensor")
        self.core = self.dp % 2
        self.x = (self.dp // 2) % 2
        self.y = (self.dp // 4) % 2
        self.to_core = (self.dp + 1 - 2 * self.core, self.t)
        self.to_x = (self.dp + 2 - 4 * self.x, self.t)
        self.to_y = (self.dp + 4 - 8 * self.y, self.t)

    def plane(self, j):
        return lax.rem(self.t + j, self.planes)

    def to_plane(self, j):
        return (self.dp, self.plane(j))

    def partners(self):
        both = (self.to_x[0] + self.to_y[0] - self.dp, self.t)
        return [self.to_core, self.to_x, self.to_y, both] + [
            self.to_plane(j) for j in range(1, self.planes)
        ]

    def greet(self):
        barrier = pltpu.get_barrier_semaphore()
        partners = self.partners()
        for device in partners:
            pl.semaphore_signal(barrier, inc=1, device_id=device, device_id_type=MESH)
        pl.semaphore_wait(barrier, len(partners))


class Rows:
    def __init__(self, place, rows):
        self.piece = rows // (2 * INNER)
        self.half = rows // 2
        quarter = rows // 4
        core, x, y = place.core, place.x, place.y
        at = lambda n: pl.multiple_of(n, 16)
        base = core * self.half
        self.mine = at(base)
        self.others = at((1 - core) * self.half)
        self.a = at(base + (2 * y + x) * self.piece)
        self.b = at(base + quarter + (2 * x + y) * self.piece)
        self.a_pair = at(base + 2 * y * self.piece)
        self.b_pair = at(base + quarter + 2 * x * self.piece)
        self.a_far_pair = at(base + 2 * (1 - y) * self.piece)
        self.b_far_pair = at(base + quarter + 2 * (1 - x) * self.piece)
        self.a_far = at(base + (2 * y + 1 - x) * self.piece)
        self.b_far = at(base + quarter + (2 * x + 1 - y) * self.piece)


class Links:
    def __init__(self, send, recv):
        self.send, self.recv, self.count, self.all = send, recv, 0, []

    def copy(self, src, dst, device, recv=None, only=None):
        k = self.count
        self.count += 1
        made = pltpu.make_async_remote_copy(
            src_ref=src,
            dst_ref=dst,
            send_sem=self.send.at[k],
            recv_sem=self.recv.at[k] if recv is None else recv,
            device_id=device,
            device_id_type=MESH,
        )
        self.all.append((made, only))
        return made

    def finish(self, copies=None):
        for made, only in list(self.all):
            if copies is None or any(made is c for c in copies):
                self.all = [entry for entry in self.all if entry[0] is not made]
                if only is None:
                    made.wait_send()
                else:
                    pl.when(only)(made.wait_send)


def start(copies):
    for c in copies:
        c.start()


def arrive(copies):
    for c in copies:
        c.wait_recv()


def mirror_end(t, low, planes):
    return t + low * (planes - 1 - 2 * t)


class Way:
    pass


LINKS = 200
LOCALS = 24
SMALL = 16


def layer_kernel(
    planes,
    heads,
    block,
    x_in,
    c_in,
    qkv_in,
    o_in,
    u_in,
    d_in,
    bias_in,
    init_ref,
    starts_ref,
    reset_ref,
    ga_out,
    gu_out,
    gd_out,
    dx_out,
    y_out,
    p_hbm,
    small_ref,
    a_w,
    u_w,
    d_w,
    xs,
    cs,
    x_s,
    bias,
    q_s,
    k_s,
    v_s,
    p2,
    o_s,
    do_s,
    delta_s,
    d_s,
    mask,
    acc,
    xhat_s,
    rstd_s,
    hb_s,
    act_s,
    dz_s,
    gb_s,
    half_in,
    pair_in,
    one_in,
    z_in,
    sm,
    sm_core,
    sm_low,
    sm_in,
    send,
    recv,
    recv_z,
    local,
):
    place = Place(planes)
    t = place.t
    others = range(1, planes)
    real, width = xs.shape[1:]
    rows = planes * block
    mem = init_ref.shape[0]
    hp = heads // planes
    hw = hp * DH
    links = Links(send, recv)
    r = Rows(place, a_w.shape[1])
    piece, half = r.piece, r.half
    vec = lambda i: bias_in[2 + i : 3 + i, :].astype(f32)
    add_up = lambda v: jnp.sum(v, axis=0, keepdims=True)

    def keep(k, src, dst):
        return pltpu.make_async_copy(src, dst, local.at[k])

    weights, g_outs = (a_w, u_w, d_w), (ga_out, gu_out, gd_out)

    low = t // 2
    middle = mirror_end(t, low, planes) == 1
    mirror = lambda n: n + low * (planes - 1 - 2 * n)

    def slot_shard(i):
        return mirror(i - mirror(t) if i == 1 else i)

    def neighbour(to):
        inside = (to >= 0) & (to < planes)
        return (place.dp, lax.rem(to + planes, planes)), inside

    gather = []
    for w in range(3):
        way = Way()
        way.own, way.z, way.one, way.two, way.core = [], [], [], [], []
        for step in (1, -1):
            device, inside = neighbour(t + step)
            way.own.append(
                (
                    inside,
                    [
                        links.copy(
                            weights[w].at[t, pl.ds(at, piece)],
                            weights[w].at[t, pl.ds(at, piece)],
                            device,
                            recv_z.at[w, t, n],
                            inside,
                        )
                        for n, at in enumerate((r.a, r.b))
                    ],
                )
            )
        for i in others:
            s = slot_shard(i)
            below = (t - s + planes - 1) // planes
            device, inside = neighbour(t + 2 * below - 1)
            here = lambda at, size: weights[w].at[s, pl.ds(at, size)]
            same = lambda at, size, to: links.copy(here(at, size), here(at, size), to)
            way.z.append(
                (
                    inside,
                    [
                        links.copy(
                            here(at, piece), here(at, piece), device, recv_z.at[w, s, n], inside
                        )
                        for n, at in enumerate((r.a, r.b))
                    ],
                )
            )
            way.one.append([same(r.a, piece, place.to_x), same(r.b, piece, place.to_y)])
            way.two.append(
                [same(r.a_pair, 2 * piece, place.to_y), same(r.b_pair, 2 * piece, place.to_x)]
            )
            way.core.append([same(r.mine, half, place.to_core)])
        gather.append(way)

    def when_start(inside, copies):
        pl.when(inside)(lambda: start(copies))

    def get_own(w):
        for inside, copies in gather[w].own:
            when_start(inside, copies)

    def get_z(w, i):
        inside, copies = gather[w].z[i - 1]
        arrive(copies)
        when_start(inside, copies)
        start(gather[w].one[i - 1])

    def get_stage(w, d):
        if d == 1:
            get_z(w, 1)
            pl.when(middle)(lambda: get_z(w, 2))
        elif d == 2:
            pl.when(middle)(lambda: get_z(w, 3))
            pl.when(~middle)(lambda: get_z(w, 2))
        else:
            pl.when(~middle)(lambda: get_z(w, 3))

    def get_one(w, i):
        arrive(gather[w].one[i - 1])
        start(gather[w].two[i - 1])

    def get_two(w, i):
        arrive(gather[w].two[i - 1])
        start(gather[w].core[i - 1])

    def get_core(w, i):
        arrive(gather[w].core[i - 1])

    def release(w):
        way = gather[w]
        links.finish([c for _, z in way.own + way.z for c in z])
        links.finish([c for part in way.one + way.two + way.core for c in part])

    def spread(sends, d):
        def go(plane, *picks):
            pl.when(t == plane)(lambda: start([sends[j - 1] for j in picks]))

        if d == 0:
            go(0, 1, 2, 3)
            go(3, 3, 2, 1)
        elif d == 1:
            go(1, 1, 2)
            go(2, 3, 2)
        else:
            go(1, 3)
            go(2, 1)

    def to_next(sends):
        pl.when((t == 0) | (t == 2))(lambda: start(sends[0:1]))
        pl.when((t == 1) | (t == 3))(lambda: start(sends[2:3]))

    def to_middle(sends):
        pl.when((t == 0) | (t == 2))(lambda: start(sends[2:3]))
        pl.when((t == 1) | (t == 3))(lambda: start(sends[0:1]))

    back_order = (2, 1, 3, 0)
    ways = []
    for w in range(3):
        g = weights[w]
        way = Way()
        way.core, way.pair, way.one, way.z = [], [], [], []
        for i in range(planes):
            j = back_order[i]
            s = place.plane(j)
            cut = lambda at, size: g.at[s, pl.ds(at, size)]
            way.core.append([links.copy(cut(r.others, half), half_in.at[w, i], place.to_core)])
            way.pair.append(
                [
                    links.copy(cut(r.a_far_pair, 2 * piece), pair_in.at[w, 0, i], place.to_y),
                    links.copy(cut(r.b_far_pair, 2 * piece), pair_in.at[w, 1, i], place.to_x),
                ]
            )
            way.one.append(
                [
                    links.copy(cut(r.a_far, piece), one_in.at[w, 0, i], place.to_x),
                    links.copy(cut(r.b_far, piece), one_in.at[w, 1, i], place.to_y),
                ]
            )
            if i + 1 < planes:
                way.z.append(
                    [
                        links.copy(cut(r.a, piece), z_in.at[w, i, 0], place.to_plane(j)),
                        links.copy(cut(r.b, piece), z_in.at[w, i, 1], place.to_plane(j)),
                    ]
                )
        at_home = lambda at: pl.multiple_of(at - r.mine, 16)
        f = half_in.at[w, 0]
        same = lambda at, size, to: links.copy(
            f.at[pl.ds(at_home(at), size)], f.at[pl.ds(at_home(at), size)], to
        )
        way.back1 = [same(r.a, piece, place.to_x), same(r.b, piece, place.to_y)]
        way.back2 = [
            same(r.a_pair, 2 * piece, place.to_y),
            same(r.b_pair, 2 * piece, place.to_x),
        ]
        mine = g_outs[w].at[pl.ds(r.mine, half)]
        way.back3 = [links.copy(f, mine, place.to_core)]
        way.out = keep(8 + w, f, mine)
        ways.append(way)

    def add_rows(g, s, at, size, got):
        span = pl.ds(at, size)
        g[s, span, :] = (g[s, span, :].astype(f32) + got.astype(f32)).astype(bf16)

    def back_shard(n):
        j = 0
        for i in range(planes - 1):
            j = jnp.where(n == i, back_order[i], j)
        return place.plane(j)

    def part_core(w, i):
        arrive(ways[w].core[i])
        add_rows(weights[w], back_shard(i), r.mine, half, half_in[w, i])
        start(ways[w].pair[i])

    def part_pair(w, i):
        arrive(ways[w].pair[i])
        s = back_shard(i)
        add_rows(weights[w], s, r.a_pair, 2 * piece, pair_in[w, 0, i])
        add_rows(weights[w], s, r.b_pair, 2 * piece, pair_in[w, 1, i])
        start(ways[w].one[i])

    def part_one(w, i):
        arrive(ways[w].one[i])
        s = back_shard(i)
        add_rows(weights[w], s, r.a, piece, one_in[w, 0, i])
        add_rows(weights[w], s, r.b, piece, one_in[w, 1, i])
        if i + 1 < planes:
            start(ways[w].z[i])

    def after_z(w):
        for z in ways[w].z:
            arrive(z)
        for i, at in enumerate((r.a, r.b)):
            v = weights[w][t, pl.ds(at, piece), :].astype(f32)
            for j in others:
                v = v + z_in[w, j - 1, i].astype(f32)
            half_in[w, 0, pl.ds(pl.multiple_of(at - r.mine, 16), piece), :] = v.astype(bf16)
        start(ways[w].back1)

    def after_back1(w):
        arrive(ways[w].back1)
        start(ways[w].back2)

    def after_back2(w):
        arrive(ways[w].back2)
        start(ways[w].back3)
        ways[w].out.start()

    def after_back3(w):
        arrive(ways[w].back3)

    x_send = [links.copy(x_in.at[place.plane(j)], xs.at[t], place.to_plane(j)) for j in others]
    c_send = [links.copy(c_in.at[place.plane(j)], cs.at[t], place.to_plane(j)) for j in others]
    b_send = [links.copy(bias_in, bias.at[t], place.to_plane(j)) for j in others]
    y_send = [links.copy(cs.at[place.plane(j)], y_out.at[t], place.to_plane(j)) for j in others]
    dx_send = [links.copy(xs.at[place.plane(j)], dx_out.at[t], place.to_plane(j)) for j in others]
    hops = []
    to_both = (place.to_x[0] + place.to_y[0] - place.dp, t)
    for e in range(2):
        mine, got = sm_low.at[e], sm_in.at[e]
        hops.append(
            [
                [links.copy(sm.at[e], sm_core.at[e], place.to_core)],
                [
                    links.copy(mine.at[0], got.at[n], to)
                    for n, to in enumerate((place.to_x, place.to_y, to_both))
                ],
                [links.copy(mine.at[1], got.at[2 + j], place.to_plane(j)) for j in others],
            ]
        )

    def in_order(parts, device):
        total = jnp.zeros_like(parts[0])
        for n in range(len(parts)):
            for part, who in zip(parts, device):
                total = total + jnp.where(who == n, part, 0.0)
        return total

    def hop(e, n):
        arrive(hops[e][n])
        low = lambda k: sm_in[e, k].astype(f32)
        if n == 0:
            sm_low[e, 0] = (sm[e] + sm_core[e]).astype(bf16)
        elif n == 1:
            x, y = place.x, place.y
            near = [2 * y + x, 2 * y + 1 - x, 2 * (1 - y) + x, 2 * (1 - y) + 1 - x]
            parts = [sm_low[e, 0].astype(f32)] + [low(k) for k in range(3)]
            sm_low[e, 1] = in_order(parts, near).astype(bf16)
        else:
            planes_of = [lax.rem(t + planes - j, planes) for j in range(planes)]
            total = in_order([sm_low[e, 1].astype(f32)] + [low(2 + j) for j in others], planes_of)
            small_ref[e * SMALL : (e + 1) * SMALL, :] = total
            return
        start(hops[e][n + 1])

    own_a = [
        keep(0, qkv_in, a_w.at[t, pl.ds(0, 3 * hw)]),
        keep(5, o_in, a_w.at[t, pl.ds(3 * hw, hw)]),
    ]
    own_u, own_d = keep(1, u_in, u_w.at[t]), keep(2, d_in, d_w.at[t])
    own_x = keep(3, x_in.at[t], xs.at[t])
    own_c = keep(4, c_in.at[t], cs.at[t])
    own_y = keep(6, cs.at[t], y_out.at[t])
    own_dx = keep(7, xs.at[t], dx_out.at[t])

    def p_at(m):
        return p_hbm.at[m]

    p_save = lambda m: keep(12 + m % 2, p2.at[m % 2], p_at(m))

    start([*own_a, own_u, own_d, own_x, own_c])
    place.greet()
    for c in own_a:
        c.wait()
    get_own(0)
    start(b_send)
    own_u.wait()
    get_own(1)
    spread(x_send, 0)

    bias[t] = bias_in[...]
    tokens = starts_ref.shape[1]

    def token_of(shape, axis):
        n = lax.broadcasted_iota(jnp.int32, shape, axis)
        inside = n % block
        return (n // block) * real + inside - mem, inside

    upto, _ = token_of((tokens, rows), 1)
    begun = lax.broadcasted_iota(jnp.int32, (tokens, rows), 0) <= upto
    begun = jnp.where(begun, 1.0, 0.0).astype(bf16)
    own_starts = starts_ref[pl.ds(t, 1), :].astype(f32).astype(bf16)
    docs = dot(jnp.broadcast_to(own_starts, (8, tokens)), begun)

    def codes(docs, axis):
        token, inside = token_of(docs.shape, axis)
        docs = jnp.where((token < 0) | (token >= tokens), -1.0, docs)
        return jnp.where(inside >= real, -2.0, docs)

    qc = codes(docs, 1)[0:1, :]
    kcodes = codes(docs.T, 0)[:, 0:1]
    for c in range(planes):
        span = slice(c * block, (c + 1) * block)
        kc = kcodes[span, :]
        allowed = ((qc == kc) | (qc < 0) | (kc < 0)) & (kc != -2.0)
        mask[span, :] = jnp.where(allowed, 0.0, NEGATIVE)
    for e in range(2):
        sm[e] = jnp.zeros((SMALL, width), f32)

    get_stage(0, 1)
    get_stage(1, 1)
    spread(x_send, 1)
    get_one(0, 1)
    pl.when(middle)(lambda: get_one(0, 2))
    get_stage(0, 2)
    get_one(1, 1)
    get_stage(1, 2)
    spread(x_send, 2)
    own_d.wait()
    get_own(2)
    get_two(0, 1)
    pl.when(~middle)(lambda: get_one(0, 2))
    get_stage(0, 3)
    get_two(1, 1)
    get_one(1, 2)
    get_stage(1, 3)
    get_two(0, 2)
    get_one(0, 3)
    get_two(1, 2)
    get_one(1, 3)
    get_two(0, 3)
    get_two(1, 3)
    for c in (own_x, own_c):
        c.wait()
    arrive(x_send)
    arrive(b_send)
    afresh = reset_ref[t] > 0
    for c in range(planes):
        x_s[c, 0:real, :] = xs[c]
        x_s[c, real:block, :] = jnp.zeros((block - real, width), bf16)
    last = real - mem
    x_s[0, 0:mem, :] = jnp.where(afresh, init_ref[...], xs[0, 0:mem, :])
    x_s[planes - 1, last:real, :] = jnp.where(afresh, init_ref[...], xs[planes - 1, last:real, :])
    acc[...] = x_s[...].reshape(rows, width).astype(f32) + vec(0)

    forward_pokes = [
        (0, 3, lambda: get_stage(2, 1)),
        (0, 3, lambda: spread(c_send, 0)),
        (0, 3, lambda: spread(c_send, 1)),
        (1, 3, lambda: get_one(2, 1)),
        (2, 0, lambda: get_stage(2, 2)),
        (2, 0, lambda: spread(c_send, 2)),
        (3, 0, lambda: get_two(2, 1)),
        (3, 0, lambda: get_one(2, 2)),
        (3, 1, lambda: get_stage(2, 3)),
    ]

    def poke_at(pokes, *now):
        for *when, poke in pokes:
            hit = now[0] == when[0]
            for a, b in zip(now[1:], when[1:]):
                hit = hit & (a == b)
            pl.when(hit)(poke)

    def forward_order(j):
        picked = t
        for i in others:
            picked = jnp.where(j == i, slot_shard(i), picked)
        return picked

    head_feats = lambda i: pl.ds(pl.multiple_of(i * DH, DH), DH)

    def attention(j):
        s = forward_order(j)
        for i in others:
            pl.when(j == i)(lambda: get_core(0, i))

        poke_at([p for p in forward_pokes if p[1] == 0], j, 0)
        x = x_s[...].reshape(rows, width)
        qkv = dot(a_w[s, 0 : 3 * hw, :], x, NT)
        b = bias[s].astype(f32).T[:, 1:2]
        q = ((qkv[0:hw] + b[0:hw]).astype(bf16).astype(f32) * (DH**-0.5)).astype(bf16)
        k = qkv[hw : 2 * hw].astype(bf16)
        v = (qkv[2 * hw :] + b[hw : 2 * hw]).astype(bf16)
        for i in range(hp):
            feats = slice(i * DH, (i + 1) * DH)
            q_s[s * hp + i], k_s[s * hp + i], v_s[s * hp + i] = q[feats], k[feats], v[feats]

        def head(i):
            h = s * hp + i
            m = j * hp + i
            poke_at([p for p in forward_pokes if p[1] > 0], j, i + 1)
            pl.when(m >= 2)(lambda: p_save(m).wait())
            scores = dot(k_s[h], q_s[h], TN) + mask[...]
            e = jnp.exp(scores - jnp.max(scores, axis=0, keepdims=True))
            p = (e * (1.0 / jnp.sum(e, axis=0, keepdims=True))).astype(bf16)
            p2[m % 2] = p
            o_s[s, head_feats(i), :] = dot(v_s[h], p).astype(bf16)
            keep(12 + m % 2, p2.at[m % 2], p_at(h)).start()

        each(hp, head)
        acc[...] += dot(o_s[s], a_w[s, 3 * hw :, :], TN)

    each(planes, attention)

    def first_norm(c):
        span = pl.ds(pl.multiple_of(c * block, block), block)
        v = acc[span, :]
        v = v - jnp.mean(v, axis=1, keepdims=True)
        rstd = lax.rsqrt(jnp.mean(v * v, axis=1, keepdims=True) + EPSILON)
        xhat = v * rstd
        rstd_s[span, :] = rstd
        xhat_s[span, :] = xhat
        h = xhat * vec(2) + vec(3)
        hb_s[span, :] = h.astype(bf16)
        acc[span, :] = h + vec(1)

    each(planes, first_norm)
    get_one(2, 3)

    def up(j):
        s = forward_order(j)
        for i in others:
            pl.when(j == i)(lambda: get_core(1, i))
        pl.when(j == 0)(lambda: get_two(2, 2))
        for c in range(planes):
            span = pl.ds(c * block, block)
            z = dot(hb_s[span, :], u_w[s]) + bias[s, 0:1, :].astype(f32)
            phi = 0.5 + 0.5 * lax.erf(z * (0.5**0.5))
            act_s[s, span, :] = (z * phi).astype(bf16)
            dz_s[s, span, :] = (phi + z * jnp.exp(-0.5 * z * z) * 0.3989422804014327).astype(bf16)

    each(planes, up)
    get_two(2, 3)

    def down(j):
        s = forward_order(j)
        for i in others:
            pl.when(j == i)(lambda: get_core(2, i))
        acc[...] += dot(act_s[s], d_w[s])

    each(planes, down)
    arrive(c_send)

    zero = jnp.zeros((1, width), f32)

    def second_norm(c, sums):
        span = pl.ds(pl.multiple_of(c * block, block), block)
        v = acc[span, :]
        v = v - jnp.mean(v, axis=1, keepdims=True)
        rstd = lax.rsqrt(jnp.mean(v * v, axis=1, keepdims=True) + EPSILON)
        xhat = v * rstd
        gb_s[span, :] = jnp.zeros((block, width), bf16)
        gb_s[pl.ds(pl.multiple_of(c * block, block), real), :] = cs[c]
        g = gb_s[span, :].astype(f32)
        cs[c] = (xhat * vec(4) + vec(5)).astype(bf16)[0:real]
        d = g * vec(4)
        g2 = rstd * (
            d
            - jnp.mean(d, axis=1, keepdims=True)
            - xhat * jnp.mean(d * xhat, axis=1, keepdims=True)
        )
        acc[span, :] = g2
        gb_s[span, :] = g2.astype(bf16)
        return sums[0] + add_up(g * xhat), sums[1] + add_up(g), sums[2] + add_up(g2)

    sums = lax.fori_loop(0, planes, second_norm, (zero, zero, zero))
    sm[0, 0:3, :] = jnp.concatenate(list(sums), axis=0)
    start(y_send)
    own_y.start()

    down_pokes = [
        (3, lambda: part_core(2, 0)),
    ]
    up_pokes = [
        (0, lambda: part_core(2, 1)),
        (1, lambda: part_core(2, 2)),
        (2, lambda: part_pair(2, 0)),
        (2, lambda: part_core(2, 3)),
        (3, lambda: part_core(1, 0)),
        (3, lambda: part_pair(2, 1)),
        (3, lambda: part_core(1, 1)),
    ]

    def back_down(n):
        s = back_shard(n)
        poke_at(down_pokes, n)
        du = dot(gb_s[...], d_w[s], NT)
        dz_s[s] = (du * dz_s[s].astype(f32)).astype(bf16)
        d_w[s] = dot(act_s[s], gb_s[...], TN).astype(bf16)
        for k in range(planes):
            pl.when(n == k)(ways[2].core[k][0].start)

    release(2)
    each(planes, back_down)

    def back_up(n):
        s = back_shard(n)
        poke_at(up_pokes, n)
        dz = dz_s[s]
        sm[0, pl.ds(6 + s, 1), :] = add_up(dz.astype(f32))
        acc[...] += dot(dz, u_w[s], NT)
        u_w[s] = dot(hb_s[...], dz, TN).astype(bf16)
        for k in range(planes):
            pl.when(n == k)(ways[1].core[k][0].start)

    release(1)
    each(planes, back_up)
    for m in (heads - 2, heads - 1):
        p_save(m).wait()

    p_load = lambda m: keep(
        12 + m % 2, p_at(back_shard(m // hp) * hp + m % hp), p2.at[m % 2]
    )
    p_load(0).start()

    part_pair(2, 2)
    part_core(1, 2)

    def back_first_norm(c, sums):
        span = pl.ds(pl.multiple_of(c * block, block), block)
        xhat = xhat_s[span, :]
        g = acc[span, :]
        d = g * vec(2)
        g1 = rstd_s[span, :] * (
            d
            - jnp.mean(d, axis=1, keepdims=True)
            - xhat * jnp.mean(d * xhat, axis=1, keepdims=True)
        )
        acc[span, :] = g1
        gb_s[span, :] = g1.astype(bf16)
        return sums[0] + add_up(g * xhat), sums[1] + add_up(g), sums[2] + add_up(g1)

    sums = lax.fori_loop(0, planes, back_first_norm, (zero, zero, zero))
    sm[0, 3:6, :] = jnp.concatenate(list(sums), axis=0)
    start(hops[0][0])
    back_pokes = [
        (0, 0, lambda: part_one(2, 0)),
        (0, 1, lambda: part_core(1, 3)),
        (0, 2, lambda: hop(0, 0)),
        (0, 2, lambda: part_pair(2, 3)),
        (0, 4, lambda: part_pair(1, 0)),
        (1, 0, lambda: part_one(2, 1)),
        (1, 3, lambda: part_pair(1, 1)),
        (1, 3, lambda: part_core(0, 0)),
        (1, 3, lambda: part_one(2, 2)),
        (2, 0, lambda: part_pair(1, 2)),
        (2, 3, lambda: part_pair(1, 3)),
        (2, 3, lambda: hop(0, 1)),
        (2, 3, lambda: part_core(0, 1)),
        (2, 4, lambda: part_one(2, 3)),
        (2, 4, lambda: after_z(2)),
        (3, 0, lambda: part_one(1, 0)),
        (3, 0, lambda: hop(0, 2)),
        (3, 1, lambda: part_one(1, 1)),
        (3, 3, lambda: part_core(0, 2)),
        (3, 3, lambda: part_pair(0, 0)),
        (3, 4, lambda: part_one(1, 2)),
    ]

    def back_attention(n):
        s = back_shard(n)
        poke_at([p for p in back_pokes if p[1] == 0], n, 0)
        do = dot(a_w[s, 3 * hw :, :], gb_s[...], NT).astype(bf16)
        do_s[...] = do
        prod = do.astype(f32) * o_s[s].astype(f32)
        for i in range(hp):
            delta_s[i] = add_up(prod[i * DH : (i + 1) * DH])

        def head(i):
            h = s * hp + i
            m = n * hp + i
            p_load(m).wait()
            pl.when(m + 1 < heads)(lambda: p_load(m + 1).start())
            poke_at([p for p in back_pokes if 0 < p[1] < 4], n, i + 1)
            slot = m % 2
            p, do = p2[slot], do_s[head_feats(i), :]
            dp = dot(v_s[h], do, TN)
            ds = (p.astype(f32) * (dp - delta_s[i])).astype(bf16)
            d_s[head_feats(i), :] = (dot(k_s[h], ds) * (DH**-0.5)).astype(bf16)
            d_s[head_feats(hp + i), :] = dot(q_s[h], ds, NT).astype(bf16)
            d_s[head_feats(2 * hp + i), :] = dot(do, p, NT).astype(bf16)

        each(hp, head)
        poke_at([p for p in back_pokes if p[1] == 4], n, 4)
        dqkv = d_s[...]
        sums = dot(jnp.ones((8, rows), bf16), dqkv, NT)[0:1, :]
        sm[1, pl.ds(10 + s, 1), 0:hw] = sums[:, 0:hw]
        sm[1, pl.ds(10 + s, 1), hw : 2 * hw] = sums[:, 2 * hw :]
        acc[...] += dot(dqkv, a_w[s, 0 : 3 * hw, :], TN)
        a_w[s, 0 : 3 * hw, :] = dot(dqkv, x_s[...].reshape(rows, width)).astype(bf16)
        a_w[s, 3 * hw :, :] = dot(o_s[s], gb_s[...]).astype(bf16)
        for k in range(planes):
            pl.when(n == k)(ways[0].core[k][0].start)

    release(0)
    each(planes, back_attention)

    for c in range(planes):
        xs[c] = acc[c * block : c * block + real, :].astype(bf16)
    part_one(1, 3)
    to_next(dx_send)
    own_dx.start()
    dx_last = (planes - 1) * block + last
    both = acc[0:mem, :] + acc[dx_last : dx_last + mem, :]
    sm[1, 0:mem, :] = jnp.where(afresh, both, 0.0)
    start(hops[1][0])
    part_pair(0, 1)
    part_core(0, 3)
    hop(1, 0)
    after_back1(2)
    part_pair(0, 2)
    after_z(1)
    part_one(0, 0)
    part_one(0, 1)
    part_pair(0, 3)
    hop(1, 1)
    after_back2(2)
    part_one(0, 2)
    start(dx_send[1:2])
    after_back1(1)
    after_back3(2)
    part_one(0, 3)
    to_middle(dx_send)
    after_z(0)
    after_back2(1)
    after_back3(1)
    after_back1(0)
    after_back2(0)
    hop(1, 2)
    after_back3(0)

    arrive(y_send)
    arrive(dx_send)
    own_y.wait()
    own_dx.wait()
    for way in ways:
        way.out.wait()
    links.finish()


def layer_call(planes, heads, x_in, c_in, qkv_in, o_in, u_in, d_in, bias_in, init, starts, reset):
    real, width = x_in.shape[1:]
    block = -(-real // 16) * 16
    rows = planes * block
    hp = heads // planes
    hw = hp * DH
    shard = u_in.shape
    hidden = shard[1]
    piece, half = shard[0] // (2 * INNER), shard[0] // 2
    S = jax.ShapeDtypeStruct
    V = pltpu.VMEM
    outs = (
        S(shard, bf16),
        S(shard, bf16),
        S(shard, bf16),
        S((planes, real, width), bf16),
        S((planes, real, width), bf16),
        S((heads, rows, rows), bf16),
        S((2 * SMALL, width), f32),
    )
    any_spec = pl.BlockSpec(memory_space=pl.ANY)
    vmem_spec = pl.BlockSpec(memory_space=pltpu.VMEM)
    return pl.pallas_call(
        functools.partial(layer_kernel, planes, heads, block),
        out_shape=outs,
        in_specs=[any_spec] * 6 + [vmem_spec] * 3 + [pl.BlockSpec(memory_space=pltpu.SMEM)],
        out_specs=[any_spec] * 6 + [vmem_spec],
        scratch_shapes=[
            V((planes, *shard), bf16),
            V((planes, *shard), bf16),
            V((planes, *shard), bf16),
            V((planes, real, width), bf16),
            V((planes, real, width), bf16),
            V((planes, block, width), bf16),
            V((planes, *bias_in.shape), bf16),
            V((heads, DH, rows), bf16),
            V((heads, DH, rows), bf16),
            V((heads, DH, rows), bf16),
            V((2, rows, rows), bf16),
            V((planes, hw, rows), bf16),
            V((hw, rows), bf16),
            V((hp, 1, rows), f32),
            V((3 * hw, rows), bf16),
            V((rows, rows), f32),
            V((rows, width), f32),
            V((rows, width), f32),
            V((rows, 1), f32),
            V((rows, width), bf16),
            V((planes, rows, hidden), bf16),
            V((planes, rows, hidden), bf16),
            V((rows, width), bf16),
            V((3, planes, half, hidden), bf16),
            V((3, 2, planes, 2 * piece, hidden), bf16),
            V((3, 2, planes, piece, hidden), bf16),
            V((3, planes - 1, 2, piece, hidden), bf16),
            V((2, SMALL, width), f32),
            V((2, SMALL, width), f32),
            V((2, 2, SMALL, width), bf16),
            V((2, 2 + planes, SMALL, width), bf16),
            pltpu.SemaphoreType.DMA((LINKS,)),
            pltpu.SemaphoreType.DMA((LINKS,)),
            pltpu.SemaphoreType.DMA((3, planes, 2)),
            pltpu.SemaphoreType.DMA((LOCALS,)),
        ],
        compiler_params=pltpu.CompilerParams(
            collective_id=0, has_side_effects=True, vmem_limit_bytes=63 * MIB
        ),
    )(x_in, c_in, qkv_in, o_in, u_in, d_in, bias_in, init, starts, reset)


def shards(
    dp_size,
    planes,
    sequence,
    query_key_value_weight,
    qv_bias,
    output_weight,
    out_bias,
    up_weight,
    up_bias,
    down_weight,
    back_bias,
    gain_one,
    shift_one,
    gain_two,
    shift_two,
    init_memory,
    reset,
    starts,
    cotangent,
):
    segs, local_rows, width = sequence.shape
    mem = init_memory.shape[0]
    tokens = starts.shape[1]
    hw = query_key_value_weight.shape[2]
    heads = hw * planes // DH
    assert segs == planes == 4 and 4 * hw == up_weight.shape[1] and mem <= local_rows and dp_size % INNER == 0
    t = lax.axis_index("tensor")
    position = t * local_rows + jnp.arange(local_rows, dtype=jnp.int32)
    is_memory = (position < mem) | (position >= mem + tokens)
    use_init = ((reset[:, None] > 0) & is_memory[None, :])[:, :, None]

    qkv_in = query_key_value_weight.transpose(1, 2, 0).reshape(3 * hw, width)
    qv_row = jnp.pad(qv_bias.reshape(2 * hw), (0, width - 2 * hw))
    bias_in = jnp.stack(
        [up_bias, qv_row, out_bias, back_bias, gain_one, shift_one, gain_two, shift_two]
        + [jnp.zeros((width,), bf16)] * 8
    )
    ga, gu, gd, dx, y, _, small = layer_call(
        planes,
        heads,
        sequence,
        cotangent,
        qkv_in,
        output_weight,
        up_weight,
        down_weight,
        bias_in,
        init_memory,
        starts,
        reset,
    )

    input_grad = jnp.where(use_init, 0.0, dx.astype(f32))
    ga, gu, gd = ga.astype(f32), gu.astype(f32), gd.astype(f32)
    if dp_size > INNER:
        groups = [[o * INNER + i for o in range(dp_size // INNER)] for i in range(INNER)]
        ga, gu, gd, small = lax.psum((ga, gu, gd, small), "dp", axis_index_groups=groups)
    own = lambda first: lax.dynamic_slice_in_dim(small, first + t, 1, 0)[0]
    return (
        y,
        input_grad,
        ga[: 3 * hw].reshape(3, hw, width).transpose(2, 0, 1),
        own(SMALL + 10)[: 2 * hw].reshape(2, hw),
        ga[3 * hw :],
        small[5],
        gu,
        own(6),
        gd,
        small[2],
        small[3],
        small[4],
        small[0],
        small[1],
        small[SMALL : SMALL + mem],
    )


def solution(mesh):
    in_specs = (
        P("dp", "tensor", None),
        P(None, None, "tensor"),
        P(None, "tensor"),
        P("tensor", None),
        P(),
        P(None, "tensor"),
        P("tensor"),
        P("tensor", None),
        P(),
        P(),
        P(),
        P(),
        P(),
        P(),
        P("dp"),
        P("dp", None),
        P("dp", "tensor", None),
    )
    out_specs = (
        P("dp", "tensor", None),
        P("dp", "tensor", None),
        P(None, None, "tensor"),
        P(None, "tensor"),
        P("tensor", None),
        P(),
        P(None, "tensor"),
        P("tensor"),
        P("tensor", None),
        P(),
        P(),
        P(),
        P(),
        P(),
        P(),
    )
    return jax.shard_map(
        functools.partial(shards, mesh.shape["dp"], mesh.shape["tensor"]),
        mesh=mesh,
        in_specs=in_specs,
        out_specs=out_specs,
        check_vma=False,
    )
```

```python
import functools

import jax
import jax.numpy as jnp
from jax import lax
from jax.experimental import pallas as pl
from jax.experimental.pallas import tpu as pltpu
from jax.sharding import PartitionSpec as P

DH = 64
NEGATIVE = -1e30
EPSILON = 1e-05
INNER = 8
MIB = 1 << 20

f32 = jnp.float32
bf16 = jnp.bfloat16
NN = (((1,), (0,)), ((), ()))
NT = (((1,), (1,)), ((), ()))
TN = (((0,), (0,)), ((), ()))
MESH = pl.DeviceIdType.MESH


def dot(a, b, dims=NN):
    return lax.dot_general(a, b, dims, preferred_element_type=f32)


def each(count, body):
    def step(i, carry):
        body(i)
        return carry

    lax.fori_loop(0, count, step, 0)


class Place:
    def __init__(self, planes):
        self.planes = planes
        self.dp = lax.axis_index("dp")
        self.t = lax.axis_index("tensor")
        self.core = self.dp % 2
        self.x = (self.dp // 2) % 2
        self.y = (self.dp // 4) % 2
        self.to_core = (self.dp + 1 - 2 * self.core, self.t)
        self.to_x = (self.dp + 2 - 4 * self.x, self.t)
        self.to_y = (self.dp + 4 - 8 * self.y, self.t)

    def plane(self, j):
        return lax.rem(self.t + j, self.planes)

    def to_plane(self, j):
        return (self.dp, self.plane(j))

    def partners(self):
        both = (self.to_x[0] + self.to_y[0] - self.dp, self.t)
        return [self.to_core, self.to_x, self.to_y, both] + [
            self.to_plane(j) for j in range(1, self.planes)
        ]

    def greet(self):
        barrier = pltpu.get_barrier_semaphore()
        partners = self.partners()
        for device in partners:
            pl.semaphore_signal(barrier, inc=1, device_id=device, device_id_type=MESH)
        pl.semaphore_wait(barrier, len(partners))


class Rows:
    def __init__(self, place, rows):
        self.piece = rows // (2 * INNER)
        self.half = rows // 2
        quarter = rows // 4
        core, x, y = place.core, place.x, place.y
        at = lambda n: pl.multiple_of(n, 16)
        base = core * self.half
        self.mine = at(base)
        self.others = at((1 - core) * self.half)
        self.a = at(base + (2 * y + x) * self.piece)
        self.b = at(base + quarter + (2 * x + y) * self.piece)
        self.a_pair = at(base + 2 * y * self.piece)
        self.b_pair = at(base + quarter + 2 * x * self.piece)
        self.a_far_pair = at(base + 2 * (1 - y) * self.piece)
        self.b_far_pair = at(base + quarter + 2 * (1 - x) * self.piece)
        self.a_far = at(base + (2 * y + 1 - x) * self.piece)
        self.b_far = at(base + quarter + (2 * x + 1 - y) * self.piece)


class Links:
    def __init__(self, send, recv):
        self.send, self.recv, self.count, self.all = send, recv, 0, []

    def copy(self, src, dst, device, recv=None, only=None):
        k = self.count
        self.count += 1
        made = pltpu.make_async_remote_copy(
            src_ref=src,
            dst_ref=dst,
            send_sem=self.send.at[k],
            recv_sem=self.recv.at[k] if recv is None else recv,
            device_id=device,
            device_id_type=MESH,
        )
        self.all.append((made, only))
        return made

    def finish(self, copies=None):
        for made, only in list(self.all):
            if copies is None or any(made is c for c in copies):
                self.all = [entry for entry in self.all if entry[0] is not made]
                if only is None:
                    made.wait_send()
                else:
                    pl.when(only)(made.wait_send)


def start(copies):
    for c in copies:
        c.start()


def arrive(copies):
    for c in copies:
        c.wait_recv()


def mirror_end(t, low, planes):
    return t + low * (planes - 1 - 2 * t)


class Way:
    pass


LINKS = 197
LOCALS = 16
SMALL = 16


def layer_kernel(
    planes,
    heads,
    block,
    x_in,
    c_in,
    qkv_in,
    o_in,
    u_in,
    d_in,
    bias_in,
    init_ref,
    starts_ref,
    reset_ref,
    ga_out,
    gu_out,
    gd_out,
    dx_out,
    y_out,
    p_hbm,
    small_ref,
    a_w,
    u_w,
    d_w,
    raw,
    x_go,
    c_go,
    y_got,
    xs,
    cs,
    x_s,
    bias,
    q_s,
    k_s,
    v_s,
    p2,
    o_s,
    do_s,
    delta_s,
    d_s,
    mask,
    acc,
    xhat_s,
    rstd_s,
    hb_s,
    act_s,
    dz_s,
    gb_s,
    half_in,
    pair_in,
    one_in,
    z_in,
    sm,
    sm_core,
    sm_low,
    sm_in,
    send,
    recv,
    recv_z,
    local,
):
    place = Place(planes)
    t = place.t
    others = range(1, planes)
    real, width = xs.shape[1:]
    rows = planes * block
    mem = init_ref.shape[0]
    hp = heads // planes
    hw = hp * DH
    links = Links(send, recv)
    r = Rows(place, a_w.shape[1])
    piece, half = r.piece, r.half
    vec = lambda i: bias_in[2 + i : 3 + i, :].astype(f32)
    add_up = lambda v: jnp.sum(v, axis=0, keepdims=True)

    def keep(k, src, dst):
        return pltpu.make_async_copy(src, dst, local.at[k])

    weights, g_outs = (a_w, u_w, d_w), (ga_out, gu_out, gd_out)

    low = t // 2
    middle = mirror_end(t, low, planes) == 1
    mirror = lambda n: n + low * (planes - 1 - 2 * n)

    def slot_shard(i):
        return mirror(i - mirror(t) if i == 1 else i)

    def neighbour(to):
        inside = (to >= 0) & (to < planes)
        return (place.dp, lax.rem(to + planes, planes)), inside

    gather = []
    for w in range(3):
        way = Way()
        way.own, way.z, way.one, way.two, way.core = [], [], [], [], []
        for step in (1, -1):
            device, inside = neighbour(t + step)
            way.own.append(
                (
                    inside,
                    [
                        links.copy(
                            weights[w].at[t, pl.ds(at, piece)],
                            weights[w].at[t, pl.ds(at, piece)],
                            device,
                            recv_z.at[w, t, n],
                            inside,
                        )
                        for n, at in enumerate((r.a, r.b))
                    ],
                )
            )
        for i in others:
            s = slot_shard(i)
            below = (t - s + planes - 1) // planes
            device, inside = neighbour(t + 2 * below - 1)
            here = lambda at, size: weights[w].at[s, pl.ds(at, size)]
            same = lambda at, size, to: links.copy(here(at, size), here(at, size), to)
            way.z.append(
                (
                    inside,
                    [
                        links.copy(
                            here(at, piece), here(at, piece), device, recv_z.at[w, s, n], inside
                        )
                        for n, at in enumerate((r.a, r.b))
                    ],
                )
            )
            way.one.append([same(r.a, piece, place.to_x), same(r.b, piece, place.to_y)])
            way.two.append(
                [same(r.a_pair, 2 * piece, place.to_y), same(r.b_pair, 2 * piece, place.to_x)]
            )
            way.core.append([same(r.mine, half, place.to_core)])
        gather.append(way)

    def when_start(inside, copies):
        pl.when(inside)(lambda: start(copies))

    def get_own(w):
        for inside, copies in gather[w].own:
            when_start(inside, copies)

    def get_z(w, i):
        inside, copies = gather[w].z[i - 1]
        arrive(copies)
        when_start(inside, copies)
        start(gather[w].one[i - 1])

    def get_stage(w, d):
        if d == 1:
            get_z(w, 1)
            pl.when(middle)(lambda: get_z(w, 2))
        elif d == 2:
            pl.when(middle)(lambda: get_z(w, 3))
            pl.when(~middle)(lambda: get_z(w, 2))
        else:
            pl.when(~middle)(lambda: get_z(w, 3))

    def get_one(w, i):
        arrive(gather[w].one[i - 1])
        start(gather[w].two[i - 1])

    def get_two(w, i):
        arrive(gather[w].two[i - 1])
        start(gather[w].core[i - 1])

    def get_core(w, i):
        arrive(gather[w].core[i - 1])

    def release(w):
        way = gather[w]
        links.finish([c for _, z in way.own + way.z for c in z])
        links.finish([c for part in way.one + way.two + way.core for c in part])

    def spread(sends, d):
        def go(plane, *picks):
            pl.when(t == plane)(lambda: start([sends[j - 1] for j in picks]))

        if d == 0:
            go(0, 1, 2, 3)
            go(3, 3, 2, 1)
        elif d == 1:
            go(1, 1, 2)
            go(2, 3, 2)
        else:
            go(1, 3)
            go(2, 1)

    def to_next(sends):
        pl.when((t == 0) | (t == 2))(lambda: start(sends[0:1]))
        pl.when((t == 1) | (t == 3))(lambda: start(sends[2:3]))

    def to_middle(sends):
        pl.when((t == 0) | (t == 2))(lambda: start(sends[2:3]))
        pl.when((t == 1) | (t == 3))(lambda: start(sends[0:1]))

    back_order = (2, 1, 3, 0)
    ways = []
    for w in range(3):
        g = weights[w]
        way = Way()
        way.core, way.pair, way.one, way.z = [], [], [], []
        for i in range(planes):
            j = back_order[i]
            s = place.plane(j)
            cut = lambda at, size: g.at[s, pl.ds(at, size)]
            way.core.append([links.copy(cut(r.others, half), half_in.at[w, i], place.to_core)])
            way.pair.append(
                [
                    links.copy(cut(r.a_far_pair, 2 * piece), pair_in.at[w, 0, i], place.to_y),
                    links.copy(cut(r.b_far_pair, 2 * piece), pair_in.at[w, 1, i], place.to_x),
                ]
            )
            way.one.append(
                [
                    links.copy(cut(r.a_far, piece), one_in.at[w, 0, i], place.to_x),
                    links.copy(cut(r.b_far, piece), one_in.at[w, 1, i], place.to_y),
                ]
            )
            if i + 1 < planes:
                way.z.append(
                    [
                        links.copy(cut(r.a, piece), z_in.at[w, i, 0], place.to_plane(j)),
                        links.copy(cut(r.b, piece), z_in.at[w, i, 1], place.to_plane(j)),
                    ]
                )
        at_home = lambda at: pl.multiple_of(at - r.mine, 16)
        f = half_in.at[w, 0]
        same = lambda at, size, to: links.copy(
            f.at[pl.ds(at_home(at), size)], f.at[pl.ds(at_home(at), size)], to
        )
        way.back1 = [same(r.a, piece, place.to_x), same(r.b, piece, place.to_y)]
        way.back2 = [
            same(r.a_pair, 2 * piece, place.to_y),
            same(r.b_pair, 2 * piece, place.to_x),
        ]
        mine = g_outs[w].at[pl.ds(r.mine, half)]
        way.back3 = [links.copy(f, mine, place.to_core)]
        way.out = keep(8 + w, f, mine)
        ways.append(way)

    def add_rows(g, s, at, size, got):
        def some(n):
            here = pl.multiple_of(n * piece, piece)
            span = pl.ds(pl.multiple_of(at + here, 16), piece)
            more = got[pl.ds(here, piece), :].astype(f32)
            g[s, span, :] = (g[s, span, :].astype(f32) + more).astype(bf16)

        if size == piece:
            some(0)
        else:
            each(size // piece, some)

    def back_shard(n):
        j = 0
        for i in range(planes - 1):
            j = jnp.where(n == i, back_order[i], j)
        return place.plane(j)

    def part_core(w, i):
        arrive(ways[w].core[i])
        add_rows(weights[w], back_shard(i), r.mine, half, half_in.at[w, i])
        start(ways[w].pair[i])

    def part_pair(w, i):
        arrive(ways[w].pair[i])
        s = back_shard(i)
        add_rows(weights[w], s, r.a_pair, 2 * piece, pair_in.at[w, 0, i])
        add_rows(weights[w], s, r.b_pair, 2 * piece, pair_in.at[w, 1, i])
        start(ways[w].one[i])

    def part_one(w, i):
        arrive(ways[w].one[i])
        s = back_shard(i)
        add_rows(weights[w], s, r.a, piece, one_in.at[w, 0, i])
        add_rows(weights[w], s, r.b, piece, one_in.at[w, 1, i])
        if i + 1 < planes:
            start(ways[w].z[i])

    def after_z(w):
        for z in ways[w].z:
            arrive(z)
        for i, at in enumerate((r.a, r.b)):
            v = weights[w][t, pl.ds(at, piece), :].astype(f32)
            for j in others:
                v = v + z_in[w, j - 1, i].astype(f32)
            half_in[w, 0, pl.ds(pl.multiple_of(at - r.mine, 16), piece), :] = v.astype(bf16)
        start(ways[w].back1)

    def after_back1(w):
        arrive(ways[w].back1)
        start(ways[w].back2)

    def after_back2(w):
        arrive(ways[w].back2)
        start(ways[w].back3)
        ways[w].out.start()

    def after_back3(w):
        arrive(ways[w].back3)

    x_send = [links.copy(x_go.at[place.plane(j)], xs.at[t], place.to_plane(j)) for j in others]
    c_send = [links.copy(c_go.at[place.plane(j)], cs.at[t], place.to_plane(j)) for j in others]
    b_send = [links.copy(bias_in, bias.at[t], place.to_plane(j)) for j in others]
    y_send = [links.copy(cs.at[place.plane(j)], y_got.at[t], place.to_plane(j)) for j in others]
    dx_send = [links.copy(xs.at[place.plane(j)], dx_out.at[t], place.to_plane(j)) for j in others]
    hops = []
    to_both = (place.to_x[0] + place.to_y[0] - place.dp, t)
    for e in range(2):
        mine, got = sm_low.at[e], sm_in.at[e]
        hops.append(
            [
                [links.copy(sm.at[e], sm_core.at[e], place.to_core)],
                [
                    links.copy(mine.at[0], got.at[n], to)
                    for n, to in enumerate((place.to_x, place.to_y, to_both))
                ],
                [links.copy(mine.at[1], got.at[2 + j], place.to_plane(j)) for j in others],
            ]
        )

    def in_order(parts, device):
        total = jnp.zeros_like(parts[0])
        for n in range(len(parts)):
            for part, who in zip(parts, device):
                total = total + jnp.where(who == n, part, 0.0)
        return total

    def hop(e, n):
        arrive(hops[e][n])
        low = lambda k: sm_in[e, k].astype(f32)
        if n == 0:
            sm_low[e, 0] = (sm[e] + sm_core[e]).astype(bf16)
        elif n == 1:
            x, y = place.x, place.y
            near = [2 * y + x, 2 * y + 1 - x, 2 * (1 - y) + x, 2 * (1 - y) + 1 - x]
            parts = [sm_low[e, 0].astype(f32)] + [low(k) for k in range(3)]
            sm_low[e, 1] = in_order(parts, near).astype(bf16)
        else:
            planes_of = [lax.rem(t + planes - j, planes) for j in range(planes)]
            total = in_order([sm_low[e, 1].astype(f32)] + [low(2 + j) for j in others], planes_of)
            small_ref[e * SMALL : (e + 1) * SMALL, :] = total
            return
        start(hops[e][n + 1])

    own_a = [
        keep(0, qkv_in, a_w.at[t, pl.ds(0, 3 * hw)]),
        keep(5, o_in, a_w.at[t, pl.ds(3 * hw, hw)]),
    ]
    own_u, own_d = keep(1, u_in, u_w.at[t]), keep(2, d_in, d_w.at[t])
    load_x, load_c = keep(3, x_in, raw), keep(4, c_in, raw)
    own_y = keep(6, cs.at[t], y_got.at[t])
    leave_y = keep(14, raw, y_out)
    own_dx = keep(7, xs.at[t], dx_out.at[t])

    def p_at(m):
        return p_hbm.at[m]

    p_save = lambda m: keep(12 + m % 2, p2.at[m % 2], p_at(m))

    start([*own_a, load_x, own_u, own_d])
    place.greet()
    for c in own_a:
        c.wait()
    get_own(0)
    start(b_send)
    own_u.wait()
    get_own(1)
    load_x.wait()
    x_go[...] = jnp.swapaxes(raw[...], 0, 1)
    spread(x_send, 0)
    xs[t] = x_go[t]
    load_c.start()

    bias[t] = bias_in[...]
    tokens = starts_ref.shape[1]

    def token_of(shape, axis):
        n = lax.broadcasted_iota(jnp.int32, shape, axis)
        inside = n % block
        return (n // block) * real + inside - mem, inside

    upto, _ = token_of((tokens, rows), 1)
    begun = lax.broadcasted_iota(jnp.int32, (tokens, rows), 0) <= upto
    begun = jnp.where(begun, 1.0, 0.0).astype(bf16)
    own_starts = starts_ref[pl.ds(t, 1), :].astype(f32).astype(bf16)
    docs = dot(jnp.broadcast_to(own_starts, (8, tokens)), begun)

    def codes(docs, axis):
        token, inside = token_of(docs.shape, axis)
        docs = jnp.where((token < 0) | (token >= tokens), -1.0, docs)
        return jnp.where(inside >= real, -2.0, docs)

    qc = codes(docs, 1)[0:1, :]
    kcodes = codes(docs.T, 0)[:, 0:1]
    for c in range(planes):
        span = slice(c * block, (c + 1) * block)
        kc = kcodes[span, :]
        allowed = ((qc == kc) | (qc < 0) | (kc < 0)) & (kc != -2.0)
        mask[span, :] = jnp.where(allowed, 0.0, NEGATIVE)
    for e in range(2):
        sm[e] = jnp.zeros((SMALL, width), f32)

    get_stage(0, 1)
    get_stage(1, 1)
    spread(x_send, 1)
    get_one(0, 1)
    pl.when(middle)(lambda: get_one(0, 2))
    get_stage(0, 2)
    spread(x_send, 2)
    get_one(1, 1)
    get_two(0, 1)
    pl.when(~middle)(lambda: get_one(0, 2))
    get_stage(0, 3)
    get_stage(1, 2)
    own_d.wait()
    get_own(2)
    get_two(1, 1)
    get_two(0, 2)
    get_one(0, 3)
    get_one(1, 2)
    load_c.wait()
    c_go[...] = jnp.swapaxes(raw[...], 0, 1)
    cs[t] = c_go[t]
    arrive(x_send)
    arrive(b_send)
    afresh = reset_ref[t] > 0
    for c in range(planes):
        x_s[c, 0:real, :] = xs[c]
        x_s[c, real:block, :] = jnp.zeros((block - real, width), bf16)
    last = real - mem
    x_s[0, 0:mem, :] = jnp.where(afresh, init_ref[...], xs[0, 0:mem, :])
    x_s[planes - 1, last:real, :] = jnp.where(afresh, init_ref[...], xs[planes - 1, last:real, :])
    acc[...] = x_s[...].reshape(rows, width).astype(f32) + vec(0)

    forward_pokes = [
        (0, 1, lambda: get_stage(1, 3)),
        (0, 2, lambda: get_two(0, 3)),
        (0, 3, lambda: get_two(1, 2)),
        (1, 0, lambda: get_stage(2, 1)),
        (1, 0, lambda: spread(c_send, 0)),
        (1, 0, lambda: spread(c_send, 1)),
        (1, 1, lambda: get_one(1, 3)),
        (2, 0, lambda: get_one(2, 1)),
        (2, 1, lambda: get_stage(2, 2)),
        (2, 1, lambda: spread(c_send, 2)),
        (2, 2, lambda: get_two(1, 3)),
        (3, 0, lambda: get_two(2, 1)),
        (3, 1, lambda: get_one(2, 2)),
        (3, 2, lambda: get_stage(2, 3)),
    ]

    def poke_at(pokes, *now):
        for *when, poke in pokes:
            hit = now[0] == when[0]
            for a, b in zip(now[1:], when[1:]):
                hit = hit & (a == b)
            pl.when(hit)(poke)

    def forward_order(j):
        picked = t
        for i in others:
            picked = jnp.where(j == i, slot_shard(i), picked)
        return picked

    head_feats = lambda i: pl.ds(pl.multiple_of(i * DH, DH), DH)

    def attention(j):
        s = forward_order(j)
        for i in others:
            pl.when(j == i)(lambda: get_core(0, i))

        poke_at([p for p in forward_pokes if p[1] == 0], j, 0)
        x = x_s[...].reshape(rows, width)
        qkv = dot(a_w[s, 0 : 3 * hw, :], x, NT)
        b = bias[s].astype(f32).T
        bq, bv = b[0:hw, 1:2], b[0:hw, 8:9]
        q = ((qkv[0:hw] + bq).astype(bf16).astype(f32) * (DH**-0.5)).astype(bf16)
        k = qkv[hw : 2 * hw].astype(bf16)
        v = (qkv[2 * hw :] + bv).astype(bf16)
        for i in range(hp):
            feats = slice(i * DH, (i + 1) * DH)
            q_s[s * hp + i], k_s[s * hp + i], v_s[s * hp + i] = q[feats], k[feats], v[feats]

        def head(i):
            h = s * hp + i
            m = j * hp + i
            poke_at([p for p in forward_pokes if p[1] > 0], j, i + 1)
            pl.when(m >= 2)(lambda: p_save(m).wait())
            scores = dot(k_s[h], q_s[h], TN) + mask[...]
            e = jnp.exp(scores - jnp.max(scores, axis=0, keepdims=True))
            p = (e * (1.0 / jnp.sum(e, axis=0, keepdims=True))).astype(bf16)
            p2[m % 2] = p
            o_s[s, head_feats(i), :] = dot(v_s[h], p).astype(bf16)
            keep(12 + m % 2, p2.at[m % 2], p_at(h)).start()

        each(hp, head)
        acc[...] += dot(o_s[s], a_w[s, 3 * hw :, :], TN)

    each(planes, attention)

    def first_norm(c):
        span = pl.ds(pl.multiple_of(c * block, block), block)
        v = acc[span, :]
        v = v - jnp.mean(v, axis=1, keepdims=True)
        rstd = lax.rsqrt(jnp.mean(v * v, axis=1, keepdims=True) + EPSILON)
        xhat = v * rstd
        rstd_s[span, :] = rstd
        xhat_s[span, :] = xhat
        h = xhat * vec(2) + vec(3)
        hb_s[span, :] = h.astype(bf16)
        acc[span, :] = h + vec(1)

    each(planes, first_norm)
    get_one(2, 3)

    def up(j):
        s = forward_order(j)
        for i in others:
            pl.when(j == i)(lambda: get_core(1, i))
        pl.when(j == 0)(lambda: get_two(2, 2))
        for c in range(planes):
            span = pl.ds(c * block, block)
            z = dot(hb_s[span, :], u_w[s]) + bias[s, 0:1, :].astype(f32)
            phi = 0.5 + 0.5 * lax.erf(z * (0.5**0.5))
            act_s[s, span, :] = (z * phi).astype(bf16)
            dz_s[s, span, :] = (phi + z * jnp.exp(-0.5 * z * z) * 0.3989422804014327).astype(bf16)

    each(planes, up)
    get_two(2, 3)

    def down(j):
        s = forward_order(j)
        for i in others:
            pl.when(j == i)(lambda: get_core(2, i))
        acc[...] += dot(act_s[s], d_w[s])

    each(planes, down)
    arrive(c_send)

    zero = jnp.zeros((1, width), f32)

    def second_norm(c, sums):
        span = pl.ds(pl.multiple_of(c * block, block), block)
        v = acc[span, :]
        v = v - jnp.mean(v, axis=1, keepdims=True)
        rstd = lax.rsqrt(jnp.mean(v * v, axis=1, keepdims=True) + EPSILON)
        xhat = v * rstd
        gb_s[span, :] = jnp.zeros((block, width), bf16)
        gb_s[pl.ds(pl.multiple_of(c * block, block), real), :] = cs[c]
        g = gb_s[span, :].astype(f32)
        cs[c] = (xhat * vec(4) + vec(5)).astype(bf16)[0:real]
        d = g * vec(4)
        g2 = rstd * (
            d
            - jnp.mean(d, axis=1, keepdims=True)
            - xhat * jnp.mean(d * xhat, axis=1, keepdims=True)
        )
        acc[span, :] = g2
        gb_s[span, :] = g2.astype(bf16)
        return sums[0] + add_up(g * xhat), sums[1] + add_up(g), sums[2] + add_up(g2)

    sums = lax.fori_loop(0, planes, second_norm, (zero, zero, zero))
    sm[0, 0:3, :] = jnp.concatenate(list(sums), axis=0)
    start(y_send)
    own_y.start()

    down_pokes = [
        (3, lambda: part_core(2, 0)),
    ]
    up_pokes = [
        (0, lambda: part_core(2, 1)),
        (1, lambda: part_core(2, 2)),
        (2, lambda: part_pair(2, 0)),
        (2, lambda: part_core(2, 3)),
        (3, lambda: part_core(1, 0)),
        (3, lambda: part_pair(2, 1)),
        (3, lambda: part_core(1, 1)),
    ]

    def back_down(n):
        s = back_shard(n)
        poke_at(down_pokes, n)
        du = dot(gb_s[...], d_w[s], NT)
        dz_s[s] = (du * dz_s[s].astype(f32)).astype(bf16)
        d_w[s] = dot(act_s[s], gb_s[...], TN).astype(bf16)
        for k in range(planes):
            pl.when(n == k)(ways[2].core[k][0].start)

    release(2)
    each(planes, back_down)

    def back_up(n):
        s = back_shard(n)
        poke_at(up_pokes, n)
        dz = dz_s[s]
        sm[0, pl.ds(6 + s, 1), :] = add_up(dz.astype(f32))
        acc[...] += dot(dz, u_w[s], NT)
        u_w[s] = dot(hb_s[...], dz, TN).astype(bf16)
        for k in range(planes):
            pl.when(n == k)(ways[1].core[k][0].start)

    release(1)
    each(planes, back_up)
    for m in (heads - 2, heads - 1):
        p_save(m).wait()

    p_load = lambda m: keep(
        12 + m % 2, p_at(back_shard(m // hp) * hp + m % hp), p2.at[m % 2]
    )
    p_load(0).start()

    part_pair(2, 2)
    part_core(1, 2)

    def back_first_norm(c, sums):
        span = pl.ds(pl.multiple_of(c * block, block), block)
        xhat = xhat_s[span, :]
        g = acc[span, :]
        d = g * vec(2)
        g1 = rstd_s[span, :] * (
            d
            - jnp.mean(d, axis=1, keepdims=True)
            - xhat * jnp.mean(d * xhat, axis=1, keepdims=True)
        )
        acc[span, :] = g1
        gb_s[span, :] = g1.astype(bf16)
        return sums[0] + add_up(g * xhat), sums[1] + add_up(g), sums[2] + add_up(g1)

    sums = lax.fori_loop(0, planes, back_first_norm, (zero, zero, zero))
    sm[0, 3:6, :] = jnp.concatenate(list(sums), axis=0)
    start(hops[0][0])
    back_pokes = [
        (0, 0, lambda: part_one(2, 0)),
        (0, 1, lambda: part_core(1, 3)),
        (0, 2, lambda: hop(0, 0)),
        (0, 2, lambda: part_pair(2, 3)),
        (0, 4, lambda: part_pair(1, 0)),
        (1, 0, lambda: part_one(2, 1)),
        (1, 3, lambda: part_pair(1, 1)),
        (1, 3, lambda: part_core(0, 0)),
        (1, 3, lambda: part_one(2, 2)),
        (2, 0, lambda: part_pair(1, 2)),
        (2, 3, lambda: part_pair(1, 3)),
        (2, 3, lambda: hop(0, 1)),
        (2, 3, lambda: part_core(0, 1)),
        (2, 4, lambda: part_one(2, 3)),
        (2, 4, lambda: after_z(2)),
        (3, 0, lambda: part_one(1, 0)),
        (3, 1, lambda: part_one(1, 1)),
        (3, 3, lambda: part_core(0, 2)),
        (3, 3, lambda: part_pair(0, 0)),
        (3, 4, lambda: part_one(1, 2)),
    ]

    def back_attention(n):
        s = back_shard(n)
        poke_at([p for p in back_pokes if p[1] == 0], n, 0)
        do = dot(a_w[s, 3 * hw :, :], gb_s[...], NT).astype(bf16)
        do_s[...] = do
        prod = do.astype(f32) * o_s[s].astype(f32)
        for i in range(hp):
            delta_s[i] = add_up(prod[i * DH : (i + 1) * DH])

        def head(i):
            h = s * hp + i
            m = n * hp + i
            p_load(m).wait()
            pl.when(m + 1 < heads)(lambda: p_load(m + 1).start())
            poke_at([p for p in back_pokes if 0 < p[1] < 4], n, i + 1)
            slot = m % 2
            p, do = p2[slot], do_s[head_feats(i), :]
            dp = dot(v_s[h], do, TN)
            ds = (p.astype(f32) * (dp - delta_s[i])).astype(bf16)
            d_s[head_feats(i), :] = (dot(k_s[h], ds) * (DH**-0.5)).astype(bf16)
            d_s[head_feats(hp + i), :] = dot(q_s[h], ds, NT).astype(bf16)
            d_s[head_feats(2 * hp + i), :] = dot(do, p, NT).astype(bf16)

        each(hp, head)
        poke_at([p for p in back_pokes if p[1] == 4], n, 4)
        dqkv = d_s[...]
        sums = dot(jnp.ones((8, rows), bf16), dqkv, NT)[0:1, :]
        sm[1, pl.ds(10 + s, 1), 0:hw] = sums[:, 0:hw]
        sm[1, pl.ds(10 + s, 1), hw : 2 * hw] = sums[:, 2 * hw :]
        acc[...] += dot(dqkv, a_w[s, 0 : 3 * hw, :], TN)
        a_w[s, 0 : 3 * hw, :] = dot(dqkv, x_s[...].reshape(rows, width)).astype(bf16)
        a_w[s, 3 * hw :, :] = dot(o_s[s], gb_s[...]).astype(bf16)
        for k in range(planes):
            pl.when(n == k)(ways[0].core[k][0].start)

    release(0)
    each(planes, back_attention)

    for c in range(planes):
        xs[c] = acc[c * block : c * block + real, :].astype(bf16)
    part_one(1, 3)
    to_next(dx_send)
    own_dx.start()
    dx_last = (planes - 1) * block + last
    both = acc[0:mem, :] + acc[dx_last : dx_last + mem, :]
    sm[1, 0:mem, :] = jnp.where(afresh, both, 0.0)
    start(hops[1][0])
    arrive(y_send)
    own_y.wait()
    raw[...] = jnp.swapaxes(y_got[...], 0, 1)
    leave_y.start()
    part_pair(0, 1)
    part_core(0, 3)
    hop(1, 0)
    after_back1(2)
    part_pair(0, 2)
    after_z(1)
    part_one(0, 0)
    part_one(0, 1)
    part_pair(0, 3)
    hop(1, 1)
    after_back2(2)
    part_one(0, 2)
    start(dx_send[1:2])
    after_back1(1)
    after_back3(2)
    part_one(0, 3)
    to_middle(dx_send)
    after_z(0)
    after_back2(1)
    after_back1(0)
    after_back2(0)
    after_back3(1)
    hop(0, 2)
    hop(1, 2)
    after_back3(0)

    arrive(dx_send)
    leave_y.wait()
    own_dx.wait()
    for way in ways:
        way.out.wait()
    links.finish()


def layer_call(planes, heads, x_in, c_in, qkv_in, o_in, u_in, d_in, bias_in, init, starts, reset):
    real, _, width = x_in.shape
    block = -(-real // 16) * 16
    rows = planes * block
    hp = heads // planes
    hw = hp * DH
    shard = u_in.shape
    hidden = shard[1]
    piece, half = shard[0] // (2 * INNER), shard[0] // 2
    S = jax.ShapeDtypeStruct
    V = pltpu.VMEM
    outs = (
        S(shard, bf16),
        S(shard, bf16),
        S(shard, bf16),
        S((planes, real, width), bf16),
        S((real, planes, width), bf16),
        S((heads, rows, rows), bf16),
        S((2 * SMALL, width), f32),
    )
    any_spec = pl.BlockSpec(memory_space=pl.ANY)
    vmem_spec = pl.BlockSpec(memory_space=pltpu.VMEM)
    return pl.pallas_call(
        functools.partial(layer_kernel, planes, heads, block),
        out_shape=outs,
        in_specs=[any_spec] * 6 + [vmem_spec] * 3 + [pl.BlockSpec(memory_space=pltpu.SMEM)],
        out_specs=[any_spec] * 6 + [vmem_spec],
        scratch_shapes=[
            V((planes, *shard), bf16),
            V((planes, *shard), bf16),
            V((planes, *shard), bf16),
            V((real, planes, width), bf16),
            V((planes, real, width), bf16),
            V((planes, real, width), bf16),
            V((planes, real, width), bf16),
            V((planes, real, width), bf16),
            V((planes, real, width), bf16),
            V((planes, block, width), bf16),
            V((planes, *bias_in.shape), bf16),
            V((heads, DH, rows), bf16),
            V((heads, DH, rows), bf16),
            V((heads, DH, rows), bf16),
            V((2, rows, rows), bf16),
            V((planes, hw, rows), bf16),
            V((hw, rows), bf16),
            V((hp, 1, rows), f32),
            V((3 * hw, rows), bf16),
            V((rows, rows), f32),
            V((rows, width), f32),
            V((rows, width), f32),
            V((rows, 1), f32),
            V((rows, width), bf16),
            V((planes, rows, hidden), bf16),
            V((planes, rows, hidden), bf16),
            V((rows, width), bf16),
            V((3, planes, half, hidden), bf16),
            V((3, 2, planes, 2 * piece, hidden), bf16),
            V((3, 2, planes, piece, hidden), bf16),
            V((3, planes - 1, 2, piece, hidden), bf16),
            V((2, SMALL, width), f32),
            V((2, SMALL, width), f32),
            V((2, 2, SMALL, width), bf16),
            V((2, 2 + planes, SMALL, width), bf16),
            pltpu.SemaphoreType.DMA((LINKS,)),
            pltpu.SemaphoreType.DMA((LINKS,)),
            pltpu.SemaphoreType.DMA((3, planes, 2)),
            pltpu.SemaphoreType.DMA((LOCALS,)),
        ],
        compiler_params=pltpu.CompilerParams(
            collective_id=0, has_side_effects=True, vmem_limit_bytes=63 * MIB
        ),
    )(x_in, c_in, qkv_in, o_in, u_in, d_in, bias_in, init, starts, reset)


def shards(
    dp_size,
    planes,
    sequence,
    query_key_value_weight,
    qv_bias,
    output_weight,
    out_bias,
    up_weight,
    up_bias,
    down_weight,
    back_bias,
    gain_one,
    shift_one,
    gain_two,
    shift_two,
    init_memory,
    reset,
    starts,
    cotangent,
):
    segs, local_rows, width = sequence.shape
    mem = init_memory.shape[0]
    tokens = starts.shape[1]
    hw = query_key_value_weight.shape[2]
    heads = hw * planes // DH
    assert segs == planes == 4 and 4 * hw == up_weight.shape[1] and mem <= local_rows and dp_size % INNER == 0
    t = lax.axis_index("tensor")
    position = t * local_rows + jnp.arange(local_rows, dtype=jnp.int32)
    is_memory = (position < mem) | (position >= mem + tokens)
    use_init = ((reset[:, None] > 0) & is_memory[None, :])[:, :, None]

    qkv_in = query_key_value_weight.transpose(1, 2, 0).reshape(3 * hw, width)
    qv_rows = jnp.pad(qv_bias, ((0, 0), (0, width - hw)))
    vectors = (out_bias, back_bias, gain_one, shift_one, gain_two, shift_two)
    bias_rows = [up_bias[None], qv_rows[0:1], *(v[None] for v in vectors), qv_rows[1:2]]
    place = jnp.arange(16)[:, None]
    bias_in = jnp.zeros((16, width), bf16)
    for k, row in enumerate(bias_rows):
        bias_in = jnp.where(place == k, row, bias_in)
    ga, gu, gd, dx, y, _, small = layer_call(
        planes,
        heads,
        jnp.swapaxes(sequence, 0, 1),
        jnp.swapaxes(cotangent, 0, 1),
        qkv_in,
        output_weight,
        up_weight,
        down_weight,
        bias_in,
        init_memory,
        starts,
        reset,
    )

    input_grad = jnp.where(use_init, 0.0, dx.astype(f32))
    ga, gu, gd = ga.astype(f32), gu.astype(f32), gd.astype(f32)
    if dp_size > INNER:
        groups = [[o * INNER + i for o in range(dp_size // INNER)] for i in range(INNER)]
        ga, gu, gd, small = lax.psum((ga, gu, gd, small), "dp", axis_index_groups=groups)
    own = lambda first: lax.dynamic_slice_in_dim(small, first + t, 1, 0)[0]
    return (
        jnp.swapaxes(y, 0, 1),
        input_grad,
        ga[: 3 * hw].reshape(3, hw, width).transpose(2, 0, 1),
        own(SMALL + 10)[: 2 * hw].reshape(2, hw),
        ga[3 * hw :],
        small[5],
        gu,
        own(6),
        gd,
        small[2],
        small[3],
        small[4],
        small[0],
        small[1],
        small[SMALL : SMALL + mem],
    )


def solution(mesh):
    in_specs = (
        P("dp", "tensor", None),
        P(None, None, "tensor"),
        P(None, "tensor"),
        P("tensor", None),
        P(),
        P(None, "tensor"),
        P("tensor"),
        P("tensor", None),
        P(),
        P(),
        P(),
        P(),
        P(),
        P(),
        P("dp"),
        P("dp", None),
        P("dp", "tensor", None),
    )
    out_specs = (
        P("dp", "tensor", None),
        P("dp", "tensor", None),
        P(None, None, "tensor"),
        P(None, "tensor"),
        P("tensor", None),
        P(),
        P(None, "tensor"),
        P("tensor"),
        P("tensor", None),
        P(),
        P(),
        P(),
        P(),
        P(),
        P(),
    )
    return jax.shard_map(
        functools.partial(shards, mesh.shape["dp"], mesh.shape["tensor"]),
        mesh=mesh,
        in_specs=in_specs,
        out_specs=out_specs,
        check_vma=False,
    )
```

```python
import functools

import jax
import jax.numpy as jnp
from jax import lax
from jax.experimental import pallas as pl
from jax.experimental.pallas import tpu as pltpu
from jax.sharding import PartitionSpec as P

DH = 64
NEGATIVE = -1e30
EPSILON = 1e-05
INNER = 8
MIB = 1 << 20

f32 = jnp.float32
bf16 = jnp.bfloat16
NN = (((1,), (0,)), ((), ()))
NT = (((1,), (1,)), ((), ()))
TN = (((0,), (0,)), ((), ()))
MESH = pl.DeviceIdType.MESH


def dot(a, b, dims=NN):
    return lax.dot_general(a, b, dims, preferred_element_type=f32)


def each(count, body):
    def step(i, carry):
        body(i)
        return carry

    lax.fori_loop(0, count, step, 0)


class Place:
    def __init__(self, planes):
        self.planes = planes
        self.dp = lax.axis_index("dp")
        self.t = lax.axis_index("tensor")
        self.core = self.dp % 2
        self.x = (self.dp // 2) % 2
        self.y = (self.dp // 4) % 2
        self.to_core = (self.dp + 1 - 2 * self.core, self.t)
        self.to_x = (self.dp + 2 - 4 * self.x, self.t)
        self.to_y = (self.dp + 4 - 8 * self.y, self.t)

    def plane(self, j):
        return lax.rem(self.t + j, self.planes)

    def to_plane(self, j):
        return (self.dp, self.plane(j))

    def partners(self):
        both = (self.to_x[0] + self.to_y[0] - self.dp, self.t)
        return [self.to_core, self.to_x, self.to_y, both] + [
            self.to_plane(j) for j in range(1, self.planes)
        ]

    def greet(self):
        barrier = pltpu.get_barrier_semaphore()
        partners = self.partners()
        for device in partners:
            pl.semaphore_signal(barrier, inc=1, device_id=device, device_id_type=MESH)
        pl.semaphore_wait(barrier, len(partners))


class Rows:
    def __init__(self, place, rows):
        self.piece = rows // (2 * INNER)
        self.half = rows // 2
        quarter = rows // 4
        core, x, y = place.core, place.x, place.y
        at = lambda n: pl.multiple_of(n, 16)
        base = core * self.half
        self.mine = at(base)
        self.others = at((1 - core) * self.half)
        self.a = at(base + (2 * y + x) * self.piece)
        self.b = at(base + quarter + (2 * x + y) * self.piece)
        self.a_pair = at(base + 2 * y * self.piece)
        self.b_pair = at(base + quarter + 2 * x * self.piece)
        self.a_far_pair = at(base + 2 * (1 - y) * self.piece)
        self.b_far_pair = at(base + quarter + 2 * (1 - x) * self.piece)
        self.a_far = at(base + (2 * y + 1 - x) * self.piece)
        self.b_far = at(base + quarter + (2 * x + 1 - y) * self.piece)


class Links:
    def __init__(self, send, recv):
        self.send, self.recv, self.count, self.all = send, recv, 0, []

    def copy(self, src, dst, device, recv=None, only=None):
        k = self.count
        self.count += 1
        made = pltpu.make_async_remote_copy(
            src_ref=src,
            dst_ref=dst,
            send_sem=self.send.at[k],
            recv_sem=self.recv.at[k] if recv is None else recv,
            device_id=device,
            device_id_type=MESH,
        )
        self.all.append((made, only))
        return made

    def finish(self, copies=None):
        for made, only in list(self.all):
            if copies is None or any(made is c for c in copies):
                self.all = [entry for entry in self.all if entry[0] is not made]
                if only is None:
                    made.wait_send()
                else:
                    pl.when(only)(made.wait_send)


def start(copies):
    for c in copies:
        c.start()


def arrive(copies):
    for c in copies:
        c.wait_recv()


def mirror_end(t, low, planes):
    return t + low * (planes - 1 - 2 * t)


class Way:
    pass


LINKS = 197
LOCALS = 16
SMALL = 16


def layer_kernel(
    planes,
    heads,
    block,
    x_in,
    c_in,
    qkv_in,
    o_in,
    u_in,
    d_in,
    up_bias,
    qv_bias,
    out_bias,
    back_bias,
    gain_one,
    shift_one,
    gain_two,
    shift_two,
    init_ref,
    starts_ref,
    reset_ref,
    ga_out,
    gu_out,
    gd_out,
    dx_out,
    y_out,
    p_hbm,
    small_ref,
    a_w,
    u_w,
    d_w,
    raw,
    x_go,
    c_go,
    y_got,
    xs,
    cs,
    x_s,
    bias,
    q_s,
    k_s,
    v_s,
    p2,
    o_s,
    do_s,
    delta_s,
    d_s,
    mask,
    acc,
    xhat_s,
    rstd_s,
    hb_s,
    act_s,
    dz_s,
    gb_s,
    half_in,
    pair_in,
    one_in,
    z_in,
    sm,
    sm_core,
    sm_low,
    sm_in,
    send,
    recv,
    recv_z,
    local,
):
    place = Place(planes)
    t = place.t
    others = range(1, planes)
    real, width = xs.shape[1:]
    rows = planes * block
    mem = init_ref.shape[0]
    hidden = u_w.shape[2]
    hp = heads // planes
    hw = hp * DH
    links = Links(send, recv)
    r = Rows(place, a_w.shape[1])
    piece, half = r.piece, r.half
    vectors = (out_bias, back_bias, gain_one, shift_one, gain_two, shift_two)
    vec = lambda i: vectors[i][...].astype(f32).reshape(1, width)
    add_up = lambda v: jnp.sum(v, axis=0, keepdims=True)

    def keep(k, src, dst):
        return pltpu.make_async_copy(src, dst, local.at[k])

    weights, g_outs = (a_w, u_w, d_w), (ga_out, gu_out, gd_out)

    low = t // 2
    middle = mirror_end(t, low, planes) == 1
    mirror = lambda n: n + low * (planes - 1 - 2 * n)

    def slot_shard(i):
        return mirror(i - mirror(t) if i == 1 else i)

    def neighbour(to):
        inside = (to >= 0) & (to < planes)
        return (place.dp, lax.rem(to + planes, planes)), inside

    gather = []
    for w in range(3):
        way = Way()
        way.own, way.z, way.one, way.two, way.core = [], [], [], [], []
        for step in (1, -1):
            device, inside = neighbour(t + step)
            way.own.append(
                (
                    inside,
                    [
                        links.copy(
                            weights[w].at[t, pl.ds(at, piece)],
                            weights[w].at[t, pl.ds(at, piece)],
                            device,
                            recv_z.at[w, t, n],
                            inside,
                        )
                        for n, at in enumerate((r.a, r.b))
                    ],
                )
            )
        for i in others:
            s = slot_shard(i)
            below = (t - s + planes - 1) // planes
            device, inside = neighbour(t + 2 * below - 1)
            here = lambda at, size: weights[w].at[s, pl.ds(at, size)]
            same = lambda at, size, to: links.copy(here(at, size), here(at, size), to)
            way.z.append(
                (
                    inside,
                    [
                        links.copy(
                            here(at, piece), here(at, piece), device, recv_z.at[w, s, n], inside
                        )
                        for n, at in enumerate((r.a, r.b))
                    ],
                )
            )
            way.one.append([same(r.a, piece, place.to_x), same(r.b, piece, place.to_y)])
            way.two.append(
                [same(r.a_pair, 2 * piece, place.to_y), same(r.b_pair, 2 * piece, place.to_x)]
            )
            way.core.append([same(r.mine, half, place.to_core)])
        gather.append(way)

    def when_start(inside, copies):
        pl.when(inside)(lambda: start(copies))

    def get_own(w):
        for inside, copies in gather[w].own:
            when_start(inside, copies)

    def get_z(w, i):
        inside, copies = gather[w].z[i - 1]
        arrive(copies)
        when_start(inside, copies)
        start(gather[w].one[i - 1])

    def get_stage(w, d):
        if d == 1:
            get_z(w, 1)
            pl.when(middle)(lambda: get_z(w, 2))
        elif d == 2:
            pl.when(middle)(lambda: get_z(w, 3))
            pl.when(~middle)(lambda: get_z(w, 2))
        else:
            pl.when(~middle)(lambda: get_z(w, 3))

    def get_one(w, i):
        arrive(gather[w].one[i - 1])
        start(gather[w].two[i - 1])

    def get_two(w, i):
        arrive(gather[w].two[i - 1])
        start(gather[w].core[i - 1])

    def get_core(w, i):
        arrive(gather[w].core[i - 1])

    def release(w):
        way = gather[w]
        links.finish([c for _, z in way.own + way.z for c in z])
        links.finish([c for part in way.one + way.two + way.core for c in part])

    def spread(sends, d):
        def go(plane, *picks):
            pl.when(t == plane)(lambda: start([sends[j - 1] for j in picks]))

        if d == 0:
            go(0, 1, 2, 3)
            go(3, 3, 2, 1)
        elif d == 1:
            go(1, 1, 2)
            go(2, 3, 2)
        else:
            go(1, 3)
            go(2, 1)

    def to_next(sends):
        pl.when((t == 0) | (t == 2))(lambda: start(sends[0:1]))
        pl.when((t == 1) | (t == 3))(lambda: start(sends[2:3]))

    def to_middle(sends):
        pl.when((t == 0) | (t == 2))(lambda: start(sends[2:3]))
        pl.when((t == 1) | (t == 3))(lambda: start(sends[0:1]))

    back_order = (2, 1, 3, 0)
    ways = []
    for w in range(3):
        g = weights[w]
        way = Way()
        way.core, way.pair, way.one, way.z = [], [], [], []
        for i in range(planes):
            j = back_order[i]
            s = place.plane(j)
            cut = lambda at, size: g.at[s, pl.ds(at, size)]
            way.core.append([links.copy(cut(r.others, half), half_in.at[w, i], place.to_core)])
            way.pair.append(
                [
                    links.copy(cut(r.a_far_pair, 2 * piece), pair_in.at[w, 0, i], place.to_y),
                    links.copy(cut(r.b_far_pair, 2 * piece), pair_in.at[w, 1, i], place.to_x),
                ]
            )
            way.one.append(
                [
                    links.copy(cut(r.a_far, piece), one_in.at[w, 0, i], place.to_x),
                    links.copy(cut(r.b_far, piece), one_in.at[w, 1, i], place.to_y),
                ]
            )
            if i + 1 < planes:
                way.z.append(
                    [
                        links.copy(cut(r.a, piece), z_in.at[w, i, 0], place.to_plane(j)),
                        links.copy(cut(r.b, piece), z_in.at[w, i, 1], place.to_plane(j)),
                    ]
                )
        at_home = lambda at: pl.multiple_of(at - r.mine, 16)
        f = half_in.at[w, 0]
        same = lambda at, size, to: links.copy(
            f.at[pl.ds(at_home(at), size)], f.at[pl.ds(at_home(at), size)], to
        )
        way.back1 = [same(r.a, piece, place.to_x), same(r.b, piece, place.to_y)]
        way.back2 = [
            same(r.a_pair, 2 * piece, place.to_y),
            same(r.b_pair, 2 * piece, place.to_x),
        ]
        mine = g_outs[w].at[pl.ds(r.mine, half)]
        way.back3 = [links.copy(f, mine, place.to_core)]
        way.out = keep(8 + w, f, mine)
        ways.append(way)

    def add_rows(g, s, at, size, got):
        def some(n):
            here = pl.multiple_of(n * piece, piece)
            span = pl.ds(pl.multiple_of(at + here, 16), piece)
            more = got[pl.ds(here, piece), :].astype(f32)
            g[s, span, :] = (g[s, span, :].astype(f32) + more).astype(bf16)

        if size == piece:
            some(0)
        else:
            each(size // piece, some)

    def back_shard(n):
        j = 0
        for i in range(planes - 1):
            j = jnp.where(n == i, back_order[i], j)
        return place.plane(j)

    def part_core(w, i):
        arrive(ways[w].core[i])
        add_rows(weights[w], back_shard(i), r.mine, half, half_in.at[w, i])
        start(ways[w].pair[i])

    def part_pair(w, i):
        arrive(ways[w].pair[i])
        s = back_shard(i)
        add_rows(weights[w], s, r.a_pair, 2 * piece, pair_in.at[w, 0, i])
        add_rows(weights[w], s, r.b_pair, 2 * piece, pair_in.at[w, 1, i])
        start(ways[w].one[i])

    def part_one(w, i):
        arrive(ways[w].one[i])
        s = back_shard(i)
        add_rows(weights[w], s, r.a, piece, one_in.at[w, 0, i])
        add_rows(weights[w], s, r.b, piece, one_in.at[w, 1, i])
        if i + 1 < planes:
            start(ways[w].z[i])

    def after_z(w):
        for z in ways[w].z:
            arrive(z)
        for i, at in enumerate((r.a, r.b)):
            v = weights[w][t, pl.ds(at, piece), :].astype(f32)
            for j in others:
                v = v + z_in[w, j - 1, i].astype(f32)
            half_in[w, 0, pl.ds(pl.multiple_of(at - r.mine, 16), piece), :] = v.astype(bf16)
        start(ways[w].back1)

    def after_back1(w):
        arrive(ways[w].back1)
        start(ways[w].back2)

    def after_back2(w):
        arrive(ways[w].back2)
        start(ways[w].back3)
        ways[w].out.start()

    def after_back3(w):
        arrive(ways[w].back3)

    x_send = [links.copy(x_go.at[place.plane(j)], xs.at[t], place.to_plane(j)) for j in others]
    c_send = [links.copy(c_go.at[place.plane(j)], cs.at[t], place.to_plane(j)) for j in others]
    b_send = [links.copy(bias.at[t], bias.at[t], place.to_plane(j)) for j in others]
    y_send = [links.copy(cs.at[place.plane(j)], y_got.at[t], place.to_plane(j)) for j in others]
    dx_send = [links.copy(xs.at[place.plane(j)], dx_out.at[t], place.to_plane(j)) for j in others]
    hops = []
    to_both = (place.to_x[0] + place.to_y[0] - place.dp, t)
    for e in range(2):
        mine, got = sm_low.at[e], sm_in.at[e]
        hops.append(
            [
                [links.copy(sm.at[e], sm_core.at[e], place.to_core)],
                [
                    links.copy(mine.at[0], got.at[n], to)
                    for n, to in enumerate((place.to_x, place.to_y, to_both))
                ],
                [links.copy(mine.at[1], got.at[2 + j], place.to_plane(j)) for j in others],
            ]
        )

    def in_order(parts, device):
        total = jnp.zeros_like(parts[0])
        for n in range(len(parts)):
            for part, who in zip(parts, device):
                total = total + jnp.where(who == n, part, 0.0)
        return total

    def hop(e, n):
        arrive(hops[e][n])
        low = lambda k: sm_in[e, k].astype(f32)
        if n == 0:
            sm_low[e, 0] = (sm[e] + sm_core[e]).astype(bf16)
        elif n == 1:
            x, y = place.x, place.y
            near = [2 * y + x, 2 * y + 1 - x, 2 * (1 - y) + x, 2 * (1 - y) + 1 - x]
            parts = [sm_low[e, 0].astype(f32)] + [low(k) for k in range(3)]
            sm_low[e, 1] = in_order(parts, near).astype(bf16)
        else:
            planes_of = [lax.rem(t + planes - j, planes) for j in range(planes)]
            total = in_order([sm_low[e, 1].astype(f32)] + [low(2 + j) for j in others], planes_of)
            small_ref[e * SMALL : (e + 1) * SMALL, :] = total
            return
        start(hops[e][n + 1])

    own_a = [
        keep(0, qkv_in, a_w.at[t, pl.ds(0, 3 * hw)]),
        keep(5, o_in, a_w.at[t, pl.ds(3 * hw, hw)]),
    ]
    own_u, own_d = keep(1, u_in, u_w.at[t]), keep(2, d_in, d_w.at[t])
    load_x, load_c = keep(3, x_in, raw), keep(4, c_in, raw)
    own_y = keep(6, cs.at[t], y_got.at[t])
    leave_y = keep(14, raw, y_out)
    own_dx = keep(7, xs.at[t], dx_out.at[t])

    def p_at(m):
        return p_hbm.at[m]

    p_save = lambda m: keep(12 + m % 2, p2.at[m % 2], p_at(m))

    start([*own_a, load_x, own_u, own_d])
    bias[t] = jnp.zeros(bias.shape[1:], bf16)
    bias[t, 0:1, :] = up_bias[...].astype(f32).reshape(1, hidden).astype(bf16)
    bias[t, 1:2, 0:hw] = qv_bias[0:1, :]
    bias[t, 8:9, 0:hw] = qv_bias[1:2, :]
    place.greet()
    for c in own_a:
        c.wait()
    get_own(0)
    start(b_send)
    own_u.wait()
    get_own(1)
    load_x.wait()
    x_go[...] = jnp.swapaxes(raw[...], 0, 1)
    spread(x_send, 0)
    xs[t] = x_go[t]
    load_c.start()

    tokens = starts_ref.shape[1]

    def token_of(shape, axis):
        n = lax.broadcasted_iota(jnp.int32, shape, axis)
        inside = n % block
        return (n // block) * real + inside - mem, inside

    upto, _ = token_of((tokens, rows), 1)
    begun = lax.broadcasted_iota(jnp.int32, (tokens, rows), 0) <= upto
    begun = jnp.where(begun, 1.0, 0.0).astype(bf16)
    own_starts = starts_ref[pl.ds(t, 1), :].astype(f32).astype(bf16)
    docs = dot(jnp.broadcast_to(own_starts, (8, tokens)), begun)

    def codes(docs, axis):
        token, inside = token_of(docs.shape, axis)
        docs = jnp.where((token < 0) | (token >= tokens), -1.0, docs)
        return jnp.where(inside >= real, -2.0, docs)

    qc = codes(docs, 1)[0:1, :]
    kcodes = codes(docs.T, 0)[:, 0:1]
    for c in range(planes):
        span = slice(c * block, (c + 1) * block)
        kc = kcodes[span, :]
        allowed = ((qc == kc) | (qc < 0) | (kc < 0)) & (kc != -2.0)
        mask[span, :] = jnp.where(allowed, 0.0, NEGATIVE)
    for e in range(2):
        sm[e] = jnp.zeros((SMALL, width), f32)

    get_stage(0, 1)
    get_stage(1, 1)
    spread(x_send, 1)
    get_one(0, 1)
    pl.when(middle)(lambda: get_one(0, 2))
    get_stage(0, 2)
    spread(x_send, 2)
    get_one(1, 1)
    get_two(0, 1)
    pl.when(~middle)(lambda: get_one(0, 2))
    get_stage(0, 3)
    get_stage(1, 2)
    own_d.wait()
    get_own(2)
    get_two(1, 1)
    get_two(0, 2)
    get_one(0, 3)
    get_one(1, 2)
    load_c.wait()
    c_go[...] = jnp.swapaxes(raw[...], 0, 1)
    cs[t] = c_go[t]
    arrive(x_send)
    arrive(b_send)
    afresh = reset_ref[t] > 0
    for c in range(planes):
        x_s[c, 0:real, :] = xs[c]
        x_s[c, real:block, :] = jnp.zeros((block - real, width), bf16)
    last = real - mem
    x_s[0, 0:mem, :] = jnp.where(afresh, init_ref[...], xs[0, 0:mem, :])
    x_s[planes - 1, last:real, :] = jnp.where(afresh, init_ref[...], xs[planes - 1, last:real, :])
    acc[...] = x_s[...].reshape(rows, width).astype(f32) + vec(0)

    forward_pokes = [
        (0, 1, lambda: get_stage(1, 3)),
        (0, 2, lambda: get_two(0, 3)),
        (0, 3, lambda: get_two(1, 2)),
        (1, 0, lambda: get_stage(2, 1)),
        (1, 0, lambda: spread(c_send, 0)),
        (1, 0, lambda: spread(c_send, 1)),
        (1, 1, lambda: get_one(1, 3)),
        (2, 0, lambda: get_one(2, 1)),
        (2, 1, lambda: get_stage(2, 2)),
        (2, 1, lambda: spread(c_send, 2)),
        (2, 2, lambda: get_two(1, 3)),
        (3, 0, lambda: get_two(2, 1)),
        (3, 1, lambda: get_one(2, 2)),
        (3, 2, lambda: get_stage(2, 3)),
    ]

    def poke_at(pokes, *now):
        for *when, poke in pokes:
            hit = now[0] == when[0]
            for a, b in zip(now[1:], when[1:]):
                hit = hit & (a == b)
            pl.when(hit)(poke)

    def forward_order(j):
        picked = t
        for i in others:
            picked = jnp.where(j == i, slot_shard(i), picked)
        return picked

    head_feats = lambda i: pl.ds(pl.multiple_of(i * DH, DH), DH)

    def attention(j):
        s = forward_order(j)
        for i in others:
            pl.when(j == i)(lambda: get_core(0, i))

        poke_at([p for p in forward_pokes if p[1] == 0], j, 0)
        x = x_s[...].reshape(rows, width)
        qkv = dot(a_w[s, 0 : 3 * hw, :], x, NT)
        b = bias[s].astype(f32).T
        bq, bv = b[0:hw, 1:2], b[0:hw, 8:9]
        q = ((qkv[0:hw] + bq).astype(bf16).astype(f32) * (DH**-0.5)).astype(bf16)
        k = qkv[hw : 2 * hw].astype(bf16)
        v = (qkv[2 * hw :] + bv).astype(bf16)
        for i in range(hp):
            feats = slice(i * DH, (i + 1) * DH)
            q_s[s * hp + i], k_s[s * hp + i], v_s[s * hp + i] = q[feats], k[feats], v[feats]

        def head(i):
            h = s * hp + i
            m = j * hp + i
            poke_at([p for p in forward_pokes if p[1] > 0], j, i + 1)
            pl.when(m >= 2)(lambda: p_save(m).wait())
            scores = dot(k_s[h], q_s[h], TN) + mask[...]
            e = jnp.exp(scores - jnp.max(scores, axis=0, keepdims=True))
            p = (e * (1.0 / jnp.sum(e, axis=0, keepdims=True))).astype(bf16)
            p2[m % 2] = p
            o_s[s, head_feats(i), :] = dot(v_s[h], p).astype(bf16)
            keep(12 + m % 2, p2.at[m % 2], p_at(h)).start()

        each(hp, head)
        acc[...] += dot(o_s[s], a_w[s, 3 * hw :, :], TN)

    each(planes, attention)

    def first_norm(c):
        span = pl.ds(pl.multiple_of(c * block, block), block)
        v = acc[span, :]
        v = v - jnp.mean(v, axis=1, keepdims=True)
        rstd = lax.rsqrt(jnp.mean(v * v, axis=1, keepdims=True) + EPSILON)
        xhat = v * rstd
        rstd_s[span, :] = rstd
        xhat_s[span, :] = xhat
        h = xhat * vec(2) + vec(3)
        hb_s[span, :] = h.astype(bf16)
        acc[span, :] = h + vec(1)

    each(planes, first_norm)
    get_one(2, 3)

    def up(j):
        s = forward_order(j)
        for i in others:
            pl.when(j == i)(lambda: get_core(1, i))
        pl.when(j == 0)(lambda: get_two(2, 2))
        for c in range(planes):
            span = pl.ds(c * block, block)
            z = dot(hb_s[span, :], u_w[s]) + bias[s, 0:1, :].astype(f32)
            phi = 0.5 + 0.5 * lax.erf(z * (0.5**0.5))
            act_s[s, span, :] = (z * phi).astype(bf16)
            dz_s[s, span, :] = (phi + z * jnp.exp(-0.5 * z * z) * 0.3989422804014327).astype(bf16)

    each(planes, up)
    get_two(2, 3)

    def down(j):
        s = forward_order(j)
        for i in others:
            pl.when(j == i)(lambda: get_core(2, i))
        acc[...] += dot(act_s[s], d_w[s])

    each(planes, down)
    arrive(c_send)

    zero = jnp.zeros((1, width), f32)

    def second_norm(c, sums):
        span = pl.ds(pl.multiple_of(c * block, block), block)
        v = acc[span, :]
        v = v - jnp.mean(v, axis=1, keepdims=True)
        rstd = lax.rsqrt(jnp.mean(v * v, axis=1, keepdims=True) + EPSILON)
        xhat = v * rstd
        gb_s[span, :] = jnp.zeros((block, width), bf16)
        gb_s[pl.ds(pl.multiple_of(c * block, block), real), :] = cs[c]
        g = gb_s[span, :].astype(f32)
        cs[c] = (xhat * vec(4) + vec(5)).astype(bf16)[0:real]
        d = g * vec(4)
        g2 = rstd * (
            d
            - jnp.mean(d, axis=1, keepdims=True)
            - xhat * jnp.mean(d * xhat, axis=1, keepdims=True)
        )
        acc[span, :] = g2
        gb_s[span, :] = g2.astype(bf16)
        return sums[0] + add_up(g * xhat), sums[1] + add_up(g), sums[2] + add_up(g2)

    sums = lax.fori_loop(0, planes, second_norm, (zero, zero, zero))
    sm[0, 0:3, :] = jnp.concatenate(list(sums), axis=0)
    start(y_send)
    own_y.start()

    down_pokes = [
        (3, lambda: part_core(2, 0)),
    ]
    up_pokes = [
        (0, lambda: part_core(2, 1)),
        (1, lambda: part_core(2, 2)),
        (2, lambda: part_pair(2, 0)),
        (2, lambda: part_core(2, 3)),
        (3, lambda: part_core(1, 0)),
        (3, lambda: part_pair(2, 1)),
        (3, lambda: part_core(1, 1)),
    ]

    def back_down(n):
        s = back_shard(n)
        poke_at(down_pokes, n)
        du = dot(gb_s[...], d_w[s], NT)
        dz_s[s] = (du * dz_s[s].astype(f32)).astype(bf16)
        d_w[s] = dot(act_s[s], gb_s[...], TN).astype(bf16)
        for k in range(planes):
            pl.when(n == k)(ways[2].core[k][0].start)

    release(2)
    each(planes, back_down)

    def back_up(n):
        s = back_shard(n)
        poke_at(up_pokes, n)
        dz = dz_s[s]
        sm[0, pl.ds(6 + s, 1), :] = add_up(dz.astype(f32))
        acc[...] += dot(dz, u_w[s], NT)
        u_w[s] = dot(hb_s[...], dz, TN).astype(bf16)
        for k in range(planes):
            pl.when(n == k)(ways[1].core[k][0].start)

    release(1)
    each(planes, back_up)
    for m in (heads - 2, heads - 1):
        p_save(m).wait()

    p_load = lambda m: keep(
        12 + m % 2, p_at(back_shard(m // hp) * hp + m % hp), p2.at[m % 2]
    )
    p_load(0).start()

    part_pair(2, 2)
    part_core(1, 2)

    def back_first_norm(c, sums):
        span = pl.ds(pl.multiple_of(c * block, block), block)
        xhat = xhat_s[span, :]
        g = acc[span, :]
        d = g * vec(2)
        g1 = rstd_s[span, :] * (
            d
            - jnp.mean(d, axis=1, keepdims=True)
            - xhat * jnp.mean(d * xhat, axis=1, keepdims=True)
        )
        acc[span, :] = g1
        gb_s[span, :] = g1.astype(bf16)
        return sums[0] + add_up(g * xhat), sums[1] + add_up(g), sums[2] + add_up(g1)

    sums = lax.fori_loop(0, planes, back_first_norm, (zero, zero, zero))
    sm[0, 3:6, :] = jnp.concatenate(list(sums), axis=0)
    start(hops[0][0])
    back_pokes = [
        (0, 0, lambda: part_one(2, 0)),
        (0, 1, lambda: part_core(1, 3)),
        (0, 2, lambda: hop(0, 0)),
        (0, 2, lambda: part_pair(2, 3)),
        (0, 4, lambda: part_pair(1, 0)),
        (1, 0, lambda: part_one(2, 1)),
        (1, 3, lambda: part_pair(1, 1)),
        (1, 3, lambda: part_core(0, 0)),
        (1, 3, lambda: part_one(2, 2)),
        (2, 0, lambda: part_pair(1, 2)),
        (2, 3, lambda: part_pair(1, 3)),
        (2, 3, lambda: hop(0, 1)),
        (2, 3, lambda: part_core(0, 1)),
        (2, 4, lambda: part_one(2, 3)),
        (2, 4, lambda: after_z(2)),
        (3, 0, lambda: part_one(1, 0)),
        (3, 1, lambda: part_one(1, 1)),
        (3, 3, lambda: part_core(0, 2)),
        (3, 3, lambda: part_pair(0, 0)),
        (3, 4, lambda: part_one(1, 2)),
    ]

    def back_attention(n):
        s = back_shard(n)
        poke_at([p for p in back_pokes if p[1] == 0], n, 0)
        do = dot(a_w[s, 3 * hw :, :], gb_s[...], NT).astype(bf16)
        do_s[...] = do
        prod = do.astype(f32) * o_s[s].astype(f32)
        for i in range(hp):
            delta_s[i] = add_up(prod[i * DH : (i + 1) * DH])

        def head(i):
            h = s * hp + i
            m = n * hp + i
            p_load(m).wait()
            pl.when(m + 1 < heads)(lambda: p_load(m + 1).start())
            poke_at([p for p in back_pokes if 0 < p[1] < 4], n, i + 1)
            slot = m % 2
            p, do = p2[slot], do_s[head_feats(i), :]
            dp = dot(v_s[h], do, TN)
            ds = (p.astype(f32) * (dp - delta_s[i])).astype(bf16)
            d_s[head_feats(i), :] = (dot(k_s[h], ds) * (DH**-0.5)).astype(bf16)
            d_s[head_feats(hp + i), :] = dot(q_s[h], ds, NT).astype(bf16)
            d_s[head_feats(2 * hp + i), :] = dot(do, p, NT).astype(bf16)

        each(hp, head)
        poke_at([p for p in back_pokes if p[1] == 4], n, 4)
        dqkv = d_s[...]
        sums = dot(jnp.ones((8, rows), bf16), dqkv, NT)[0:1, :]
        sm[1, pl.ds(10 + s, 1), 0:hw] = sums[:, 0:hw]
        sm[1, pl.ds(10 + s, 1), hw : 2 * hw] = sums[:, 2 * hw :]
        acc[...] += dot(dqkv, a_w[s, 0 : 3 * hw, :], TN)
        a_w[s, 0 : 3 * hw, :] = dot(dqkv, x_s[...].reshape(rows, width)).astype(bf16)
        a_w[s, 3 * hw :, :] = dot(o_s[s], gb_s[...]).astype(bf16)
        for k in range(planes):
            pl.when(n == k)(ways[0].core[k][0].start)

    release(0)
    each(planes, back_attention)

    for c in range(planes):
        xs[c] = acc[c * block : c * block + real, :].astype(bf16)
    part_one(1, 3)
    to_next(dx_send)
    own_dx.start()
    dx_last = (planes - 1) * block + last
    both = acc[0:mem, :] + acc[dx_last : dx_last + mem, :]
    sm[1, 0:mem, :] = jnp.where(afresh, both, 0.0)
    start(hops[1][0])
    arrive(y_send)
    own_y.wait()
    raw[...] = jnp.swapaxes(y_got[...], 0, 1)
    leave_y.start()
    part_pair(0, 1)
    part_core(0, 3)
    hop(1, 0)
    after_back1(2)
    part_pair(0, 2)
    after_z(1)
    part_one(0, 0)
    part_one(0, 1)
    part_pair(0, 3)
    hop(1, 1)
    after_back2(2)
    part_one(0, 2)
    start(dx_send[1:2])
    after_back1(1)
    after_back3(2)
    part_one(0, 3)
    to_middle(dx_send)
    after_z(0)
    after_back2(1)
    after_back1(0)
    after_back2(0)
    after_back3(1)
    hop(0, 2)
    hop(1, 2)
    after_back3(0)

    arrive(dx_send)
    leave_y.wait()
    own_dx.wait()
    for way in ways:
        way.out.wait()
    links.finish()


def layer_call(planes, heads, x_in, c_in, qkv_in, o_in, u_in, d_in, vectors, init, starts, reset):
    real, _, width = x_in.shape
    block = -(-real // 16) * 16
    rows = planes * block
    hp = heads // planes
    hw = hp * DH
    shard = u_in.shape
    hidden = shard[1]
    piece, half = shard[0] // (2 * INNER), shard[0] // 2
    S = jax.ShapeDtypeStruct
    V = pltpu.VMEM
    outs = (
        S(shard, bf16),
        S(shard, bf16),
        S(shard, bf16),
        S((planes, real, width), bf16),
        S((real, planes, width), bf16),
        S((heads, rows, rows), bf16),
        S((2 * SMALL, width), f32),
    )
    any_spec = pl.BlockSpec(memory_space=pl.ANY)
    vmem_spec = pl.BlockSpec(memory_space=pltpu.VMEM)
    return pl.pallas_call(
        functools.partial(layer_kernel, planes, heads, block),
        out_shape=outs,
        in_specs=[any_spec] * 6 + [vmem_spec] * 10 + [pl.BlockSpec(memory_space=pltpu.SMEM)],
        out_specs=[any_spec] * 6 + [vmem_spec],
        scratch_shapes=[
            V((planes, *shard), bf16),
            V((planes, *shard), bf16),
            V((planes, *shard), bf16),
            V((real, planes, width), bf16),
            V((planes, real, width), bf16),
            V((planes, real, width), bf16),
            V((planes, real, width), bf16),
            V((planes, real, width), bf16),
            V((planes, real, width), bf16),
            V((planes, block, width), bf16),
            V((planes, 16, hidden), bf16),
            V((heads, DH, rows), bf16),
            V((heads, DH, rows), bf16),
            V((heads, DH, rows), bf16),
            V((2, rows, rows), bf16),
            V((planes, hw, rows), bf16),
            V((hw, rows), bf16),
            V((hp, 1, rows), f32),
            V((3 * hw, rows), bf16),
            V((rows, rows), f32),
            V((rows, width), f32),
            V((rows, width), f32),
            V((rows, 1), f32),
            V((rows, width), bf16),
            V((planes, rows, hidden), bf16),
            V((planes, rows, hidden), bf16),
            V((rows, width), bf16),
            V((3, planes, half, hidden), bf16),
            V((3, 2, planes, 2 * piece, hidden), bf16),
            V((3, 2, planes, piece, hidden), bf16),
            V((3, planes - 1, 2, piece, hidden), bf16),
            V((2, SMALL, width), f32),
            V((2, SMALL, width), f32),
            V((2, 2, SMALL, width), bf16),
            V((2, 2 + planes, SMALL, width), bf16),
            pltpu.SemaphoreType.DMA((LINKS,)),
            pltpu.SemaphoreType.DMA((LINKS,)),
            pltpu.SemaphoreType.DMA((3, planes, 2)),
            pltpu.SemaphoreType.DMA((LOCALS,)),
        ],
        compiler_params=pltpu.CompilerParams(
            collective_id=0, has_side_effects=True, vmem_limit_bytes=63 * MIB
        ),
    )(x_in, c_in, qkv_in, o_in, u_in, d_in, *vectors, init, starts, reset)


STEPS = 2


def finish_kernel(
    planes,
    mem,
    qkv_in,
    o_in,
    u_in,
    d_in,
    dx_in,
    small_in,
    reset_ref,
    y_in,
    qkv_out,
    o_out,
    u_out,
    d_out,
    qv_out,
    mem_out,
    dx_out,
    y_out,
    *rest,
):
    sums, (dx_s, y_s, sem) = rest[:-3], rest[-3:]
    step = pl.program_id(0)
    leave = pltpu.make_async_copy(dx_s, dx_out, sem.at[0])
    take_y = pltpu.make_async_copy(y_in, y_s, sem.at[1])
    leave_y = pltpu.make_async_copy(y_s, y_out, sem.at[2])
    real = dx_in.shape[1]
    hw = qv_out.shape[1]

    @pl.when(step == 0)
    def _():
        take_y.start()
        t = lax.axis_index("tensor")
        qv = small_in[pl.ds(SMALL + 10 + t, 1), :]
        qv_out[0:1, :] = qv[:, 0:hw]
        qv_out[1:2, :] = qv[:, hw : 2 * hw]
        mem_out[...] = small_in[SMALL : SMALL + mem, :]
        for k, out in enumerate(sums):
            at = pl.ds(6 + t, 1) if k == 6 else slice(k, k + 1)
            out[...] = small_in[at, :].reshape(out.shape)
        row = lax.broadcasted_iota(jnp.int32, dx_in.shape[1:], 0)
        memory = ((t == 0) & (row < mem)) | ((t == planes - 1) & (row >= real - mem))
        kept = [
            jnp.where(memory & (reset_ref[k] > 0), 0.0, dx_in[k].astype(f32))[None]
            for k in range(dx_in.shape[0])
        ]
        dx_s[...] = jnp.swapaxes(jnp.concatenate(kept, 0), 0, 1)
        leave.start()
        take_y.wait()
        leave_y.start()

    for ins, outs in ((qkv_in, qkv_out), (o_in, o_out), (u_in, u_out), (d_in, d_out)):
        outs[...] = ins[...].astype(f32)

    @pl.when(step == STEPS - 1)
    def _():
        leave.wait()
        leave_y.wait()


def finish_call(planes, mem, qkv_rows, ga, gu, gd, dx, small, reset, y):
    rows, width = ga.shape
    o_rows = rows - qkv_rows
    S = jax.ShapeDtypeStruct
    segs, real, _ = dx.shape
    whole = lambda *shape: pl.BlockSpec(shape, lambda i: (0,) * len(shape))
    part = lambda size, first=0: pl.BlockSpec(
        (size // STEPS, width), lambda i: (first // (size // STEPS) + i, 0)
    )
    return pl.pallas_call(
        functools.partial(finish_kernel, planes, mem),
        grid=(STEPS,),
        out_shape=(
            S((qkv_rows, width), f32),
            S((o_rows, width), f32),
            S(gu.shape, f32),
            S(gd.shape, f32),
            S((2, o_rows), f32),
            S((mem, width), f32),
            S((real, segs, width), f32),
            S(y.shape, y.dtype),
            *[S((width,), f32)] * 7,
        ),
        in_specs=[
            part(qkv_rows),
            part(o_rows, qkv_rows),
            part(rows),
            part(rows),
            whole(*dx.shape),
            whole(*small.shape),
            pl.BlockSpec(memory_space=pltpu.SMEM),
            pl.BlockSpec(memory_space=pl.ANY),
        ],
        out_specs=[
            part(qkv_rows),
            part(o_rows),
            part(rows),
            part(rows),
            whole(2, o_rows),
            whole(mem, width),
            pl.BlockSpec(memory_space=pl.ANY),
            pl.BlockSpec(memory_space=pl.ANY),
            *[whole(width)] * 7,
        ],
        scratch_shapes=[
            pltpu.VMEM((real, segs, width), f32),
            pltpu.VMEM(y.shape, y.dtype),
            pltpu.SemaphoreType.DMA((3,)),
        ],
        compiler_params=pltpu.CompilerParams(vmem_limit_bytes=63 * MIB),
    )(ga, ga, gu, gd, dx, small, reset, y)


def shards(
    dp_size,
    planes,
    sequence,
    query_key_value_weight,
    qv_bias,
    output_weight,
    out_bias,
    up_weight,
    up_bias,
    down_weight,
    back_bias,
    gain_one,
    shift_one,
    gain_two,
    shift_two,
    init_memory,
    reset,
    starts,
    cotangent,
):
    segs, local_rows, width = sequence.shape
    mem = init_memory.shape[0]
    tokens = starts.shape[1]
    hw = query_key_value_weight.shape[2]
    heads = hw * planes // DH
    assert segs == planes == 4 and 4 * hw == up_weight.shape[1] and mem <= local_rows and dp_size % INNER == 0
    qkv_in = query_key_value_weight.transpose(1, 2, 0).reshape(3 * hw, width)
    ga, gu, gd, dx, y, _, small = layer_call(
        planes,
        heads,
        jnp.swapaxes(sequence, 0, 1),
        jnp.swapaxes(cotangent, 0, 1),
        qkv_in,
        output_weight,
        up_weight,
        down_weight,
        (up_bias, qv_bias, out_bias, back_bias, gain_one, shift_one, gain_two, shift_two),
        init_memory,
        starts,
        reset,
    )

    if dp_size > INNER:
        groups = [[o * INNER + i for o in range(dp_size // INNER)] for i in range(INNER)]
        ga, gu, gd, small = lax.psum(
            (ga.astype(f32), gu.astype(f32), gd.astype(f32), small),
            "dp",
            axis_index_groups=groups,
        )
    g_qkv, g_o, g_u, g_d, g_qv, g_mem, input_grad, y, *sums = finish_call(
        planes, mem, 3 * hw, ga, gu, gd, dx, small, reset, y
    )
    return (
        jnp.swapaxes(y, 0, 1),
        jnp.swapaxes(input_grad, 0, 1),
        g_qkv.reshape(3, hw, width).transpose(2, 0, 1),
        g_qv,
        g_o,
        sums[5],
        g_u,
        sums[6],
        g_d,
        sums[2],
        sums[3],
        sums[4],
        sums[0],
        sums[1],
        g_mem,
    )


def solution(mesh):
    in_specs = (
        P("dp", "tensor", None),
        P(None, None, "tensor"),
        P(None, "tensor"),
        P("tensor", None),
        P(),
        P(None, "tensor"),
        P("tensor"),
        P("tensor", None),
        P(),
        P(),
        P(),
        P(),
        P(),
        P(),
        P("dp"),
        P("dp", None),
        P("dp", "tensor", None),
    )
    out_specs = (
        P("dp", "tensor", None),
        P("dp", "tensor", None),
        P(None, None, "tensor"),
        P(None, "tensor"),
        P("tensor", None),
        P(),
        P(None, "tensor"),
        P("tensor"),
        P("tensor", None),
        P(),
        P(),
        P(),
        P(),
        P(),
        P(),
    )
    return jax.shard_map(
        functools.partial(shards, mesh.shape["dp"], mesh.shape["tensor"]),
        mesh=mesh,
        in_specs=in_specs,
        out_specs=out_specs,
        check_vma=False,
    )
```

```python
import functools

import jax
import jax.numpy as jnp
from jax import lax
from jax.experimental import pallas as pl
from jax.experimental.pallas import tpu as pltpu
from jax.sharding import PartitionSpec as P

DH = 64
NEGATIVE = -1e30
EPSILON = 1e-05
INNER = 8
MIB = 1 << 20

f32 = jnp.float32
bf16 = jnp.bfloat16
NN = (((1,), (0,)), ((), ()))
NT = (((1,), (1,)), ((), ()))
TN = (((0,), (0,)), ((), ()))
MESH = pl.DeviceIdType.MESH


def dot(a, b, dims=NN):
    return lax.dot_general(a, b, dims, preferred_element_type=f32)


def each(count, body):
    def step(i, carry):
        body(i)
        return carry

    lax.fori_loop(0, count, step, 0)


class Place:
    def __init__(self, planes):
        self.planes = planes
        self.dp = lax.axis_index("dp")
        self.t = lax.axis_index("tensor")
        self.core = self.dp % 2
        self.x = (self.dp // 2) % 2
        self.y = (self.dp // 4) % 2
        self.to_core = (self.dp + 1 - 2 * self.core, self.t)
        self.to_x = (self.dp + 2 - 4 * self.x, self.t)
        self.to_y = (self.dp + 4 - 8 * self.y, self.t)

    def plane(self, j):
        return lax.rem(self.t + j, self.planes)

    def to_plane(self, j):
        return (self.dp, self.plane(j))

    def partners(self):
        both = (self.to_x[0] + self.to_y[0] - self.dp, self.t)
        return [self.to_core, self.to_x, self.to_y, both] + [
            self.to_plane(j) for j in range(1, self.planes)
        ]

    def greet(self):
        for device in self.partners():
            pl.semaphore_signal(
                pltpu.get_barrier_semaphore(), inc=1, device_id=device, device_id_type=MESH
            )

    def all_here(self):
        pl.semaphore_wait(pltpu.get_barrier_semaphore(), len(self.partners()))


class Rows:
    def __init__(self, place, rows):
        self.piece = rows // (2 * INNER)
        self.half = rows // 2
        quarter = rows // 4
        core, x, y = place.core, place.x, place.y
        at = lambda n: pl.multiple_of(n, 16)
        base = core * self.half
        self.mine = at(base)
        self.others = at((1 - core) * self.half)
        self.a = at(base + (2 * y + x) * self.piece)
        self.b = at(base + quarter + (2 * x + y) * self.piece)
        self.a_pair = at(base + 2 * y * self.piece)
        self.b_pair = at(base + quarter + 2 * x * self.piece)
        self.a_far_pair = at(base + 2 * (1 - y) * self.piece)
        self.b_far_pair = at(base + quarter + 2 * (1 - x) * self.piece)
        self.a_far = at(base + (2 * y + 1 - x) * self.piece)
        self.b_far = at(base + quarter + (2 * x + 1 - y) * self.piece)


class Links:
    def __init__(self, send, recv):
        self.send, self.recv, self.count, self.all = send, recv, 0, []

    def copy(self, src, dst, device, recv=None, only=None):
        k = self.count
        self.count += 1
        made = pltpu.make_async_remote_copy(
            src_ref=src,
            dst_ref=dst,
            send_sem=self.send.at[k],
            recv_sem=self.recv.at[k] if recv is None else recv,
            device_id=device,
            device_id_type=MESH,
        )
        self.all.append((made, only))
        return made

    def finish(self, copies=None):
        for made, only in list(self.all):
            if copies is None or any(made is c for c in copies):
                self.all = [entry for entry in self.all if entry[0] is not made]
                if only is None:
                    made.wait_send()
                else:
                    pl.when(only)(made.wait_send)


def start(copies):
    for c in copies:
        c.start()


def arrive(copies):
    for c in copies:
        c.wait_recv()


def mirror_end(t, low, planes):
    return t + low * (planes - 1 - 2 * t)


class Way:
    pass


LINKS = 197
LOCALS = 16
SMALL = 16


def layer_kernel(
    planes,
    heads,
    block,
    x_in,
    c_in,
    qkv_in,
    o_in,
    u_in,
    d_in,
    up_bias,
    qv_bias,
    out_bias,
    back_bias,
    gain_one,
    shift_one,
    gain_two,
    shift_two,
    init_ref,
    starts_ref,
    reset_ref,
    ga_out,
    gu_out,
    gd_out,
    dx_out,
    y_out,
    p_hbm,
    small_ref,
    a_w,
    u_w,
    d_w,
    raw,
    x_go,
    c_go,
    y_got,
    xs,
    cs,
    x_s,
    bias,
    q_s,
    k_s,
    v_s,
    p2,
    o_s,
    do_s,
    delta_s,
    d_s,
    mask,
    acc,
    xhat_s,
    rstd_s,
    hb_s,
    act_s,
    dz_s,
    gb_s,
    half_in,
    pair_in,
    one_in,
    z_in,
    sm,
    sm_core,
    sm_low,
    sm_in,
    send,
    recv,
    recv_z,
    local,
):
    place = Place(planes)
    t = place.t
    others = range(1, planes)
    real, width = xs.shape[1:]
    rows = planes * block
    mem = init_ref.shape[0]
    hidden = u_w.shape[2]
    hp = heads // planes
    hw = hp * DH
    links = Links(send, recv)
    r = Rows(place, a_w.shape[1])
    piece, half = r.piece, r.half
    vectors = (out_bias, back_bias, gain_one, shift_one, gain_two, shift_two)
    vec = lambda i: vectors[i][...].astype(f32).reshape(1, width)
    add_up = lambda v: jnp.sum(v, axis=0, keepdims=True)

    def keep(k, src, dst):
        return pltpu.make_async_copy(src, dst, local.at[k])

    weights, g_outs = (a_w, u_w, d_w), (ga_out, gu_out, gd_out)

    low = t // 2
    middle = mirror_end(t, low, planes) == 1
    mirror = lambda n: n + low * (planes - 1 - 2 * n)

    def slot_shard(i):
        return mirror(i - mirror(t) if i == 1 else i)

    def neighbour(to):
        inside = (to >= 0) & (to < planes)
        return (place.dp, lax.rem(to + planes, planes)), inside

    gather = []
    for w in range(3):
        way = Way()
        way.own, way.z, way.one, way.two, way.core = [], [], [], [], []
        for step in (1, -1):
            device, inside = neighbour(t + step)
            way.own.append(
                (
                    inside,
                    [
                        links.copy(
                            weights[w].at[t, pl.ds(at, piece)],
                            weights[w].at[t, pl.ds(at, piece)],
                            device,
                            recv_z.at[w, t, n],
                            inside,
                        )
                        for n, at in enumerate((r.a, r.b))
                    ],
                )
            )
        for i in others:
            s = slot_shard(i)
            below = (t - s + planes - 1) // planes
            device, inside = neighbour(t + 2 * below - 1)
            here = lambda at, size: weights[w].at[s, pl.ds(at, size)]
            same = lambda at, size, to: links.copy(here(at, size), here(at, size), to)
            way.z.append(
                (
                    inside,
                    [
                        links.copy(
                            here(at, piece), here(at, piece), device, recv_z.at[w, s, n], inside
                        )
                        for n, at in enumerate((r.a, r.b))
                    ],
                )
            )
            way.one.append([same(r.a, piece, place.to_x), same(r.b, piece, place.to_y)])
            way.two.append(
                [same(r.a_pair, 2 * piece, place.to_y), same(r.b_pair, 2 * piece, place.to_x)]
            )
            way.core.append([same(r.mine, half, place.to_core)])
        gather.append(way)

    def when_start(inside, copies):
        pl.when(inside)(lambda: start(copies))

    def get_own(w):
        for inside, copies in gather[w].own:
            when_start(inside, copies)

    def get_z(w, i):
        inside, copies = gather[w].z[i - 1]
        arrive(copies)
        when_start(inside, copies)
        start(gather[w].one[i - 1])

    def get_stage(w, d):
        if d == 1:
            get_z(w, 1)
            pl.when(middle)(lambda: get_z(w, 2))
        elif d == 2:
            pl.when(middle)(lambda: get_z(w, 3))
            pl.when(~middle)(lambda: get_z(w, 2))
        else:
            pl.when(~middle)(lambda: get_z(w, 3))

    def get_one(w, i):
        arrive(gather[w].one[i - 1])
        start(gather[w].two[i - 1])

    def get_two(w, i):
        arrive(gather[w].two[i - 1])
        start(gather[w].core[i - 1])

    def get_core(w, i):
        arrive(gather[w].core[i - 1])

    def release(w):
        way = gather[w]
        links.finish([c for _, z in way.own + way.z for c in z])
        links.finish([c for part in way.one + way.two + way.core for c in part])

    def spread(sends, d):
        def go(plane, *picks):
            pl.when(t == plane)(lambda: start([sends[j - 1] for j in picks]))

        if d == 0:
            go(0, 1, 2, 3)
            go(3, 3, 2, 1)
        elif d == 1:
            go(1, 1, 2)
            go(2, 3, 2)
        else:
            go(1, 3)
            go(2, 1)

    def to_next(sends):
        pl.when((t == 0) | (t == 2))(lambda: start(sends[0:1]))
        pl.when((t == 1) | (t == 3))(lambda: start(sends[2:3]))

    def to_middle(sends):
        pl.when((t == 0) | (t == 2))(lambda: start(sends[2:3]))
        pl.when((t == 1) | (t == 3))(lambda: start(sends[0:1]))

    back_order = (2, 3, 1, 0)
    ways = []
    for w in range(3):
        g = weights[w]
        way = Way()
        way.core, way.pair, way.one, way.z = [], [], [], []
        for i in range(planes):
            j = back_order[i]
            s = place.plane(j)
            cut = lambda at, size: g.at[s, pl.ds(at, size)]
            way.core.append([links.copy(cut(r.others, half), half_in.at[w, i], place.to_core)])
            way.pair.append(
                [
                    links.copy(cut(r.a_far_pair, 2 * piece), pair_in.at[w, 0, i], place.to_y),
                    links.copy(cut(r.b_far_pair, 2 * piece), pair_in.at[w, 1, i], place.to_x),
                ]
            )
            way.one.append(
                [
                    links.copy(cut(r.a_far, piece), one_in.at[w, 0, i], place.to_x),
                    links.copy(cut(r.b_far, piece), one_in.at[w, 1, i], place.to_y),
                ]
            )
            if i + 1 < planes:
                way.z.append(
                    [
                        links.copy(cut(r.a, piece), z_in.at[w, i, 0], place.to_plane(j)),
                        links.copy(cut(r.b, piece), z_in.at[w, i, 1], place.to_plane(j)),
                    ]
                )
        at_home = lambda at: pl.multiple_of(at - r.mine, 16)
        f = half_in.at[w, 0]
        same = lambda at, size, to: links.copy(
            f.at[pl.ds(at_home(at), size)], f.at[pl.ds(at_home(at), size)], to
        )
        way.back1 = [same(r.a, piece, place.to_x), same(r.b, piece, place.to_y)]
        way.back2 = [
            same(r.a_pair, 2 * piece, place.to_y),
            same(r.b_pair, 2 * piece, place.to_x),
        ]
        mine = g_outs[w].at[pl.ds(r.mine, half)]
        way.back3 = [links.copy(f, mine, place.to_core)]
        way.out = keep(8 + w, f, mine)
        ways.append(way)

    def add_rows(g, s, at, size, got):
        def some(n):
            here = pl.multiple_of(n * piece, piece)
            span = pl.ds(pl.multiple_of(at + here, 16), piece)
            more = got[pl.ds(here, piece), :].astype(f32)
            g[s, span, :] = (g[s, span, :].astype(f32) + more).astype(bf16)

        if size == piece:
            some(0)
        else:
            each(size // piece, some)

    def back_shard(n):
        j = 0
        for i in range(planes - 1):
            j = jnp.where(n == i, back_order[i], j)
        return place.plane(j)

    def part_core(w, i):
        arrive(ways[w].core[i])
        add_rows(weights[w], back_shard(i), r.mine, half, half_in.at[w, i])
        start(ways[w].pair[i])

    def part_pair(w, i):
        arrive(ways[w].pair[i])
        s = back_shard(i)
        add_rows(weights[w], s, r.a_pair, 2 * piece, pair_in.at[w, 0, i])
        add_rows(weights[w], s, r.b_pair, 2 * piece, pair_in.at[w, 1, i])
        start(ways[w].one[i])

    def part_one(w, i):
        arrive(ways[w].one[i])
        s = back_shard(i)
        add_rows(weights[w], s, r.a, piece, one_in.at[w, 0, i])
        add_rows(weights[w], s, r.b, piece, one_in.at[w, 1, i])
        if i + 1 < planes:
            start(ways[w].z[i])

    def after_z(w):
        for z in ways[w].z:
            arrive(z)
        for i, at in enumerate((r.a, r.b)):
            v = weights[w][t, pl.ds(at, piece), :].astype(f32)
            for j in others:
                v = v + z_in[w, j - 1, i].astype(f32)
            half_in[w, 0, pl.ds(pl.multiple_of(at - r.mine, 16), piece), :] = v.astype(bf16)
        start(ways[w].back1)

    def after_back1(w):
        arrive(ways[w].back1)
        start(ways[w].back2)

    def after_back2(w):
        arrive(ways[w].back2)
        start(ways[w].back3)
        ways[w].out.start()

    def after_back3(w):
        arrive(ways[w].back3)

    x_send = [links.copy(x_go.at[place.plane(j)], xs.at[t], place.to_plane(j)) for j in others]
    c_send = [links.copy(c_go.at[place.plane(j)], cs.at[t], place.to_plane(j)) for j in others]
    b_send = [links.copy(bias.at[t], bias.at[t], place.to_plane(j)) for j in others]
    y_send = [links.copy(cs.at[place.plane(j)], y_got.at[t], place.to_plane(j)) for j in others]
    dx_send = [links.copy(xs.at[place.plane(j)], dx_out.at[t], place.to_plane(j)) for j in others]
    hops = []
    to_both = (place.to_x[0] + place.to_y[0] - place.dp, t)
    for e in range(2):
        mine, got = sm_low.at[e], sm_in.at[e]
        hops.append(
            [
                [links.copy(sm.at[e], sm_core.at[e], place.to_core)],
                [
                    links.copy(mine.at[0], got.at[n], to)
                    for n, to in enumerate((place.to_x, place.to_y, to_both))
                ],
                [links.copy(mine.at[1], got.at[2 + j], place.to_plane(j)) for j in others],
            ]
        )

    def in_order(parts, device):
        total = jnp.zeros_like(parts[0])
        for n in range(len(parts)):
            for part, who in zip(parts, device):
                total = total + jnp.where(who == n, part, 0.0)
        return total

    def hop(e, n):
        arrive(hops[e][n])
        low = lambda k: sm_in[e, k].astype(f32)
        if n == 0:
            sm_low[e, 0] = (sm[e] + sm_core[e]).astype(bf16)
        elif n == 1:
            x, y = place.x, place.y
            near = [2 * y + x, 2 * y + 1 - x, 2 * (1 - y) + x, 2 * (1 - y) + 1 - x]
            parts = [sm_low[e, 0].astype(f32)] + [low(k) for k in range(3)]
            sm_low[e, 1] = in_order(parts, near).astype(bf16)
        else:
            planes_of = [lax.rem(t + planes - j, planes) for j in range(planes)]
            total = in_order([sm_low[e, 1].astype(f32)] + [low(2 + j) for j in others], planes_of)
            small_ref[e * SMALL : (e + 1) * SMALL, :] = total
            return
        start(hops[e][n + 1])

    own_a = [
        keep(0, qkv_in, a_w.at[t, pl.ds(0, 3 * hw)]),
        keep(5, o_in, a_w.at[t, pl.ds(3 * hw, hw)]),
    ]
    own_u, own_d = keep(1, u_in, u_w.at[t]), keep(2, d_in, d_w.at[t])
    load_x, load_c = keep(3, x_in, raw), keep(4, c_in, raw)
    own_y = keep(6, cs.at[t], y_got.at[t])
    leave_y = keep(14, raw, y_out)
    own_dx = keep(7, xs.at[t], dx_out.at[t])

    def p_at(m):
        return p_hbm.at[m]

    p_save = lambda m: keep(12 + m % 2, p2.at[m % 2], p_at(m))

    place.greet()
    start([*own_a, load_x, own_u, own_d])
    bias[t] = jnp.zeros(bias.shape[1:], bf16)
    bias[t, 0:1, :] = up_bias[...].astype(f32).reshape(1, hidden).astype(bf16)
    bias[t, 1:2, 0:hw] = qv_bias[0:1, :]
    bias[t, 8:9, 0:hw] = qv_bias[1:2, :]
    place.all_here()
    for c in own_a:
        c.wait()
    get_own(0)
    start(b_send)
    own_u.wait()
    get_own(1)
    load_x.wait()
    x_go[...] = jnp.swapaxes(raw[...], 0, 1)
    spread(x_send, 0)
    xs[t] = x_go[t]
    load_c.start()

    tokens = starts_ref.shape[1]

    def token_of(shape, axis):
        n = lax.broadcasted_iota(jnp.int32, shape, axis)
        inside = n % block
        return (n // block) * real + inside - mem, inside

    upto, _ = token_of((tokens, rows), 1)
    begun = lax.broadcasted_iota(jnp.int32, (tokens, rows), 0) <= upto
    begun = jnp.where(begun, 1.0, 0.0).astype(bf16)
    own_starts = starts_ref[pl.ds(t, 1), :].astype(f32).astype(bf16)
    docs = dot(jnp.broadcast_to(own_starts, (8, tokens)), begun)

    def codes(docs, axis):
        token, inside = token_of(docs.shape, axis)
        docs = jnp.where((token < 0) | (token >= tokens), -1.0, docs)
        return jnp.where(inside >= real, -2.0, docs)

    qc = codes(docs, 1)[0:1, :]
    kcodes = codes(docs.T, 0)[:, 0:1]
    for c in range(planes):
        span = slice(c * block, (c + 1) * block)
        kc = kcodes[span, :]
        allowed = ((qc == kc) | (qc < 0) | (kc < 0)) & (kc != -2.0)
        mask[span, :] = jnp.where(allowed, 0.0, NEGATIVE)
    for e in range(2):
        sm[e] = jnp.zeros((SMALL, width), f32)

    get_stage(0, 1)
    get_stage(1, 1)
    spread(x_send, 1)
    get_one(0, 1)
    pl.when(middle)(lambda: get_one(0, 2))
    get_stage(0, 2)
    spread(x_send, 2)
    get_one(1, 1)
    get_two(0, 1)
    pl.when(~middle)(lambda: get_one(0, 2))
    get_stage(0, 3)
    get_stage(1, 2)
    own_d.wait()
    get_own(2)
    get_two(1, 1)
    get_two(0, 2)
    get_one(0, 3)
    get_one(1, 2)
    load_c.wait()
    c_go[...] = jnp.swapaxes(raw[...], 0, 1)
    cs[t] = c_go[t]
    arrive(x_send)
    arrive(b_send)
    afresh = reset_ref[t] > 0
    for c in range(planes):
        x_s[c, 0:real, :] = xs[c]
        x_s[c, real:block, :] = jnp.zeros((block - real, width), bf16)
    last = real - mem
    x_s[0, 0:mem, :] = jnp.where(afresh, init_ref[...], xs[0, 0:mem, :])
    x_s[planes - 1, last:real, :] = jnp.where(afresh, init_ref[...], xs[planes - 1, last:real, :])
    acc[...] = x_s[...].reshape(rows, width).astype(f32) + vec(0)

    forward_pokes = [
        (0, 1, lambda: get_stage(1, 3)),
        (0, 2, lambda: get_two(0, 3)),
        (0, 3, lambda: get_two(1, 2)),
        (1, 0, lambda: get_stage(2, 1)),
        (1, 0, lambda: spread(c_send, 0)),
        (1, 0, lambda: spread(c_send, 1)),
        (1, 1, lambda: get_one(1, 3)),
        (2, 0, lambda: get_one(2, 1)),
        (2, 1, lambda: get_stage(2, 2)),
        (2, 1, lambda: spread(c_send, 2)),
        (2, 2, lambda: get_two(1, 3)),
        (3, 0, lambda: get_two(2, 1)),
        (3, 1, lambda: get_one(2, 2)),
        (3, 2, lambda: get_stage(2, 3)),
    ]

    def poke_at(pokes, *now):
        for *when, poke in pokes:
            hit = now[0] == when[0]
            for a, b in zip(now[1:], when[1:]):
                hit = hit & (a == b)
            pl.when(hit)(poke)

    def forward_order(j):
        picked = t
        for i in others:
            picked = jnp.where(j == i, slot_shard(i), picked)
        return picked

    head_feats = lambda i: pl.ds(pl.multiple_of(i * DH, DH), DH)

    def attention(j):
        s = forward_order(j)
        for i in others:
            pl.when(j == i)(lambda: get_core(0, i))

        poke_at([p for p in forward_pokes if p[1] == 0], j, 0)
        x = x_s[...].reshape(rows, width)
        qkv = dot(a_w[s, 0 : 3 * hw, :], x, NT)
        b = bias[s].astype(f32).T
        bq, bv = b[0:hw, 1:2], b[0:hw, 8:9]
        q = ((qkv[0:hw] + bq).astype(bf16).astype(f32) * (DH**-0.5)).astype(bf16)
        k = qkv[hw : 2 * hw].astype(bf16)
        v = (qkv[2 * hw :] + bv).astype(bf16)
        for i in range(hp):
            feats = slice(i * DH, (i + 1) * DH)
            q_s[s * hp + i], k_s[s * hp + i], v_s[s * hp + i] = q[feats], k[feats], v[feats]

        def head(i):
            h = s * hp + i
            m = j * hp + i
            poke_at([p for p in forward_pokes if p[1] > 0], j, i + 1)
            pl.when(m >= 2)(lambda: p_save(m).wait())
            scores = dot(k_s[h], q_s[h], TN) + mask[...]
            e = jnp.exp(scores - jnp.max(scores, axis=0, keepdims=True))
            p = (e * (1.0 / jnp.sum(e, axis=0, keepdims=True))).astype(bf16)
            p2[m % 2] = p
            o_s[s, head_feats(i), :] = dot(v_s[h], p).astype(bf16)
            keep(12 + m % 2, p2.at[m % 2], p_at(h)).start()

        each(hp, head)
        acc[...] += dot(o_s[s], a_w[s, 3 * hw :, :], TN)

    each(planes, attention)

    def first_norm(c):
        span = pl.ds(pl.multiple_of(c * block, block), block)
        v = acc[span, :]
        v = v - jnp.mean(v, axis=1, keepdims=True)
        rstd = lax.rsqrt(jnp.mean(v * v, axis=1, keepdims=True) + EPSILON)
        xhat = v * rstd
        rstd_s[span, :] = rstd
        xhat_s[span, :] = xhat
        h = xhat * vec(2) + vec(3)
        hb_s[span, :] = h.astype(bf16)
        acc[span, :] = h + vec(1)

    each(planes, first_norm)
    get_one(2, 3)

    def up(j):
        s = forward_order(j)
        for i in others:
            pl.when(j == i)(lambda: get_core(1, i))
        pl.when(j == 0)(lambda: get_two(2, 2))
        for c in range(planes):
            span = pl.ds(c * block, block)
            z = dot(hb_s[span, :], u_w[s]) + bias[s, 0:1, :].astype(f32)
            phi = 0.5 + 0.5 * lax.erf(z * (0.5**0.5))
            act_s[s, span, :] = (z * phi).astype(bf16)
            dz_s[s, span, :] = (phi + z * jnp.exp(-0.5 * z * z) * 0.3989422804014327).astype(bf16)

    each(planes, up)
    get_two(2, 3)

    def down(j):
        s = forward_order(j)
        for i in others:
            pl.when(j == i)(lambda: get_core(2, i))
        acc[...] += dot(act_s[s], d_w[s])

    each(planes, down)
    arrive(c_send)

    zero = jnp.zeros((1, width), f32)

    def second_norm(c, sums):
        span = pl.ds(pl.multiple_of(c * block, block), block)
        v = acc[span, :]
        v = v - jnp.mean(v, axis=1, keepdims=True)
        rstd = lax.rsqrt(jnp.mean(v * v, axis=1, keepdims=True) + EPSILON)
        xhat = v * rstd
        gb_s[span, :] = jnp.zeros((block, width), bf16)
        gb_s[pl.ds(pl.multiple_of(c * block, block), real), :] = cs[c]
        g = gb_s[span, :].astype(f32)
        cs[c] = (xhat * vec(4) + vec(5)).astype(bf16)[0:real]
        d = g * vec(4)
        g2 = rstd * (
            d
            - jnp.mean(d, axis=1, keepdims=True)
            - xhat * jnp.mean(d * xhat, axis=1, keepdims=True)
        )
        acc[span, :] = g2
        gb_s[span, :] = g2.astype(bf16)
        return sums[0] + add_up(g * xhat), sums[1] + add_up(g), sums[2] + add_up(g2)

    sums = lax.fori_loop(0, planes, second_norm, (zero, zero, zero))
    sm[0, 0:3, :] = jnp.concatenate(list(sums), axis=0)
    start(y_send)
    own_y.start()

    down_pokes = [
        (3, lambda: part_core(2, 0)),
    ]
    up_pokes = [
        (0, lambda: part_core(2, 1)),
        (1, lambda: part_core(2, 2)),
        (2, lambda: part_pair(2, 0)),
        (2, lambda: part_core(2, 3)),
        (3, lambda: part_core(1, 0)),
        (3, lambda: part_pair(2, 1)),
        (3, lambda: part_core(1, 1)),
    ]

    def back_down(n):
        s = back_shard(n)
        poke_at(down_pokes, n)
        du = dot(gb_s[...], d_w[s], NT)
        dz_s[s] = (du * dz_s[s].astype(f32)).astype(bf16)
        d_w[s] = dot(act_s[s], gb_s[...], TN).astype(bf16)
        for k in range(planes):
            pl.when(n == k)(ways[2].core[k][0].start)

    release(2)
    each(planes, back_down)

    def back_up(n):
        s = back_shard(n)
        poke_at(up_pokes, n)
        dz = dz_s[s]
        sm[0, pl.ds(6 + s, 1), :] = add_up(dz.astype(f32))
        acc[...] += dot(dz, u_w[s], NT)
        u_w[s] = dot(hb_s[...], dz, TN).astype(bf16)
        for k in range(planes):
            pl.when(n == k)(ways[1].core[k][0].start)

    release(1)
    each(planes, back_up)
    for m in (heads - 2, heads - 1):
        p_save(m).wait()

    p_load = lambda m: keep(
        12 + m % 2, p_at(back_shard(m // hp) * hp + m % hp), p2.at[m % 2]
    )
    p_load(0).start()

    part_pair(2, 2)
    part_core(1, 2)

    def back_first_norm(c, sums):
        span = pl.ds(pl.multiple_of(c * block, block), block)
        xhat = xhat_s[span, :]
        g = acc[span, :]
        d = g * vec(2)
        g1 = rstd_s[span, :] * (
            d
            - jnp.mean(d, axis=1, keepdims=True)
            - xhat * jnp.mean(d * xhat, axis=1, keepdims=True)
        )
        acc[span, :] = g1
        gb_s[span, :] = g1.astype(bf16)
        return sums[0] + add_up(g * xhat), sums[1] + add_up(g), sums[2] + add_up(g1)

    sums = lax.fori_loop(0, planes, back_first_norm, (zero, zero, zero))
    sm[0, 3:6, :] = jnp.concatenate(list(sums), axis=0)
    start(hops[0][0])
    back_pokes = [
        (0, 0, lambda: part_one(2, 0)),
        (0, 1, lambda: part_core(1, 3)),
        (0, 2, lambda: hop(0, 0)),
        (0, 2, lambda: part_pair(2, 3)),
        (0, 4, lambda: part_pair(1, 0)),
        (1, 0, lambda: part_one(2, 1)),
        (1, 3, lambda: part_pair(1, 1)),
        (1, 3, lambda: part_core(0, 0)),
        (1, 3, lambda: part_one(2, 2)),
        (2, 0, lambda: part_pair(1, 2)),
        (2, 3, lambda: part_pair(1, 3)),
        (2, 3, lambda: hop(0, 1)),
        (2, 3, lambda: part_core(0, 1)),
        (2, 4, lambda: part_one(2, 3)),
        (3, 0, lambda: part_one(1, 0)),
        (3, 1, lambda: part_one(1, 1)),
        (3, 3, lambda: part_core(0, 2)),
        (3, 3, lambda: part_pair(0, 0)),
        (3, 4, lambda: part_one(1, 2)),
    ]

    def back_attention(n):
        s = back_shard(n)
        poke_at([p for p in back_pokes if p[1] == 0], n, 0)
        do = dot(a_w[s, 3 * hw :, :], gb_s[...], NT).astype(bf16)
        do_s[...] = do
        prod = do.astype(f32) * o_s[s].astype(f32)
        for i in range(hp):
            delta_s[i] = add_up(prod[i * DH : (i + 1) * DH])

        def head(i):
            h = s * hp + i
            m = n * hp + i
            p_load(m).wait()
            pl.when(m + 1 < heads)(lambda: p_load(m + 1).start())
            poke_at([p for p in back_pokes if 0 < p[1] < 4], n, i + 1)
            slot = m % 2
            p, do = p2[slot], do_s[head_feats(i), :]
            dp = dot(v_s[h], do, TN)
            ds = (p.astype(f32) * (dp - delta_s[i])).astype(bf16)
            d_s[head_feats(i), :] = (dot(k_s[h], ds) * (DH**-0.5)).astype(bf16)
            d_s[head_feats(hp + i), :] = dot(q_s[h], ds, NT).astype(bf16)
            d_s[head_feats(2 * hp + i), :] = dot(do, p, NT).astype(bf16)

        each(hp, head)
        poke_at([p for p in back_pokes if p[1] == 4], n, 4)
        dqkv = d_s[...]
        sums = dot(jnp.ones((8, rows), bf16), dqkv, NT)[0:1, :]
        sm[1, pl.ds(10 + s, 1), 0:hw] = sums[:, 0:hw]
        sm[1, pl.ds(10 + s, 1), hw : 2 * hw] = sums[:, 2 * hw :]
        acc[...] += dot(dqkv, a_w[s, 0 : 3 * hw, :], TN)
        a_w[s, 0 : 3 * hw, :] = dot(dqkv, x_s[...].reshape(rows, width)).astype(bf16)
        a_w[s, 3 * hw :, :] = dot(o_s[s], gb_s[...]).astype(bf16)
        for k in range(planes):
            pl.when(n == k)(ways[0].core[k][0].start)

    release(0)
    each(planes, back_attention)

    for c in range(planes):
        xs[c] = acc[c * block : c * block + real, :].astype(bf16)
    part_one(1, 3)
    to_next(dx_send)
    own_dx.start()
    dx_last = (planes - 1) * block + last
    both = acc[0:mem, :] + acc[dx_last : dx_last + mem, :]
    sm[1, 0:mem, :] = jnp.where(afresh, both, 0.0)
    start(hops[1][0])
    arrive(y_send)
    own_y.wait()
    raw[...] = jnp.swapaxes(y_got[...], 0, 1)
    leave_y.start()
    part_pair(0, 1)
    part_core(0, 3)
    hop(1, 0)
    part_pair(0, 2)
    part_one(0, 0)
    part_one(0, 1)
    part_pair(0, 3)
    after_z(2)
    after_z(1)
    part_one(0, 2)
    start(dx_send[1:2])
    hop(1, 1)
    part_one(0, 3)
    to_middle(dx_send)
    after_z(0)
    after_back1(2)
    after_back1(1)
    after_back1(0)
    after_back2(2)
    after_back2(1)
    after_back2(0)
    after_back3(2)
    after_back3(1)
    hop(0, 2)
    hop(1, 2)
    after_back3(0)

    arrive(dx_send)
    leave_y.wait()
    own_dx.wait()
    for way in ways:
        way.out.wait()
    links.finish()


def layer_call(planes, heads, x_in, c_in, qkv_in, o_in, u_in, d_in, vectors, init, starts, reset):
    real, _, width = x_in.shape
    block = -(-real // 16) * 16
    rows = planes * block
    hp = heads // planes
    hw = hp * DH
    shard = u_in.shape
    hidden = shard[1]
    piece, half = shard[0] // (2 * INNER), shard[0] // 2
    S = jax.ShapeDtypeStruct
    V = pltpu.VMEM
    outs = (
        S(shard, bf16),
        S(shard, bf16),
        S(shard, bf16),
        S((planes, real, width), bf16),
        S((real, planes, width), bf16),
        S((heads, rows, rows), bf16),
        S((2 * SMALL, width), f32),
    )
    any_spec = pl.BlockSpec(memory_space=pl.ANY)
    vmem_spec = pl.BlockSpec(memory_space=pltpu.VMEM)
    return pl.pallas_call(
        functools.partial(layer_kernel, planes, heads, block),
        out_shape=outs,
        in_specs=[any_spec] * 6 + [vmem_spec] * 10 + [pl.BlockSpec(memory_space=pltpu.SMEM)],
        out_specs=[any_spec] * 6 + [vmem_spec],
        scratch_shapes=[
            V((planes, *shard), bf16),
            V((planes, *shard), bf16),
            V((planes, *shard), bf16),
            V((real, planes, width), bf16),
            V((planes, real, width), bf16),
            V((planes, real, width), bf16),
            V((planes, real, width), bf16),
            V((planes, real, width), bf16),
            V((planes, real, width), bf16),
            V((planes, block, width), bf16),
            V((planes, 16, hidden), bf16),
            V((heads, DH, rows), bf16),
            V((heads, DH, rows), bf16),
            V((heads, DH, rows), bf16),
            V((2, rows, rows), bf16),
            V((planes, hw, rows), bf16),
            V((hw, rows), bf16),
            V((hp, 1, rows), f32),
            V((3 * hw, rows), bf16),
            V((rows, rows), f32),
            V((rows, width), f32),
            V((rows, width), f32),
            V((rows, 1), f32),
            V((rows, width), bf16),
            V((planes, rows, hidden), bf16),
            V((planes, rows, hidden), bf16),
            V((rows, width), bf16),
            V((3, planes, half, hidden), bf16),
            V((3, 2, planes, 2 * piece, hidden), bf16),
            V((3, 2, planes, piece, hidden), bf16),
            V((3, planes - 1, 2, piece, hidden), bf16),
            V((2, SMALL, width), f32),
            V((2, SMALL, width), f32),
            V((2, 2, SMALL, width), bf16),
            V((2, 2 + planes, SMALL, width), bf16),
            pltpu.SemaphoreType.DMA((LINKS,)),
            pltpu.SemaphoreType.DMA((LINKS,)),
            pltpu.SemaphoreType.DMA((3, planes, 2)),
            pltpu.SemaphoreType.DMA((LOCALS,)),
        ],
        compiler_params=pltpu.CompilerParams(
            collective_id=0, has_side_effects=True, vmem_limit_bytes=63 * MIB
        ),
    )(x_in, c_in, qkv_in, o_in, u_in, d_in, *vectors, init, starts, reset)


STEPS = 2


def finish_kernel(
    planes,
    mem,
    qkv_in,
    o_in,
    u_in,
    d_in,
    dx_in,
    small_in,
    reset_ref,
    y_in,
    qkv_out,
    o_out,
    u_out,
    d_out,
    qv_out,
    mem_out,
    dx_out,
    y_out,
    *rest,
):
    sums, (dx_s, y_s, sem) = rest[:-3], rest[-3:]
    step = pl.program_id(0)
    leave = pltpu.make_async_copy(dx_s, dx_out, sem.at[0])
    take_y = pltpu.make_async_copy(y_in, y_s, sem.at[1])
    leave_y = pltpu.make_async_copy(y_s, y_out, sem.at[2])
    real = dx_in.shape[1]
    hw = qv_out.shape[1]

    @pl.when(step == 0)
    def _():
        take_y.start()
        t = lax.axis_index("tensor")
        qv = small_in[pl.ds(SMALL + 10 + t, 1), :]
        qv_out[0:1, :] = qv[:, 0:hw]
        qv_out[1:2, :] = qv[:, hw : 2 * hw]
        mem_out[...] = small_in[SMALL : SMALL + mem, :]
        for k, out in enumerate(sums):
            at = pl.ds(6 + t, 1) if k == 6 else slice(k, k + 1)
            out[...] = small_in[at, :].reshape(out.shape)
        row = lax.broadcasted_iota(jnp.int32, dx_in.shape[1:], 0)
        memory = ((t == 0) & (row < mem)) | ((t == planes - 1) & (row >= real - mem))
        kept = [
            jnp.where(memory & (reset_ref[k] > 0), 0.0, dx_in[k].astype(f32))[None]
            for k in range(dx_in.shape[0])
        ]
        dx_s[...] = jnp.swapaxes(jnp.concatenate(kept, 0), 0, 1)
        leave.start()
        take_y.wait()
        leave_y.start()

    for ins, outs in ((qkv_in, qkv_out), (o_in, o_out), (u_in, u_out), (d_in, d_out)):
        outs[...] = ins[...].astype(f32)

    @pl.when(step == STEPS - 1)
    def _():
        leave.wait()
        leave_y.wait()


def finish_call(planes, mem, qkv_rows, ga, gu, gd, dx, small, reset, y):
    rows, width = ga.shape
    o_rows = rows - qkv_rows
    S = jax.ShapeDtypeStruct
    segs, real, _ = dx.shape
    whole = lambda *shape: pl.BlockSpec(shape, lambda i: (0,) * len(shape))
    part = lambda size, first=0: pl.BlockSpec(
        (size // STEPS, width), lambda i: (first // (size // STEPS) + i, 0)
    )
    return pl.pallas_call(
        functools.partial(finish_kernel, planes, mem),
        grid=(STEPS,),
        out_shape=(
            S((qkv_rows, width), f32),
            S((o_rows, width), f32),
            S(gu.shape, f32),
            S(gd.shape, f32),
            S((2, o_rows), f32),
            S((mem, width), f32),
            S((real, segs, width), f32),
            S(y.shape, y.dtype),
            *[S((width,), f32)] * 7,
        ),
        in_specs=[
            part(qkv_rows),
            part(o_rows, qkv_rows),
            part(rows),
            part(rows),
            whole(*dx.shape),
            whole(*small.shape),
            pl.BlockSpec(memory_space=pltpu.SMEM),
            pl.BlockSpec(memory_space=pl.ANY),
        ],
        out_specs=[
            part(qkv_rows),
            part(o_rows),
            part(rows),
            part(rows),
            whole(2, o_rows),
            whole(mem, width),
            pl.BlockSpec(memory_space=pl.ANY),
            pl.BlockSpec(memory_space=pl.ANY),
            *[whole(width)] * 7,
        ],
        scratch_shapes=[
            pltpu.VMEM((real, segs, width), f32),
            pltpu.VMEM(y.shape, y.dtype),
            pltpu.SemaphoreType.DMA((3,)),
        ],
        compiler_params=pltpu.CompilerParams(vmem_limit_bytes=63 * MIB),
    )(ga, ga, gu, gd, dx, small, reset, y)


def shards(
    dp_size,
    planes,
    sequence,
    query_key_value_weight,
    qv_bias,
    output_weight,
    out_bias,
    up_weight,
    up_bias,
    down_weight,
    back_bias,
    gain_one,
    shift_one,
    gain_two,
    shift_two,
    init_memory,
    reset,
    starts,
    cotangent,
):
    segs, local_rows, width = sequence.shape
    mem = init_memory.shape[0]
    tokens = starts.shape[1]
    hw = query_key_value_weight.shape[2]
    heads = hw * planes // DH
    assert segs == planes == 4 and 4 * hw == up_weight.shape[1] and mem <= local_rows and dp_size % INNER == 0
    qkv_in = query_key_value_weight.transpose(1, 2, 0).reshape(3 * hw, width)
    ga, gu, gd, dx, y, _, small = layer_call(
        planes,
        heads,
        jnp.swapaxes(sequence, 0, 1),
        jnp.swapaxes(cotangent, 0, 1),
        qkv_in,
        output_weight,
        up_weight,
        down_weight,
        (up_bias, qv_bias, out_bias, back_bias, gain_one, shift_one, gain_two, shift_two),
        init_memory,
        starts,
        reset,
    )

    if dp_size > INNER:
        groups = [[o * INNER + i for o in range(dp_size // INNER)] for i in range(INNER)]
        ga, gu, gd, small = lax.psum(
            (ga.astype(f32), gu.astype(f32), gd.astype(f32), small),
            "dp",
            axis_index_groups=groups,
        )
    g_qkv, g_o, g_u, g_d, g_qv, g_mem, input_grad, y, *sums = finish_call(
        planes, mem, 3 * hw, ga, gu, gd, dx, small, reset, y
    )
    return (
        jnp.swapaxes(y, 0, 1),
        jnp.swapaxes(input_grad, 0, 1),
        g_qkv.reshape(3, hw, width).transpose(2, 0, 1),
        g_qv,
        g_o,
        sums[5],
        g_u,
        sums[6],
        g_d,
        sums[2],
        sums[3],
        sums[4],
        sums[0],
        sums[1],
        g_mem,
    )


def solution(mesh):
    in_specs = (
        P("dp", "tensor", None),
        P(None, None, "tensor"),
        P(None, "tensor"),
        P("tensor", None),
        P(),
        P(None, "tensor"),
        P("tensor"),
        P("tensor", None),
        P(),
        P(),
        P(),
        P(),
        P(),
        P(),
        P("dp"),
        P("dp", None),
        P("dp", "tensor", None),
    )
    out_specs = (
        P("dp", "tensor", None),
        P("dp", "tensor", None),
        P(None, None, "tensor"),
        P(None, "tensor"),
        P("tensor", None),
        P(),
        P(None, "tensor"),
        P("tensor"),
        P("tensor", None),
        P(),
        P(),
        P(),
        P(),
        P(),
        P(),
    )
    return jax.shard_map(
        functools.partial(shards, mesh.shape["dp"], mesh.shape["tensor"]),
        mesh=mesh,
        in_specs=in_specs,
        out_specs=out_specs,
        check_vma=False,
    )
```

```python
import functools

import jax
import jax.numpy as jnp
from jax import lax
from jax.experimental import pallas as pl
from jax.experimental.pallas import tpu as pltpu
from jax.sharding import PartitionSpec as P

DH = 64
NEGATIVE = -1e30
EPSILON = 1e-05
INNER = 8
MIB = 1 << 20

f32 = jnp.float32
bf16 = jnp.bfloat16
NN = (((1,), (0,)), ((), ()))
NT = (((1,), (1,)), ((), ()))
TN = (((0,), (0,)), ((), ()))
MESH = pl.DeviceIdType.MESH


def dot(a, b, dims=NN):
    return lax.dot_general(a, b, dims, preferred_element_type=f32)


def each(count, body):
    def step(i, carry):
        body(i)
        return carry

    lax.fori_loop(0, count, step, 0)


class Place:
    def __init__(self, planes):
        self.planes = planes
        self.dp = lax.axis_index("dp")
        self.t = lax.axis_index("tensor")
        self.core = self.dp % 2
        self.x = (self.dp // 2) % 2
        self.y = (self.dp // 4) % 2
        self.to_core = (self.dp + 1 - 2 * self.core, self.t)
        self.to_x = (self.dp + 2 - 4 * self.x, self.t)
        self.to_y = (self.dp + 4 - 8 * self.y, self.t)

    def plane(self, j):
        return lax.rem(self.t + j, self.planes)

    def to_plane(self, j):
        return (self.dp, self.plane(j))

    def partners(self):
        both = (self.to_x[0] + self.to_y[0] - self.dp, self.t)
        return [self.to_core, self.to_x, self.to_y, both] + [
            self.to_plane(j) for j in range(1, self.planes)
        ]

    def greet(self):
        for device in self.partners():
            pl.semaphore_signal(
                pltpu.get_barrier_semaphore(), inc=1, device_id=device, device_id_type=MESH
            )

    def all_here(self):
        pl.semaphore_wait(pltpu.get_barrier_semaphore(), len(self.partners()))


class Rows:
    def __init__(self, place, rows):
        self.piece = rows // (2 * INNER)
        self.half = rows // 2
        quarter = rows // 4
        core, x, y = place.core, place.x, place.y
        at = lambda n: pl.multiple_of(n, 16)
        base = core * self.half
        self.mine = at(base)
        self.others = at((1 - core) * self.half)
        self.a = at(base + (2 * y + x) * self.piece)
        self.b = at(base + quarter + (2 * x + y) * self.piece)
        self.a_pair = at(base + 2 * y * self.piece)
        self.b_pair = at(base + quarter + 2 * x * self.piece)
        self.a_far_pair = at(base + 2 * (1 - y) * self.piece)
        self.b_far_pair = at(base + quarter + 2 * (1 - x) * self.piece)
        self.a_far = at(base + (2 * y + 1 - x) * self.piece)
        self.b_far = at(base + quarter + (2 * x + 1 - y) * self.piece)


class Links:
    def __init__(self, send, recv):
        self.send, self.recv, self.count, self.all = send, recv, 0, []

    def copy(self, src, dst, device, recv=None, only=None):
        k = self.count
        self.count += 1
        made = pltpu.make_async_remote_copy(
            src_ref=src,
            dst_ref=dst,
            send_sem=self.send.at[k],
            recv_sem=self.recv.at[k] if recv is None else recv,
            device_id=device,
            device_id_type=MESH,
        )
        self.all.append((made, only))
        return made

    def finish(self, copies=None):
        for made, only in list(self.all):
            if copies is None or any(made is c for c in copies):
                self.all = [entry for entry in self.all if entry[0] is not made]
                if only is None:
                    made.wait_send()
                else:
                    pl.when(only)(made.wait_send)


def start(copies):
    for c in copies:
        c.start()


def arrive(copies):
    for c in copies:
        c.wait_recv()


def mirror_end(t, low, planes):
    return t + low * (planes - 1 - 2 * t)


class Way:
    pass


LINKS = 197
LOCALS = 16
SMALL = 16


def layer_kernel(
    planes,
    heads,
    block,
    x_in,
    c_in,
    qkv_in,
    o_in,
    u_in,
    d_in,
    up_bias,
    qv_bias,
    out_bias,
    back_bias,
    gain_one,
    shift_one,
    gain_two,
    shift_two,
    init_ref,
    starts_ref,
    reset_ref,
    ga_out,
    gu_out,
    gd_out,
    dx_out,
    y_out,
    p_hbm,
    small_ref,
    a_w,
    u_w,
    d_w,
    raw,
    x_go,
    c_go,
    y_got,
    xs,
    cs,
    x_s,
    bias,
    q_s,
    k_s,
    v_s,
    p2,
    o_s,
    do_s,
    delta_s,
    d_s,
    mask,
    acc,
    xhat_s,
    rstd_s,
    hb_s,
    act_s,
    dz_s,
    gb_s,
    half_in,
    pair_in,
    one_in,
    z_in,
    sm,
    sm_core,
    sm_low,
    sm_in,
    send,
    recv,
    recv_z,
    local,
):
    place = Place(planes)
    t = place.t
    others = range(1, planes)
    real, width = xs.shape[1:]
    rows = planes * block
    mem = init_ref.shape[0]
    hidden = u_w.shape[2]
    hp = heads // planes
    hw = hp * DH
    links = Links(send, recv)
    r = Rows(place, a_w.shape[1])
    piece, half = r.piece, r.half
    vectors = (out_bias, back_bias, gain_one, shift_one, gain_two, shift_two)
    vec = lambda i: vectors[i][...].astype(f32).reshape(1, width)
    add_up = lambda v: jnp.sum(v, axis=0, keepdims=True)

    def keep(k, src, dst):
        return pltpu.make_async_copy(src, dst, local.at[k])

    weights, g_outs = (a_w, u_w, d_w), (ga_out, gu_out, gd_out)

    low = t // 2
    middle = mirror_end(t, low, planes) == 1
    mirror = lambda n: n + low * (planes - 1 - 2 * n)

    def slot_shard(i):
        return mirror(i - mirror(t) if i == 1 else i)

    def neighbour(to):
        inside = (to >= 0) & (to < planes)
        return (place.dp, lax.rem(to + planes, planes)), inside

    gather = []
    for w in range(3):
        way = Way()
        way.own, way.z, way.one, way.two, way.core = [], [], [], [], []
        for step in (1, -1):
            device, inside = neighbour(t + step)
            way.own.append(
                (
                    inside,
                    [
                        links.copy(
                            weights[w].at[t, pl.ds(at, piece)],
                            weights[w].at[t, pl.ds(at, piece)],
                            device,
                            recv_z.at[w, t, n],
                            inside,
                        )
                        for n, at in enumerate((r.a, r.b))
                    ],
                )
            )
        for i in others:
            s = slot_shard(i)
            below = (t - s + planes - 1) // planes
            device, inside = neighbour(t + 2 * below - 1)
            here = lambda at, size: weights[w].at[s, pl.ds(at, size)]
            same = lambda at, size, to: links.copy(here(at, size), here(at, size), to)
            way.z.append(
                (
                    inside,
                    [
                        links.copy(
                            here(at, piece), here(at, piece), device, recv_z.at[w, s, n], inside
                        )
                        for n, at in enumerate((r.a, r.b))
                    ],
                )
            )
            way.one.append([same(r.a, piece, place.to_x), same(r.b, piece, place.to_y)])
            way.two.append(
                [same(r.a_pair, 2 * piece, place.to_y), same(r.b_pair, 2 * piece, place.to_x)]
            )
            way.core.append([same(r.mine, half, place.to_core)])
        gather.append(way)

    def when_start(inside, copies):
        pl.when(inside)(lambda: start(copies))

    def get_own(w):
        for inside, copies in gather[w].own:
            when_start(inside, copies)

    def get_z(w, i):
        inside, copies = gather[w].z[i - 1]
        arrive(copies)
        when_start(inside, copies)
        start(gather[w].one[i - 1])

    def get_stage(w, d):
        if d == 1:
            get_z(w, 1)
            pl.when(middle)(lambda: get_z(w, 2))
        elif d == 2:
            pl.when(middle)(lambda: get_z(w, 3))
            pl.when(~middle)(lambda: get_z(w, 2))
        else:
            pl.when(~middle)(lambda: get_z(w, 3))

    def get_one(w, i):
        arrive(gather[w].one[i - 1])
        start(gather[w].two[i - 1])

    def get_two(w, i):
        arrive(gather[w].two[i - 1])
        start(gather[w].core[i - 1])

    def get_core(w, i):
        arrive(gather[w].core[i - 1])

    def release(w):
        way = gather[w]
        links.finish([c for _, z in way.own + way.z for c in z])
        links.finish([c for part in way.one + way.two + way.core for c in part])

    def spread(sends, d):
        def go(plane, *picks):
            pl.when(t == plane)(lambda: start([sends[j - 1] for j in picks]))

        if d == 0:
            go(0, 1, 2, 3)
            go(3, 3, 2, 1)
        elif d == 1:
            go(1, 1, 2)
            go(2, 3, 2)
        else:
            go(1, 3)
            go(2, 1)

    def to_next(sends):
        pl.when((t == 0) | (t == 2))(lambda: start(sends[0:1]))
        pl.when((t == 1) | (t == 3))(lambda: start(sends[2:3]))

    def to_middle(sends):
        pl.when((t == 0) | (t == 2))(lambda: start(sends[2:3]))
        pl.when((t == 1) | (t == 3))(lambda: start(sends[0:1]))

    back_order = (2, 3, 1, 0)
    ways = []
    for w in range(3):
        g = weights[w]
        way = Way()
        way.core, way.pair, way.one, way.z = [], [], [], []
        for i in range(planes):
            j = back_order[i]
            s = place.plane(j)
            cut = lambda at, size: g.at[s, pl.ds(at, size)]
            way.core.append([links.copy(cut(r.others, half), half_in.at[w, i], place.to_core)])
            way.pair.append(
                [
                    links.copy(cut(r.a_far_pair, 2 * piece), pair_in.at[w, 0, i], place.to_y),
                    links.copy(cut(r.b_far_pair, 2 * piece), pair_in.at[w, 1, i], place.to_x),
                ]
            )
            way.one.append(
                [
                    links.copy(cut(r.a_far, piece), one_in.at[w, 0, i], place.to_x),
                    links.copy(cut(r.b_far, piece), one_in.at[w, 1, i], place.to_y),
                ]
            )
            if i + 1 < planes:
                way.z.append(
                    [
                        links.copy(cut(r.a, piece), z_in.at[w, i, 0], place.to_plane(j)),
                        links.copy(cut(r.b, piece), z_in.at[w, i, 1], place.to_plane(j)),
                    ]
                )
        at_home = lambda at: pl.multiple_of(at - r.mine, 16)
        f = half_in.at[w, 0]
        same = lambda at, size, to: links.copy(
            f.at[pl.ds(at_home(at), size)], f.at[pl.ds(at_home(at), size)], to
        )
        way.back1 = [same(r.a, piece, place.to_x), same(r.b, piece, place.to_y)]
        way.back2 = [
            same(r.a_pair, 2 * piece, place.to_y),
            same(r.b_pair, 2 * piece, place.to_x),
        ]
        mine = g_outs[w].at[pl.ds(r.mine, half)]
        way.back3 = [links.copy(f, mine, place.to_core)]
        way.out = keep(8 + w, f, mine)
        ways.append(way)

    def add_rows(g, s, at, size, got):
        def some(n):
            here = pl.multiple_of(n * piece, piece)
            span = pl.ds(pl.multiple_of(at + here, 16), piece)
            more = got[pl.ds(here, piece), :].astype(f32)
            g[s, span, :] = (g[s, span, :].astype(f32) + more).astype(bf16)

        if size == piece:
            some(0)
        else:
            each(size // piece, some)

    def back_shard(n):
        j = 0
        for i in range(planes - 1):
            j = jnp.where(n == i, back_order[i], j)
        return place.plane(j)

    def part_core(w, i):
        arrive(ways[w].core[i])
        add_rows(weights[w], back_shard(i), r.mine, half, half_in.at[w, i])
        start(ways[w].pair[i])

    def part_pair(w, i):
        arrive(ways[w].pair[i])
        s = back_shard(i)
        add_rows(weights[w], s, r.a_pair, 2 * piece, pair_in.at[w, 0, i])
        add_rows(weights[w], s, r.b_pair, 2 * piece, pair_in.at[w, 1, i])
        start(ways[w].one[i])

    def part_one(w, i):
        arrive(ways[w].one[i])
        s = back_shard(i)
        add_rows(weights[w], s, r.a, piece, one_in.at[w, 0, i])
        add_rows(weights[w], s, r.b, piece, one_in.at[w, 1, i])
        if i + 1 < planes:
            start(ways[w].z[i])

    def after_z(w):
        for z in ways[w].z:
            arrive(z)
        for i, at in enumerate((r.a, r.b)):
            v = weights[w][t, pl.ds(at, piece), :].astype(f32)
            for j in others:
                v = v + z_in[w, j - 1, i].astype(f32)
            half_in[w, 0, pl.ds(pl.multiple_of(at - r.mine, 16), piece), :] = v.astype(bf16)
        start(ways[w].back1)

    def after_back1(w):
        arrive(ways[w].back1)
        start(ways[w].back2)

    def after_back2(w):
        arrive(ways[w].back2)
        start(ways[w].back3)
        ways[w].out.start()

    def after_back3(w):
        arrive(ways[w].back3)

    x_send = [links.copy(x_go.at[place.plane(j)], xs.at[t], place.to_plane(j)) for j in others]
    c_send = [links.copy(c_go.at[place.plane(j)], cs.at[t], place.to_plane(j)) for j in others]
    b_send = [links.copy(bias.at[t], bias.at[t], place.to_plane(j)) for j in others]
    y_send = [links.copy(cs.at[place.plane(j)], y_got.at[t], place.to_plane(j)) for j in others]
    dx_send = [links.copy(xs.at[place.plane(j)], dx_out.at[t], place.to_plane(j)) for j in others]
    hops = []
    to_both = (place.to_x[0] + place.to_y[0] - place.dp, t)
    for e in range(2):
        mine, got = sm_low.at[e], sm_in.at[e]
        hops.append(
            [
                [links.copy(sm.at[e], sm_core.at[e], place.to_core)],
                [
                    links.copy(mine.at[0], got.at[n], to)
                    for n, to in enumerate((place.to_x, place.to_y, to_both))
                ],
                [links.copy(mine.at[1], got.at[2 + j], place.to_plane(j)) for j in others],
            ]
        )

    def in_order(parts, device):
        total = jnp.zeros_like(parts[0])
        for n in range(len(parts)):
            for part, who in zip(parts, device):
                total = total + jnp.where(who == n, part, 0.0)
        return total

    def hop(e, n):
        arrive(hops[e][n])
        low = lambda k: sm_in[e, k].astype(f32)
        if n == 0:
            sm_low[e, 0] = (sm[e] + sm_core[e]).astype(bf16)
        elif n == 1:
            x, y = place.x, place.y
            near = [2 * y + x, 2 * y + 1 - x, 2 * (1 - y) + x, 2 * (1 - y) + 1 - x]
            parts = [sm_low[e, 0].astype(f32)] + [low(k) for k in range(3)]
            sm_low[e, 1] = in_order(parts, near).astype(bf16)
        else:
            planes_of = [lax.rem(t + planes - j, planes) for j in range(planes)]
            total = in_order([sm_low[e, 1].astype(f32)] + [low(2 + j) for j in others], planes_of)
            small_ref[e * SMALL : (e + 1) * SMALL, :] = total
            return
        start(hops[e][n + 1])

    own_a = [
        keep(0, qkv_in, a_w.at[t, pl.ds(0, 3 * hw)]),
        keep(5, o_in, a_w.at[t, pl.ds(3 * hw, hw)]),
    ]
    own_u, own_d = keep(1, u_in, u_w.at[t]), keep(2, d_in, d_w.at[t])
    load_x, load_c = keep(3, x_in, raw), keep(4, c_in, raw)
    own_y = keep(6, cs.at[t], y_got.at[t])
    leave_y = keep(14, raw, y_out)
    own_dx = keep(7, xs.at[t], dx_out.at[t])

    def p_at(m):
        return p_hbm.at[m]

    p_save = lambda m: keep(12 + m % 2, p2.at[m % 2], p_at(m))

    place.greet()
    start([*own_a, load_x, own_u, own_d])
    bias[t] = jnp.zeros(bias.shape[1:], bf16)
    bias[t, 0:1, :] = up_bias[...].astype(f32).reshape(1, hidden).astype(bf16)
    bias[t, 1:2, 0:hw] = qv_bias[0:1, :]
    bias[t, 8:9, 0:hw] = qv_bias[1:2, :]
    place.all_here()
    for c in own_a:
        c.wait()
    get_own(0)
    start(b_send)
    own_u.wait()
    get_own(1)
    load_x.wait()
    x_go[...] = jnp.swapaxes(raw[...], 0, 1)
    spread(x_send, 0)
    xs[t] = x_go[t]
    load_c.start()

    tokens = starts_ref.shape[1]

    def token_of(shape, axis):
        n = lax.broadcasted_iota(jnp.int32, shape, axis)
        inside = n % block
        return (n // block) * real + inside - mem, inside

    upto, _ = token_of((tokens, rows), 1)
    begun = lax.broadcasted_iota(jnp.int32, (tokens, rows), 0) <= upto
    begun = jnp.where(begun, 1.0, 0.0).astype(bf16)
    own_starts = starts_ref[pl.ds(t, 1), :].astype(f32).astype(bf16)
    docs = dot(jnp.broadcast_to(own_starts, (8, tokens)), begun)

    def codes(docs, axis):
        token, inside = token_of(docs.shape, axis)
        docs = jnp.where((token < 0) | (token >= tokens), -1.0, docs)
        return jnp.where(inside >= real, -2.0, docs)

    qc = codes(docs, 1)[0:1, :]
    kcodes = codes(docs.T, 0)[:, 0:1]
    for c in range(planes):
        span = slice(c * block, (c + 1) * block)
        kc = kcodes[span, :]
        allowed = ((qc == kc) | (qc < 0) | (kc < 0)) & (kc != -2.0)
        mask[span, :] = jnp.where(allowed, 0.0, NEGATIVE)
    for e in range(2):
        sm[e] = jnp.zeros((SMALL, width), f32)

    get_stage(0, 1)
    get_stage(1, 1)
    spread(x_send, 1)
    get_one(0, 1)
    pl.when(middle)(lambda: get_one(0, 2))
    get_stage(0, 2)
    spread(x_send, 2)
    get_one(1, 1)
    get_two(0, 1)
    pl.when(~middle)(lambda: get_one(0, 2))
    get_stage(0, 3)
    get_stage(1, 2)
    own_d.wait()
    get_own(2)
    get_two(1, 1)
    get_two(0, 2)
    get_one(0, 3)
    get_one(1, 2)
    load_c.wait()
    c_go[...] = jnp.swapaxes(raw[...], 0, 1)
    cs[t] = c_go[t]
    arrive(x_send)
    arrive(b_send)
    afresh = reset_ref[t] > 0
    for c in range(planes):
        x_s[c, 0:real, :] = xs[c]
        x_s[c, real:block, :] = jnp.zeros((block - real, width), bf16)
    last = real - mem
    x_s[0, 0:mem, :] = jnp.where(afresh, init_ref[...], xs[0, 0:mem, :])
    x_s[planes - 1, last:real, :] = jnp.where(afresh, init_ref[...], xs[planes - 1, last:real, :])
    acc[...] = x_s[...].reshape(rows, width).astype(f32) + vec(0)

    forward_pokes = [
        (0, 1, lambda: get_stage(1, 3)),
        (0, 2, lambda: get_two(0, 3)),
        (0, 3, lambda: get_two(1, 2)),
        (1, 0, lambda: get_stage(2, 1)),
        (1, 0, lambda: spread(c_send, 0)),
        (1, 0, lambda: spread(c_send, 1)),
        (1, 1, lambda: get_one(1, 3)),
        (2, 0, lambda: get_one(2, 1)),
        (2, 1, lambda: get_stage(2, 2)),
        (2, 1, lambda: spread(c_send, 2)),
        (2, 2, lambda: get_two(1, 3)),
        (3, 0, lambda: get_two(2, 1)),
        (3, 1, lambda: get_one(2, 2)),
        (3, 2, lambda: get_stage(2, 3)),
    ]

    def poke_at(pokes, *now):
        for *when, poke in pokes:
            hit = now[0] == when[0]
            for a, b in zip(now[1:], when[1:]):
                hit = hit & (a == b)
            pl.when(hit)(poke)

    def forward_order(j):
        picked = t
        for i in others:
            picked = jnp.where(j == i, slot_shard(i), picked)
        return picked

    head_feats = lambda i: pl.ds(pl.multiple_of(i * DH, DH), DH)

    def attention(j):
        s = forward_order(j)
        for i in others:
            pl.when(j == i)(lambda: get_core(0, i))

        poke_at([p for p in forward_pokes if p[1] == 0], j, 0)
        x = x_s[...].reshape(rows, width)
        qkv = dot(a_w[s, 0 : 3 * hw, :], x, NT)
        b = bias[s].astype(f32).T
        bq, bv = b[0:hw, 1:2], b[0:hw, 8:9]
        q = ((qkv[0:hw] + bq).astype(bf16).astype(f32) * (DH**-0.5)).astype(bf16)
        k = qkv[hw : 2 * hw].astype(bf16)
        v = (qkv[2 * hw :] + bv).astype(bf16)
        for i in range(hp):
            feats = slice(i * DH, (i + 1) * DH)
            q_s[s * hp + i], k_s[s * hp + i], v_s[s * hp + i] = q[feats], k[feats], v[feats]

        def head(i):
            h = s * hp + i
            m = j * hp + i
            poke_at([p for p in forward_pokes if p[1] > 0], j, i + 1)
            pl.when(m >= 2)(lambda: p_save(m).wait())
            scores = dot(k_s[h], q_s[h], TN) + mask[...]
            e = jnp.exp(scores - jnp.max(scores, axis=0, keepdims=True))
            p = (e * (1.0 / jnp.sum(e, axis=0, keepdims=True))).astype(bf16)
            p2[m % 2] = p
            o_s[s, head_feats(i), :] = dot(v_s[h], p).astype(bf16)
            keep(12 + m % 2, p2.at[m % 2], p_at(h)).start()

        each(hp, head)
        acc[...] += dot(o_s[s], a_w[s, 3 * hw :, :], TN)

    each(planes, attention)

    def first_norm(c):
        span = pl.ds(pl.multiple_of(c * block, block), block)
        v = acc[span, :]
        v = v - jnp.mean(v, axis=1, keepdims=True)
        rstd = lax.rsqrt(jnp.mean(v * v, axis=1, keepdims=True) + EPSILON)
        xhat = v * rstd
        rstd_s[span, :] = rstd
        xhat_s[span, :] = xhat
        h = xhat * vec(2) + vec(3)
        hb_s[span, :] = h.astype(bf16)
        acc[span, :] = h + vec(1)

    each(planes, first_norm)
    get_one(2, 3)

    def up(j):
        s = forward_order(j)
        for i in others:
            pl.when(j == i)(lambda: get_core(1, i))
        pl.when(j == 0)(lambda: get_two(2, 2))
        for c in range(planes):
            span = pl.ds(c * block, block)
            z = dot(hb_s[span, :], u_w[s]) + bias[s, 0:1, :].astype(f32)
            phi = 0.5 + 0.5 * lax.erf(z * (0.5**0.5))
            act_s[s, span, :] = (z * phi).astype(bf16)
            dz_s[s, span, :] = (phi + z * jnp.exp(-0.5 * z * z) * 0.3989422804014327).astype(bf16)

    each(planes, up)
    get_two(2, 3)

    def down(j):
        s = forward_order(j)
        for i in others:
            pl.when(j == i)(lambda: get_core(2, i))
        acc[...] += dot(act_s[s], d_w[s])

    each(planes, down)
    arrive(c_send)

    zero = jnp.zeros((1, width), f32)

    def second_norm(c, sums):
        span = pl.ds(pl.multiple_of(c * block, block), block)
        v = acc[span, :]
        v = v - jnp.mean(v, axis=1, keepdims=True)
        rstd = lax.rsqrt(jnp.mean(v * v, axis=1, keepdims=True) + EPSILON)
        xhat = v * rstd
        gb_s[span, :] = jnp.zeros((block, width), bf16)
        gb_s[pl.ds(pl.multiple_of(c * block, block), real), :] = cs[c]
        g = gb_s[span, :].astype(f32)
        cs[c] = (xhat * vec(4) + vec(5)).astype(bf16)[0:real]
        d = g * vec(4)
        g2 = rstd * (
            d
            - jnp.mean(d, axis=1, keepdims=True)
            - xhat * jnp.mean(d * xhat, axis=1, keepdims=True)
        )
        acc[span, :] = g2
        gb_s[span, :] = g2.astype(bf16)
        return sums[0] + add_up(g * xhat), sums[1] + add_up(g), sums[2] + add_up(g2)

    sums = lax.fori_loop(0, planes, second_norm, (zero, zero, zero))
    sm[0, 0:3, :] = jnp.concatenate(list(sums), axis=0)
    start(y_send)
    own_y.start()

    down_pokes = [
        (3, lambda: part_core(2, 0)),
    ]
    up_pokes = [
        (0, lambda: part_core(2, 1)),
        (1, lambda: part_core(2, 2)),
        (2, lambda: part_pair(2, 0)),
        (2, lambda: part_core(2, 3)),
        (3, lambda: part_core(1, 0)),
        (3, lambda: part_pair(2, 1)),
        (3, lambda: part_core(1, 1)),
    ]

    def back_down(n):
        s = back_shard(n)
        poke_at(down_pokes, n)
        du = dot(gb_s[...], d_w[s], NT)
        dz_s[s] = (du * dz_s[s].astype(f32)).astype(bf16)
        d_w[s] = dot(act_s[s], gb_s[...], TN).astype(bf16)
        for k in range(planes):
            pl.when(n == k)(ways[2].core[k][0].start)

    release(2)
    each(planes, back_down)

    def back_up(n):
        s = back_shard(n)
        poke_at(up_pokes, n)
        dz = dz_s[s]
        sm[0, pl.ds(6 + s, 1), :] = add_up(dz.astype(f32))
        acc[...] += dot(dz, u_w[s], NT)
        u_w[s] = dot(hb_s[...], dz, TN).astype(bf16)
        for k in range(planes):
            pl.when(n == k)(ways[1].core[k][0].start)

    release(1)
    each(planes, back_up)
    for m in (heads - 2, heads - 1):
        p_save(m).wait()

    p_load = lambda m: keep(
        12 + m % 2, p_at(back_shard(m // hp) * hp + m % hp), p2.at[m % 2]
    )
    p_load(0).start()

    part_pair(2, 2)
    part_core(1, 2)

    def back_first_norm(c, sums):
        span = pl.ds(pl.multiple_of(c * block, block), block)
        xhat = xhat_s[span, :]
        g = acc[span, :]
        d = g * vec(2)
        g1 = rstd_s[span, :] * (
            d
            - jnp.mean(d, axis=1, keepdims=True)
            - xhat * jnp.mean(d * xhat, axis=1, keepdims=True)
        )
        acc[span, :] = g1
        gb_s[span, :] = g1.astype(bf16)
        return sums[0] + add_up(g * xhat), sums[1] + add_up(g), sums[2] + add_up(g1)

    sums = lax.fori_loop(0, planes, back_first_norm, (zero, zero, zero))
    sm[0, 3:6, :] = jnp.concatenate(list(sums), axis=0)
    start(hops[0][0])
    back_pokes = [
        (0, 0, lambda: part_one(2, 0)),
        (0, 1, lambda: part_core(1, 3)),
        (0, 2, lambda: hop(0, 0)),
        (0, 2, lambda: part_pair(2, 3)),
        (0, 4, lambda: part_pair(1, 0)),
        (1, 0, lambda: part_one(2, 1)),
        (1, 3, lambda: part_pair(1, 1)),
        (1, 3, lambda: part_core(0, 0)),
        (1, 3, lambda: part_one(2, 2)),
        (2, 0, lambda: part_pair(1, 2)),
        (2, 3, lambda: part_pair(1, 3)),
        (2, 3, lambda: hop(0, 1)),
        (2, 3, lambda: part_core(0, 1)),
        (2, 4, lambda: part_one(2, 3)),
        (3, 0, lambda: part_one(1, 0)),
        (3, 1, lambda: part_one(1, 1)),
        (3, 3, lambda: part_core(0, 2)),
        (3, 3, lambda: part_pair(0, 0)),
        (3, 4, lambda: part_one(1, 2)),
    ]

    def back_attention(n):
        s = back_shard(n)
        poke_at([p for p in back_pokes if p[1] == 0], n, 0)
        do = dot(a_w[s, 3 * hw :, :], gb_s[...], NT).astype(bf16)
        do_s[...] = do
        prod = do.astype(f32) * o_s[s].astype(f32)
        for i in range(hp):
            delta_s[i] = add_up(prod[i * DH : (i + 1) * DH])

        def head(i):
            h = s * hp + i
            m = n * hp + i
            p_load(m).wait()
            pl.when(m + 1 < heads)(lambda: p_load(m + 1).start())
            poke_at([p for p in back_pokes if 0 < p[1] < 4], n, i + 1)
            slot = m % 2
            p, do = p2[slot], do_s[head_feats(i), :]
            dp = dot(v_s[h], do, TN)
            ds = (p.astype(f32) * (dp - delta_s[i])).astype(bf16)
            d_s[head_feats(i), :] = (dot(k_s[h], ds) * (DH**-0.5)).astype(bf16)
            d_s[head_feats(hp + i), :] = dot(q_s[h], ds, NT).astype(bf16)
            d_s[head_feats(2 * hp + i), :] = dot(do, p, NT).astype(bf16)

        each(hp, head)
        poke_at([p for p in back_pokes if p[1] == 4], n, 4)
        dqkv = d_s[...]
        sums = dot(jnp.ones((8, rows), bf16), dqkv, NT)[0:1, :]
        sm[1, pl.ds(10 + s, 1), 0:hw] = sums[:, 0:hw]
        sm[1, pl.ds(10 + s, 1), hw : 2 * hw] = sums[:, 2 * hw :]
        acc[...] += dot(dqkv, a_w[s, 0 : 3 * hw, :], TN)
        a_w[s, 0 : 3 * hw, :] = dot(dqkv, x_s[...].reshape(rows, width)).astype(bf16)
        a_w[s, 3 * hw :, :] = dot(o_s[s], gb_s[...]).astype(bf16)
        for k in range(planes):
            pl.when(n == k)(ways[0].core[k][0].start)

    release(0)
    each(planes, back_attention)

    for c in range(planes):
        xs[c] = acc[c * block : c * block + real, :].astype(bf16)
    part_one(1, 3)
    to_next(dx_send)
    own_dx.start()
    dx_last = (planes - 1) * block + last
    both = acc[0:mem, :] + acc[dx_last : dx_last + mem, :]
    sm[1, 0:mem, :] = jnp.where(afresh, both, 0.0)
    start(hops[1][0])
    arrive(y_send)
    own_y.wait()
    raw[...] = jnp.swapaxes(y_got[...], 0, 1)
    leave_y.start()
    part_pair(0, 1)
    part_core(0, 3)
    hop(1, 0)
    part_pair(0, 2)
    part_one(0, 0)
    part_one(0, 1)
    part_pair(0, 3)
    after_z(2)
    after_z(1)
    part_one(0, 2)
    part_one(0, 3)
    start(dx_send[1:2])
    hop(1, 1)
    to_middle(dx_send)
    after_z(0)
    after_back1(2)
    after_back1(1)
    after_back1(0)
    gone = [*x_send, *c_send, *b_send, *y_send]
    for way in ways:
        gone += [c for part in way.core + way.pair + way.one + way.z for c in part]
    links.finish(gone + ways[2].back1 + ways[1].back1)
    after_back2(2)
    after_back2(1)
    after_back2(0)
    after_back3(2)
    after_back3(1)
    hop(0, 2)
    hop(1, 2)
    after_back3(0)

    arrive(dx_send)
    leave_y.wait()
    own_dx.wait()
    for way in ways:
        way.out.wait()
    links.finish()


def layer_call(planes, heads, x_in, c_in, qkv_in, o_in, u_in, d_in, vectors, init, starts, reset):
    real, _, width = x_in.shape
    block = -(-real // 16) * 16
    rows = planes * block
    hp = heads // planes
    hw = hp * DH
    shard = u_in.shape
    hidden = shard[1]
    piece, half = shard[0] // (2 * INNER), shard[0] // 2
    S = jax.ShapeDtypeStruct
    V = pltpu.VMEM
    outs = (
        S(shard, bf16),
        S(shard, bf16),
        S(shard, bf16),
        S((planes, real, width), bf16),
        S((real, planes, width), bf16),
        S((heads, rows, rows), bf16),
        S((2 * SMALL, width), f32),
    )
    any_spec = pl.BlockSpec(memory_space=pl.ANY)
    vmem_spec = pl.BlockSpec(memory_space=pltpu.VMEM)
    return pl.pallas_call(
        functools.partial(layer_kernel, planes, heads, block),
        out_shape=outs,
        in_specs=[any_spec] * 6 + [vmem_spec] * 10 + [pl.BlockSpec(memory_space=pltpu.SMEM)],
        out_specs=[any_spec] * 6 + [vmem_spec],
        scratch_shapes=[
            V((planes, *shard), bf16),
            V((planes, *shard), bf16),
            V((planes, *shard), bf16),
            V((real, planes, width), bf16),
            V((planes, real, width), bf16),
            V((planes, real, width), bf16),
            V((planes, real, width), bf16),
            V((planes, real, width), bf16),
            V((planes, real, width), bf16),
            V((planes, block, width), bf16),
            V((planes, 16, hidden), bf16),
            V((heads, DH, rows), bf16),
            V((heads, DH, rows), bf16),
            V((heads, DH, rows), bf16),
            V((2, rows, rows), bf16),
            V((planes, hw, rows), bf16),
            V((hw, rows), bf16),
            V((hp, 1, rows), f32),
            V((3 * hw, rows), bf16),
            V((rows, rows), f32),
            V((rows, width), f32),
            V((rows, width), f32),
            V((rows, 1), f32),
            V((rows, width), bf16),
            V((planes, rows, hidden), bf16),
            V((planes, rows, hidden), bf16),
            V((rows, width), bf16),
            V((3, planes, half, hidden), bf16),
            V((3, 2, planes, 2 * piece, hidden), bf16),
            V((3, 2, planes, piece, hidden), bf16),
            V((3, planes - 1, 2, piece, hidden), bf16),
            V((2, SMALL, width), f32),
            V((2, SMALL, width), f32),
            V((2, 2, SMALL, width), bf16),
            V((2, 2 + planes, SMALL, width), bf16),
            pltpu.SemaphoreType.DMA((LINKS,)),
            pltpu.SemaphoreType.DMA((LINKS,)),
            pltpu.SemaphoreType.DMA((3, planes, 2)),
            pltpu.SemaphoreType.DMA((LOCALS,)),
        ],
        compiler_params=pltpu.CompilerParams(
            collective_id=0, has_side_effects=True, vmem_limit_bytes=63 * MIB
        ),
    )(x_in, c_in, qkv_in, o_in, u_in, d_in, *vectors, init, starts, reset)


STEPS = 2


def finish_kernel(
    planes,
    mem,
    qkv_in,
    o_in,
    u_in,
    d_in,
    dx_in,
    small_in,
    reset_ref,
    y_in,
    qkv_out,
    o_out,
    u_out,
    d_out,
    qv_out,
    mem_out,
    dx_out,
    y_out,
    *rest,
):
    sums, (dx_s, y_s, sem) = rest[:-3], rest[-3:]
    step = pl.program_id(0)
    leave = pltpu.make_async_copy(dx_s, dx_out, sem.at[0])
    take_y = pltpu.make_async_copy(y_in, y_s, sem.at[1])
    leave_y = pltpu.make_async_copy(y_s, y_out, sem.at[2])
    real = dx_in.shape[1]
    hw = qv_out.shape[1]

    @pl.when(step == 0)
    def _():
        take_y.start()
        t = lax.axis_index("tensor")
        qv = small_in[pl.ds(SMALL + 10 + t, 1), :]
        qv_out[0:1, :] = qv[:, 0:hw]
        qv_out[1:2, :] = qv[:, hw : 2 * hw]
        mem_out[...] = small_in[SMALL : SMALL + mem, :]
        for k, out in enumerate(sums):
            at = pl.ds(6 + t, 1) if k == 6 else slice(k, k + 1)
            out[...] = small_in[at, :].reshape(out.shape)
        row = lax.broadcasted_iota(jnp.int32, dx_in.shape[1:], 0)
        memory = ((t == 0) & (row < mem)) | ((t == planes - 1) & (row >= real - mem))
        kept = [
            jnp.where(memory & (reset_ref[k] > 0), 0.0, dx_in[k].astype(f32))[None]
            for k in range(dx_in.shape[0])
        ]
        dx_s[...] = jnp.swapaxes(jnp.concatenate(kept, 0), 0, 1)
        leave.start()
        take_y.wait()
        leave_y.start()

    for ins, outs in ((qkv_in, qkv_out), (o_in, o_out), (u_in, u_out), (d_in, d_out)):
        outs[...] = ins[...].astype(f32)

    @pl.when(step == STEPS - 1)
    def _():
        leave.wait()
        leave_y.wait()


def finish_call(planes, mem, qkv_rows, ga, gu, gd, dx, small, reset, y):
    rows, width = ga.shape
    o_rows = rows - qkv_rows
    S = jax.ShapeDtypeStruct
    segs, real, _ = dx.shape
    whole = lambda *shape: pl.BlockSpec(shape, lambda i: (0,) * len(shape))
    part = lambda size, first=0: pl.BlockSpec(
        (size // STEPS, width), lambda i: (first // (size // STEPS) + i, 0)
    )
    return pl.pallas_call(
        functools.partial(finish_kernel, planes, mem),
        grid=(STEPS,),
        out_shape=(
            S((qkv_rows, width), f32),
            S((o_rows, width), f32),
            S(gu.shape, f32),
            S(gd.shape, f32),
            S((2, o_rows), f32),
            S((mem, width), f32),
            S((real, segs, width), f32),
            S(y.shape, y.dtype),
            *[S((width,), f32)] * 7,
        ),
        in_specs=[
            part(qkv_rows),
            part(o_rows, qkv_rows),
            part(rows),
            part(rows),
            whole(*dx.shape),
            whole(*small.shape),
            pl.BlockSpec(memory_space=pltpu.SMEM),
            pl.BlockSpec(memory_space=pl.ANY),
        ],
        out_specs=[
            part(qkv_rows),
            part(o_rows),
            part(rows),
            part(rows),
            whole(2, o_rows),
            whole(mem, width),
            pl.BlockSpec(memory_space=pl.ANY),
            pl.BlockSpec(memory_space=pl.ANY),
            *[whole(width)] * 7,
        ],
        scratch_shapes=[
            pltpu.VMEM((real, segs, width), f32),
            pltpu.VMEM(y.shape, y.dtype),
            pltpu.SemaphoreType.DMA((3,)),
        ],
        compiler_params=pltpu.CompilerParams(vmem_limit_bytes=63 * MIB),
    )(ga, ga, gu, gd, dx, small, reset, y)


def shards(
    dp_size,
    planes,
    sequence,
    query_key_value_weight,
    qv_bias,
    output_weight,
    out_bias,
    up_weight,
    up_bias,
    down_weight,
    back_bias,
    gain_one,
    shift_one,
    gain_two,
    shift_two,
    init_memory,
    reset,
    starts,
    cotangent,
):
    segs, local_rows, width = sequence.shape
    mem = init_memory.shape[0]
    tokens = starts.shape[1]
    hw = query_key_value_weight.shape[2]
    heads = hw * planes // DH
    assert segs == planes == 4 and 4 * hw == up_weight.shape[1] and mem <= local_rows and dp_size % INNER == 0
    qkv_in = query_key_value_weight.transpose(1, 2, 0).reshape(3 * hw, width)
    ga, gu, gd, dx, y, _, small = layer_call(
        planes,
        heads,
        jnp.swapaxes(sequence, 0, 1),
        jnp.swapaxes(cotangent, 0, 1),
        qkv_in,
        output_weight,
        up_weight,
        down_weight,
        (up_bias, qv_bias, out_bias, back_bias, gain_one, shift_one, gain_two, shift_two),
        init_memory,
        starts,
        reset,
    )

    if dp_size > INNER:
        groups = [[o * INNER + i for o in range(dp_size // INNER)] for i in range(INNER)]
        ga, gu, gd, small = lax.psum(
            (ga.astype(f32), gu.astype(f32), gd.astype(f32), small),
            "dp",
            axis_index_groups=groups,
        )
    g_qkv, g_o, g_u, g_d, g_qv, g_mem, input_grad, y, *sums = finish_call(
        planes, mem, 3 * hw, ga, gu, gd, dx, small, reset, y
    )
    return (
        jnp.swapaxes(y, 0, 1),
        jnp.swapaxes(input_grad, 0, 1),
        g_qkv.reshape(3, hw, width).transpose(2, 0, 1),
        g_qv,
        g_o,
        sums[5],
        g_u,
        sums[6],
        g_d,
        sums[2],
        sums[3],
        sums[4],
        sums[0],
        sums[1],
        g_mem,
    )


def solution(mesh):
    in_specs = (
        P("dp", "tensor", None),
        P(None, None, "tensor"),
        P(None, "tensor"),
        P("tensor", None),
        P(),
        P(None, "tensor"),
        P("tensor"),
        P("tensor", None),
        P(),
        P(),
        P(),
        P(),
        P(),
        P(),
        P("dp"),
        P("dp", None),
        P("dp", "tensor", None),
    )
    out_specs = (
        P("dp", "tensor", None),
        P("dp", "tensor", None),
        P(None, None, "tensor"),
        P(None, "tensor"),
        P("tensor", None),
        P(),
        P(None, "tensor"),
        P("tensor"),
        P("tensor", None),
        P(),
        P(),
        P(),
        P(),
        P(),
        P(),
    )
    return jax.shard_map(
        functools.partial(shards, mesh.shape["dp"], mesh.shape["tensor"]),
        mesh=mesh,
        in_specs=in_specs,
        out_specs=out_specs,
        check_vma=False,
    )
```
